1024 devices in a mesh: gx: 64 (over y, z), gz: 16 (over x, core).
Axes of the slice: x: 8, y: 8, z: 8, core: 2. Of those that a mesh axis runs over, the one named last changes fastest.
Arguments:
- previous_basis: float32 [4, 512, 128, 128], P(None, 'gx', 'gz'), may hold values from -4 to 4
- restart_column: int32 [1], replicated, may hold values from 0 to 3
- diffusivity: float32 [3, 512, 128, 128], P(None, 'gx', 'gz'), may hold values from 0.05 to 0.5
- speed: float32 [3, 512, 128, 128], P(None, 'gx', 'gz'), may hold values from 0.05 to 0.5
- upwind: int32 [3, 512, 128, 128], P(None, 'gx', 'gz'), may hold values from 0 to 1
Outputs:
- basis_q: float32 [9, 512, 128, 128], P(None, 'gx', 'gz')
- factor_r: float32 [9, 9], replicated
- hessenberg: float32 [9, 8], replicated
The draws below stay inside these ranges and needn't reach their ends.
Inputs may be any that keep to these rules, and one draw needn't show every extreme that they name: `upwind`: 1 means the flow across the face runs toward the upper neighbour, 0 toward the cell. `restart_column`: index into the first dimension of previous_basis.
All inputs are finite; a program needn't handle non-finite values.
Results may differ from the reference program's by a relative error of at most 0.0003.
Values sent between devices are 32-bit elements; how exact they have to be, the bound alone decides.
No kernel may reach another device: no remote copies, remote signals or barrier semaphores. Data moves between devices by JAX's collectives and lax.ppermute only.
A program may use at most 32 MiB of HBM per device.

```python
import math
import jax
import jax.numpy as jnp
import numpy as np
from jax import lax

NZ = 128
S = 8
NX = 512
NY = 128


def draw_previous_basis(key, part):
    key = jax.random.fold_in(key, 11)
    amp_key, rough_key = jax.random.split(key)
    amplitude = jnp.exp(jax.random.uniform(amp_key, (4, 1, 1, 1), jnp.float32, math.log(2.5), math.log(3.5)))
    along_x = jnp.sin(math.pi * (jnp.arange(NX, dtype=jnp.float32) + 0.5) / NX)
    along_y = jnp.sin(math.pi * (jnp.arange(NY, dtype=jnp.float32) + 0.5) / NY)
    along_z = jnp.sin(math.pi * (jnp.arange(NZ, dtype=jnp.float32) + 0.5) / NZ)
    bump = along_x[:, None, None] * along_y[None, :, None] * along_z[None, None, :]
    rough = jnp.clip(jax.random.normal(rough_key, (4, NX, NY, NZ), jnp.float32), -6.0, 6.0)
    return amplitude * bump[None] + 0.03 * rough


def set_ends(values, own_key, low, largest):
    shape = values.shape
    index_at = [jax.random.randint(jax.random.fold_in(own_key, axis), (), 0, shape[axis]) for axis in range(len(shape))]
    values = values.at[tuple(index_at)].set(low)
    longest = shape.index(max(shape))
    index_at[longest] = (index_at[longest] + 1) % shape[longest]
    return values.at[tuple(index_at)].set(largest)


def level_of(rng, shape, cuts, smallest, largest):
    loudness = 1.0
    for axis_at, blocks in cuts:
        heights = jax.random.uniform(jax.random.fold_in(jax.random.fold_in(rng, 6), axis_at), (blocks,), jnp.float32, smallest / len(cuts), largest / len(cuts))
        loudness = loudness * jnp.repeat(jnp.exp(heights), shape[axis_at] // blocks).reshape((-1,) + (1,) * (len(shape) - 1 - axis_at))
    return loudness


def setup_inputs(seed: int = 0) -> dict:
    splits = jax.random.split(jax.random.key(seed), 6)
    previous_basis = draw_previous_basis(jax.random.fold_in(splits[5], 71), 0)
    restart_column = jax.random.randint(splits[1], (1,), 0, 4).astype(jnp.int32)
    diffusivity = jnp.clip(jnp.exp(math.log(0.5) - 2.3025851 * jax.random.uniform(splits[2], (3, NX, NY, NZ), jnp.float32) ** level_of(splits[2], (3, NX, NY, NZ), ((1, 64), (2, 16)), -0.2, 0.2)), 0.05, 0.5)
    speed = jnp.clip(jnp.exp(math.log(0.5) - 2.3025851 * jax.random.uniform(splits[3], (3, NX, NY, NZ), jnp.float32) ** level_of(splits[3], (3, NX, NY, NZ), ((1, 64), (2, 16)), -0.2, 0.2)), 0.05, 0.5)
    upwind = set_ends(jax.random.randint(splits[4], (3, NX, NY, NZ), 0, 2), jax.random.fold_in(splits[4], 1), 0, 1).astype(jnp.int32)
    return {"previous_basis": previous_basis, "restart_column": restart_column, "diffusivity": diffusivity, "speed": speed, "upwind": upwind}


CENTER = 2.5
HALF = 1.5

def stencil(field, pco, qco):
    f = jnp.pad(field, ((0, 0), (0, 0), (1, 1)))
    p = jnp.pad(pco, ((0, 0), (0, 0), (0, 0), (1, 1)))
    q = jnp.pad(qco, ((0, 0), (0, 0), (0, 0), (1, 1)))
    centre = f[1:-1, 1:-1, 1:-1]
    total = centre
    total = total + p[0, 1:-1, 1:-1, 1:-1] * (centre - f[2:, 1:-1, 1:-1]) - q[0, :-2, 1:-1, 1:-1] * (f[:-2, 1:-1, 1:-1] - centre)
    total = total + p[1, 1:-1, 1:-1, 1:-1] * (centre - f[1:-1, 2:, 1:-1]) - q[1, 1:-1, :-2, 1:-1] * (f[1:-1, :-2, 1:-1] - centre)
    total = total + p[2, 1:-1, 1:-1, 1:-1] * (centre - f[1:-1, 1:-1, 2:]) - q[2, 1:-1, 1:-1, :-2] * (f[1:-1, 1:-1, :-2] - centre)
    return total

def upper_inverse(upper):
    order = upper.shape[0]
    identity = jnp.eye(order, dtype=jnp.float32)
    rows = [None] * order
    for row_index in reversed(range(order)):
        remainder = identity[row_index]
        for other in range(row_index + 1, order):
            remainder = remainder - upper[row_index, other] * rows[other]
        rows[row_index] = remainder / upper[row_index, row_index]
    return jnp.stack(rows, 0)

def gram_of(block):
    return jnp.einsum('kxyz,lxyz->kl', block, block, precision=lax.Precision.HIGHEST)

def chol_upper(gram):
    return jnp.transpose(jnp.linalg.cholesky(gram))

def apply_inverse(block, upper):
    inverse = upper_inverse(upper)
    return jnp.einsum('jk,jxyz->kxyz', inverse, block, precision=lax.Precision.HIGHEST)

def change_matrix():
    table = np.zeros((9, 8))
    for col in range(8):
        table[col, col] = CENTER
        if col == 0:
            table[1, 0] = HALF
        else:
            table[col - 1, col] = 0.5 * HALF
            table[col + 1, col] = 0.5 * HALF
    return jnp.asarray(table, dtype=jnp.float32)

def hessenberg_of(upper):
    product = jnp.dot(upper, change_matrix(), precision=lax.Precision.HIGHEST)
    inverse = upper_inverse(upper[:8, :8])
    return jnp.dot(product, inverse, precision=lax.Precision.HIGHEST)

def reference(previous_basis, restart_column, diffusivity, speed, upwind):
    flow = upwind.astype(jnp.float32)
    p_face = diffusivity + speed * flow
    q_face = diffusivity + speed * (1.0 - flow)
    p_pad = jnp.pad(p_face, ((0, 0), (1, 1), (1, 1), (0, 0)))
    q_pad = jnp.pad(q_face, ((0, 0), (1, 1), (1, 1), (0, 0)))

    def zmap(v):
        image = stencil(jnp.pad(v, ((1, 1), (1, 1), (0, 0))), p_pad, q_pad)
        return (image - CENTER * v) / HALF
    start = lax.dynamic_index_in_dim(previous_basis, restart_column[0], 0, keepdims=False)
    vectors = [start, zmap(start)]
    for step in range(1, S):
        vectors.append(2.0 * zmap(vectors[-1]) - vectors[-2])
    block = jnp.stack(vectors, 0)
    upper_one = chol_upper(gram_of(block))
    first_q = apply_inverse(block, upper_one)
    upper_two = chol_upper(gram_of(first_q))
    final_q = apply_inverse(first_q, upper_two)
    upper = jnp.dot(upper_two, upper_one, precision=lax.Precision.HIGHEST)
    scale = math.sqrt(NX * NY * NZ)
    return (final_q * scale, upper / scale, hessenberg_of(upper))
```

```python
import math

import jax
import jax.numpy as jnp
from jax import lax
from jax.experimental import pallas as pl
from jax.experimental.pallas import tpu as pltpu
from jax.sharding import PartitionSpec as P

S = 8
COLS = S + 1
CENTER = 2.5
HALF = 1.5
B = 8
WIDE = 3 * B
LANES = 128
FIELDS = 7
F32 = jnp.float32
VMEM = pl.BlockSpec(memory_space=pltpu.VMEM)
SMEM = pl.BlockSpec(memory_space=pltpu.SMEM)
PARAMS = pltpu.CompilerParams(vmem_limit_bytes=16 * 1024 * 1024)


def iota(shape, dim):
    return lax.broadcasted_iota(jnp.int32, shape, dim)


def two_sum(a, b):
    s = a + b
    t = s - a
    return s, (a - (s - t)) + (b - t)


def fast_two_sum(a, b):
    s = a + b
    return s, b - (s - a)


def split(a):
    c = a * 4097.0
    high = c - (c - a)
    return high, a - high


def two_prod(a, b):
    ah, al = split(a)
    bh, bl = split(b)
    p = a * b
    return p, ((ah * bh - p) + (ah * bl + al * bh)) + al * bl


def pair_add(a, b):
    s, e = two_sum(a[0], b[0])
    return fast_two_sum(s, e + (a[1] + b[1]))


def pair_mul(a, b):
    p, e = two_prod(a[0], b[0])
    return fast_two_sum(p, e + (a[0] * b[1] + a[1] * b[0]))


def pair_roll(a, shift, axis):
    return tuple(pltpu.roll(part, shift, axis) for part in a)


def pair_where(mask, a, b):
    return tuple(jnp.where(mask, x, y) for x, y in zip(a, b))


def pack_kernel(column, basis, diffusivity, speed, upwind, out):
    out[0] = basis[column[0]]
    factor = -2.0 / HALF
    for dim in range(3):
        flow = upwind[dim].astype(F32)
        out[1 + dim] = (diffusivity[dim] + speed[dim] * flow) * factor
        out[4 + dim] = (diffusivity[dim] + speed[dim] * (1.0 - flow)) * factor


def side_kernel(own, below, above, to_next, to_last):
    row = iota((FIELDS, B, LANES), 1)
    to_next[:, 0:B] = own[...]
    to_last[:, 0:B] = own[...]
    for side in range(2):
        layer = (lambda m: below[:, B - m]) if side == 0 else (lambda m: above[:, m - 1])
        for m in range(1, 5):
            near = layer(m)
            at = B + 4 * side + m - 1
            if m == 4:
                to_next[:, at] = near
                to_last[:, at] = near
            else:
                far = layer(B - m)
                to_next[:, at] = jnp.where(row >= m, near, pltpu.roll(far, m, 1))
                to_last[:, at] = jnp.where(row < B - m, near, pltpu.roll(far, B - m, 1))


def basis_kernel(own, below, above, last, following, block, gram, coeff, field, high, low):
    def wide(f, a):
        if B <= a < 2 * B:
            return jnp.concatenate([last[f, a - B], own[f, a - B], following[f, a - B]], 0)
        side = 0 if a < B else 1
        m = B - a if side == 0 else a - (2 * B - 1)
        middle = below[f, a] if side == 0 else above[f, a - 2 * B]
        if m == B:
            lower = upper = jnp.zeros((B, LANES), F32)
        elif m <= 4:
            at = B + 4 * side + m - 1
            lower, upper = last[f, at], following[f, at]
        else:
            other = B - m
            at = B + 4 * side + other - 1
            lower = pltpu.roll(last[f, at], B - other, 0)
            upper = pltpu.roll(following[f, at], other, 0)
        return jnp.concatenate([lower, middle, upper], 0)

    lane = iota((WIDE, LANES), 1)
    zero = jnp.zeros((WIDE, LANES), F32)
    q_below = wide(4, 0)
    field[0, 0] = wide(0, 0)
    field[0, WIDE - 1] = wide(0, WIDE - 1)
    for a in range(1, WIDE - 1):
        field[0, a] = wide(0, a)
        p = [wide(1 + dim, a) for dim in range(3)]
        q = [wide(4 + dim, a) for dim in range(3)]
        inside = p[0] < 0.0
        qx = jnp.where(inside, q_below, zero)
        qy = jnp.where(inside, pltpu.roll(q[1], 1, 0), zero)
        qz = jnp.where(lane == 0, zero, pltpu.roll(q[2], 1, 1))
        q_below = q[0]
        coeff[0, a] = (-2.0 * (CENTER - 1.0) / HALF) - ((p[0] + p[1]) + (p[2] + qx) + (qy + qz))
        coeff[1, a] = p[0]
        coeff[2, a] = qx
        coeff[3, a] = p[1]
        coeff[4, a] = qy
        coeff[5, a] = jnp.where(lane == LANES - 1, zero, p[2])
        coeff[6, a] = qz

    block[0] = own[0]
    for k in range(1, COLS):
        src, dst = (k - 1) % 2, k % 2

        def layer(a, carry, k=k, src=src, dst=dst):
            v = field[src, a]
            x = coeff[0, a] * v + coeff[1, a] * field[src, a + 1] + coeff[2, a] * field[src, a - 1]
            y = coeff[3, a] * pltpu.roll(v, WIDE - 1, 0) + coeff[4, a] * pltpu.roll(v, 1, 0)
            z = coeff[5, a] * pltpu.roll(v, LANES - 1, 1) + coeff[6, a] * pltpu.roll(v, 1, 1)
            total = x + (y + z)
            new = 0.5 * total if k == 1 else total - field[dst, a]
            if k == S:
                block[k, a - B] = new[B : 2 * B]
            else:
                field[dst, a] = new
            return carry

        lax.fori_loop(k, WIDE - k, layer, 0, unroll=2)
        if k < S:
            block[k] = field[dst, B : 2 * B, B : 2 * B, :]

    for k in range(COLS):
        h, l = split(block[k])
        high[k] = h
        low[k] = l

    def product(i, j):
        total = None
        for x in range(B):
            ah, al, bh, bl = high[i, x], low[i, x], high[j, x], low[j, x]
            p = block[i, x] * block[j, x]
            e = ((ah * bh - p) + (ah * bl + al * bh)) + al * bl
            if total is None:
                total, rest = p, e
            else:
                total, err = two_sum(total, p)
                rest = rest + (e + err)
        return fast_two_sum(total, rest)

    row = iota((B, LANES), 0)
    lane = iota((B, LANES), 1)
    nothing = (jnp.zeros((B, LANES), F32),) * 2

    def merged(a, b, distance, axis):
        if a is None and b is None:
            return None
        a = nothing if a is None else a
        b = nothing if b is None else b
        mask = ((row if axis == 0 else lane) & distance) == 0
        return pair_add(pair_where(mask, a, b), pair_roll(pair_where(mask, b, a), distance, axis))

    def fold(items, axis):
        distance = 1
        while len(items) > 1:
            items = [merged(items[t], items[t + 1], distance, axis) for t in range(0, len(items), 2)]
            distance *= 2
        return items[0]

    products = {(i, j): product(i, j) for i in range(COLS) for j in range(i, COLS)}
    slots = []
    for m in range(16):
        if m < COLS:
            items = [products[min(r, m), max(r, m)] for r in range(B)]
        else:
            items = [products[m - COLS, S]] + [products[m - 2, S] if m - 2 < COLS else None] + [None] * 6
        slots.append(fold(items, 0))
    table = fold(slots, 1)
    for distance in (16, 32, 64):
        table = pair_add(table, pair_roll(table, distance, 1))
    mine = lane // 16 == row
    rows = [jnp.sum(jnp.where(mine, part, 0.0), axis=0, keepdims=True) for part in table]
    tile = jnp.where(row % 2 == 0, rows[0], rows[1])
    for t in range(gram.shape[0] // B):
        gram[B * t : B * (t + 1), :] = tile


def summed(ref):
    tiles = [ref[B * t : B * (t + 1), :] for t in range(ref.shape[0] // B)]
    pairs = [(t, pltpu.roll(t, B - 1, 0)) for t in tiles]
    while len(pairs) > 1:
        pairs = [pair_add(pairs[t], pairs[t + 1]) for t in range(0, len(pairs), 2)]
    total = pairs[0]
    for distance in (2, 4):
        total = pair_add(total, pair_roll(total, distance, 0))
    return total


def sum_kernel(parts, out):
    total = summed(parts)
    row = iota((B, LANES), 0)
    tile = jnp.where(row % 2 == 0, total[0], pltpu.roll(total[1], 1, 0))
    for t in range(out.shape[0] // B):
        out[B * t : B * (t + 1), :] = tile


def factor_kernel(scale, parts, block, basis_q, factor_r, hessenberg, inverse):
    shape = (2 * B, LANES)
    row = iota(shape, 0)
    lane = iota(shape, 1)

    def matrix(part):
        line = jnp.broadcast_to(part[0:1, :], shape)
        out = jnp.zeros(shape, F32)
        for r in range(B):
            moved = line if r == 0 else pltpu.roll(line, LANES - 16 * r, 1)
            out = jnp.where((row == r) & (lane < COLS), moved, out)
        out = jnp.where((row == S) & (lane < 7), pltpu.roll(line, LANES - 9, 1), out)
        return jnp.where((row == S) & ((lane == 7) | (lane == 8)), pltpu.roll(line, LANES - 18, 1), out)

    high, low = (matrix(part) for part in summed(parts))
    high = jnp.where((lane == row + 64) & (row < COLS), 1.0, high)
    pivots = jnp.ones(shape, F32)
    for j in range(COLS):
        d = tuple(jnp.broadcast_to(part[j : j + 1, j : j + 1], shape) for part in (high, low))
        pivots = jnp.where(row == j, d[0], pivots)
        if j == S:
            break
        top = tuple(jnp.broadcast_to(part[j : j + 1, :], shape) for part in (high, low))
        col = tuple(jnp.broadcast_to(part[:, j : j + 1], shape) for part in (high, low))
        inv = 1.0 / d[0]
        ratio = col[0] * inv
        back, err = two_prod(ratio, d[0])
        rest = (((col[0] - back) - err) + (col[1] - ratio * d[1])) * inv
        ratio = fast_two_sum(ratio, rest)
        change = pair_mul(ratio, top)
        change = tuple(jnp.where(row > j, -part, 0.0) for part in change)
        high, low = pair_add((high, low), change)
    root = jnp.sqrt(pivots)
    scaled = high / root
    upper = jnp.where((lane >= row) & (lane < COLS) & (row < COLS), scaled, 0.0)
    lower = jnp.where((lane <= row) & (row < COLS), pltpu.roll(scaled, 64, 1), 0.0)
    factor_r[...] = (upper / scale)[:COLS, :COLS]
    right = pltpu.roll(upper, LANES - 1, 1)
    product = CENTER * upper + jnp.where(lane == 0, HALF, 0.5 * HALF) * right + (0.5 * HALF) * pltpu.roll(upper, 1, 1)
    product = jnp.where(lane < S, product, 0.0)
    small = lax.dot_general(
        product,
        jnp.where(lane < S, lower, 0.0),
        (((1,), (1,)), ((), ())),
        precision=lax.Precision.HIGHEST,
        preferred_element_type=F32,
    )
    hessenberg[...] = small[:COLS, :S]
    lower = lower * scale
    for k in range(COLS):
        inverse[k] = jnp.broadcast_to(lower[:, k : k + 1], shape)
    for j in range(COLS):
        total = None
        for k in range(j + 1):
            factor = jnp.broadcast_to(inverse[k, j : j + 1, :], (B, LANES))[None]
            term = factor * block[k]
            total = term if total is None else total + term
        basis_q[j] = total


def moved(array, axis, distance):
    count = lax.axis_size(axis)
    route = [(i, i + distance) for i in range(count) if 0 <= i + distance < count]
    return lax.ppermute(array, axis, route)


def body(previous_basis, restart_column, diffusivity, speed, upwind):
    count_x, count_y = lax.axis_size("gx"), lax.axis_size("gz")
    brick = (FIELDS, B, B, LANES)
    own = pl.pallas_call(
        pack_kernel,
        out_shape=jax.ShapeDtypeStruct(brick, F32),
        in_specs=[SMEM] + [VMEM] * 4,
        out_specs=VMEM,
        compiler_params=PARAMS,
        name="pack",
    )(restart_column, previous_basis, diffusivity, speed, upwind)
    below = moved(own, "gx", 1)
    above = moved(own, "gx", -1)
    sides = jax.ShapeDtypeStruct((FIELDS, 2 * B, B, LANES), F32)
    to_next, to_last = pl.pallas_call(
        side_kernel,
        out_shape=(sides, sides),
        in_specs=[VMEM] * 3,
        out_specs=(VMEM, VMEM),
        compiler_params=PARAMS,
        name="sides",
    )(own, below, above)
    last = moved(to_next, "gz", 1)
    following = moved(to_last, "gz", -1)
    wide = (WIDE, WIDE, LANES)
    block, gram = pl.pallas_call(
        basis_kernel,
        out_shape=(
            jax.ShapeDtypeStruct((COLS, B, B, LANES), F32),
            jax.ShapeDtypeStruct((2 * count_y, LANES), F32),
        ),
        in_specs=[VMEM] * 5,
        out_specs=(VMEM, VMEM),
        scratch_shapes=[
            pltpu.VMEM((FIELDS,) + wide, F32),
            pltpu.VMEM((2,) + wide, F32),
            pltpu.VMEM((COLS, B, B, LANES), F32),
            pltpu.VMEM((COLS, B, B, LANES), F32),
        ],
        compiler_params=PARAMS,
        name="basis",
    )(own, below, above, last, following)
    parts = lax.all_to_all(gram, "gz", 0, 0, tiled=True)
    line = pl.pallas_call(
        sum_kernel,
        out_shape=jax.ShapeDtypeStruct((2 * count_x, LANES), F32),
        in_specs=[VMEM],
        out_specs=VMEM,
        compiler_params=PARAMS,
        name="line_sum",
    )(parts)
    parts = lax.all_to_all(line, "gx", 0, 0, tiled=True)
    scale = math.sqrt(B * B * LANES * count_x * count_y)
    return pl.pallas_call(
        lambda *refs: factor_kernel(scale, *refs),
        out_shape=(
            jax.ShapeDtypeStruct((COLS, B, B, LANES), F32),
            jax.ShapeDtypeStruct((COLS, COLS), F32),
            jax.ShapeDtypeStruct((COLS, S), F32),
        ),
        in_specs=[VMEM] * 2,
        out_specs=(VMEM,) * 3,
        scratch_shapes=[pltpu.VMEM((COLS, 2 * B, LANES), F32)],
        compiler_params=PARAMS,
        name="factor",
    )(parts, block)


def solution(mesh):
    return jax.shard_map(
        body,
        mesh=mesh,
        in_specs=(
            P(None, "gx", "gz", None),
            P(),
            P(None, "gx", "gz", None),
            P(None, "gx", "gz", None),
            P(None, "gx", "gz", None),
        ),
        out_specs=(P(None, "gx", "gz", None), P(), P()),
        check_vma=False,
    )
```

```python
import math

import jax
import jax.numpy as jnp
from jax import lax
from jax.experimental import pallas as pl
from jax.experimental.pallas import tpu as pltpu
from jax.sharding import PartitionSpec as P

S = 8
COLS = S + 1
CENTER = 2.5
HALF = 1.5
B = 8
WIDE = 3 * B
LANES = 128
FIELDS = 7
F32 = jnp.float32
VMEM = pl.BlockSpec(memory_space=pltpu.VMEM)
HBM = pl.BlockSpec(memory_space=pltpu.HBM)
SMEM = pl.BlockSpec(memory_space=pltpu.SMEM)
PARAMS = pltpu.CompilerParams(vmem_limit_bytes=16 * 1024 * 1024)
ALL_VMEM = pltpu.CompilerParams(vmem_limit_bytes=63 * 1024 * 1024)


def iota(shape, dim):
    return lax.broadcasted_iota(jnp.int32, shape, dim)


def two_sum(a, b):
    s = a + b
    t = s - a
    return s, (a - (s - t)) + (b - t)


def fast_two_sum(a, b):
    s = a + b
    return s, b - (s - a)


def split(a):
    c = a * 4097.0
    high = c - (c - a)
    return high, a - high


def two_prod(a, b):
    ah, al = split(a)
    bh, bl = split(b)
    p = a * b
    return p, ((ah * bh - p) + (ah * bl + al * bh)) + al * bl


def pair_add(a, b):
    s, e = two_sum(a[0], b[0])
    return fast_two_sum(s, e + (a[1] + b[1]))


def pair_mul(a, b):
    p, e = two_prod(a[0], b[0])
    return fast_two_sum(p, e + (a[0] * b[1] + a[1] * b[0]))


def pair_roll(a, shift, axis):
    return tuple(pltpu.roll(part, shift, axis) for part in a)


def pair_where(mask, a, b):
    return tuple(jnp.where(mask, x, y) for x, y in zip(a, b))


def pack_kernel(column, basis, diffusivity_in, speed_in, upwind_in, out, diffusivity, speed, upwind, sems):
    copies = [
        pltpu.make_async_copy(src, dst, sems.at[n])
        for n, (src, dst) in enumerate(
            (
                (basis.at[column[0]], out.at[0]),
                (diffusivity_in, diffusivity),
                (speed_in, speed),
                (upwind_in, upwind),
            )
        )
    ]
    for copy in copies:
        copy.start()
    for copy in copies:
        copy.wait()
    factor = -2.0 / HALF
    for dim in range(3):
        flow = upwind[dim].astype(F32)
        out[1 + dim] = (diffusivity[dim] + speed[dim] * flow) * factor
        out[4 + dim] = (diffusivity[dim] + speed[dim] * (1.0 - flow)) * factor


def side_kernel(even, own, first, second, wide, to_first, to_second):
    @pl.when(even[0] == 1)
    def _():
        wide[:, 0:B] = second[...]
        wide[:, 2 * B : WIDE] = first[...]

    @pl.when(even[0] == 0)
    def _():
        wide[:, 0:B] = first[...]
        wide[:, 2 * B : WIDE] = second[...]

    wide[:, B : 2 * B] = own[...]

    @pl.when(even[1] == 1)
    def _():
        emit_sides(wide, to_first, to_second)

    @pl.when(even[1] == 0)
    def _():
        emit_sides(wide, to_second, to_first)


def emit_sides(wide, to_next, to_last):
    row = iota((FIELDS, B, LANES), 1)
    own = wide[:, B : 2 * B]
    to_next[:, 0:B] = own
    to_last[:, 0:B] = own
    for side in range(2):
        for m in range(1, 5):
            near = wide[:, B - m if side == 0 else 2 * B - 1 + m]
            at = B + 4 * side + m - 1
            if m == 4:
                to_next[:, at] = near
                to_last[:, at] = near
            else:
                far = wide[:, m if side == 0 else WIDE - 1 - m]
                to_next[:, at] = jnp.where(row >= m, near, pltpu.roll(far, m, 1))
                to_last[:, at] = jnp.where(row < B - m, near, pltpu.roll(far, B - m, 1))


def start_fields(strip, last, following, coeff, field):
    def wide(f, a):
        if B <= a < 2 * B:
            return jnp.concatenate([last[f, a - B], strip[f, a], following[f, a - B]], 0)
        side = 0 if a < B else 1
        m = B - a if side == 0 else a - (2 * B - 1)
        middle = strip[f, a]
        if m == B:
            lower = upper = jnp.zeros((B, LANES), F32)
        elif m <= 4:
            at = B + 4 * side + m - 1
            lower, upper = last[f, at], following[f, at]
        else:
            other = B - m
            at = B + 4 * side + other - 1
            lower = pltpu.roll(last[f, at], B - other, 0)
            upper = pltpu.roll(following[f, at], other, 0)
        return jnp.concatenate([lower, middle, upper], 0)

    lane = iota((WIDE, LANES), 1)
    zero = jnp.zeros((WIDE, LANES), F32)
    q_below = wide(4, 0)
    field[0, 0] = wide(0, 0)
    field[0, WIDE - 1] = wide(0, WIDE - 1)
    for a in range(1, WIDE - 1):
        field[0, a] = wide(0, a)
        p = [wide(1 + dim, a) for dim in range(3)]
        q = [wide(4 + dim, a) for dim in range(3)]
        inside = p[0] < 0.0
        qx = jnp.where(inside, q_below, zero)
        qy = jnp.where(inside, pltpu.roll(q[1], 1, 0), zero)
        qz = jnp.where(lane == 0, zero, pltpu.roll(q[2], 1, 1))
        q_below = q[0]
        coeff[0, a] = (-2.0 * (CENTER - 1.0) / HALF) - ((p[0] + p[1]) + (p[2] + qx) + (qy + qz))
        coeff[1, a] = p[0]
        coeff[2, a] = qx
        coeff[3, a] = p[1]
        coeff[4, a] = qy
        coeff[5, a] = jnp.where(lane == LANES - 1, zero, p[2])
        coeff[6, a] = qz


def basis_kernel(even, strip, first, second, block, gram, coeff, field, high, low):
    @pl.when(even[1] == 1)
    def _():
        start_fields(strip, second, first, coeff, field)

    @pl.when(even[1] == 0)
    def _():
        start_fields(strip, first, second, coeff, field)

    block[0] = strip[0, B : 2 * B]
    for k in range(1, COLS):
        src, dst = (k - 1) % 2, k % 2

        def layer(a, carry, k=k, src=src, dst=dst):
            v = field[src, a]
            x = coeff[0, a] * v + coeff[1, a] * field[src, a + 1] + coeff[2, a] * field[src, a - 1]
            y = coeff[3, a] * pltpu.roll(v, WIDE - 1, 0) + coeff[4, a] * pltpu.roll(v, 1, 0)
            z = coeff[5, a] * pltpu.roll(v, LANES - 1, 1) + coeff[6, a] * pltpu.roll(v, 1, 1)
            total = x + (y + z)
            new = 0.5 * total if k == 1 else total - field[dst, a]
            if k == S:
                block[k, a - B] = new[B : 2 * B]
            else:
                field[dst, a] = new
            return carry

        lax.fori_loop(k, WIDE - k, layer, 0, unroll=True)
        if k < S:
            block[k] = field[dst, B : 2 * B, B : 2 * B, :]

    for k in range(COLS):
        h, l = split(block[k])
        high[k] = h
        low[k] = l

    def product(i, j):
        total = None
        for x in range(B):
            ah, al, bh, bl = high[i, x], low[i, x], high[j, x], low[j, x]
            p = block[i, x] * block[j, x]
            e = ((ah * bh - p) + (ah * bl + al * bh)) + al * bl
            if total is None:
                total, rest = p, e
            else:
                total, err = two_sum(total, p)
                rest = rest + (e + err)
        return fast_two_sum(total, rest)

    row = iota((B, LANES), 0)
    lane = iota((B, LANES), 1)
    nothing = (jnp.zeros((B, LANES), F32),) * 2

    def merged(a, b, distance, axis):
        if a is None and b is None:
            return None
        a = nothing if a is None else a
        b = nothing if b is None else b
        mask = ((row if axis == 0 else lane) & distance) == 0
        return pair_add(pair_where(mask, a, b), pair_roll(pair_where(mask, b, a), distance, axis))

    def fold(items, axis):
        distance = 1
        while len(items) > 1:
            items = [merged(items[t], items[t + 1], distance, axis) for t in range(0, len(items), 2)]
            distance *= 2
        return items[0]

    products = {(i, j): product(i, j) for i in range(COLS) for j in range(i, COLS)}
    slots = []
    for m in range(16):
        if m < COLS:
            items = [products[min(r, m), max(r, m)] for r in range(B)]
        else:
            items = [products[m - COLS, S]] + [products[m - 2, S] if m - 2 < COLS else None] + [None] * 6
        slots.append(fold(items, 0))
    table = fold(slots, 1)
    for distance in (16, 32, 64):
        table = pair_add(table, pair_roll(table, distance, 1))
    mine = lane // 16 == row
    rows = [jnp.sum(jnp.where(mine, part, 0.0), axis=0, keepdims=True) for part in table]
    tile = jnp.where(row % 2 == 0, rows[0], rows[1])
    for t in range(gram.shape[0] // B):
        gram[B * t : B * (t + 1), :] = tile


def summed(ref):
    tiles = [ref[B * t : B * (t + 1), :] for t in range(ref.shape[0] // B)]
    pairs = [(t, pltpu.roll(t, B - 1, 0)) for t in tiles]
    while len(pairs) > 1:
        pairs = [pair_add(pairs[t], pairs[t + 1]) for t in range(0, len(pairs), 2)]
    total = pairs[0]
    for distance in (2, 4):
        total = pair_add(total, pair_roll(total, distance, 0))
    return total


def sum_kernel(parts, out):
    total = summed(parts)
    row = iota((B, LANES), 0)
    tile = jnp.where(row % 2 == 0, total[0], pltpu.roll(total[1], 1, 0))
    for t in range(out.shape[0] // B):
        out[B * t : B * (t + 1), :] = tile


def factor_kernel(scale, parts, block, basis_q, factor_r, hessenberg, inverse):
    shape = (2 * B, LANES)
    row = iota(shape, 0)
    lane = iota(shape, 1)

    def matrix(part):
        line = jnp.broadcast_to(part[0:1, :], shape)
        out = jnp.zeros(shape, F32)
        for r in range(B):
            moved = line if r == 0 else pltpu.roll(line, LANES - 16 * r, 1)
            out = jnp.where((row == r) & (lane < COLS), moved, out)
        out = jnp.where((row == S) & (lane < 7), pltpu.roll(line, LANES - 9, 1), out)
        return jnp.where((row == S) & ((lane == 7) | (lane == 8)), pltpu.roll(line, LANES - 18, 1), out)

    high, low = (matrix(part) for part in summed(parts))
    high = jnp.where((lane == row + 64) & (row < COLS), 1.0, high)
    pivots = jnp.ones(shape, F32)
    for j in range(COLS):
        d = tuple(jnp.broadcast_to(part[j : j + 1, j : j + 1], shape) for part in (high, low))
        pivots = jnp.where(row == j, d[0], pivots)
        if j == S:
            break
        top = tuple(jnp.broadcast_to(part[j : j + 1, :], shape) for part in (high, low))
        col = tuple(jnp.broadcast_to(part[:, j : j + 1], shape) for part in (high, low))
        inv = 1.0 / d[0]
        ratio = col[0] * inv
        back, err = two_prod(ratio, d[0])
        rest = (((col[0] - back) - err) + (col[1] - ratio * d[1])) * inv
        ratio = fast_two_sum(ratio, rest)
        change = pair_mul(ratio, top)
        change = tuple(jnp.where(row > j, -part, 0.0) for part in change)
        high, low = pair_add((high, low), change)
    root = jnp.sqrt(pivots)
    scaled = high / root
    upper = jnp.where((lane >= row) & (lane < COLS) & (row < COLS), scaled, 0.0)
    lower = jnp.where((lane <= row) & (row < COLS), pltpu.roll(scaled, 64, 1), 0.0)
    factor_r[...] = (upper / scale)[:COLS, :COLS]
    right = pltpu.roll(upper, LANES - 1, 1)
    product = CENTER * upper + jnp.where(lane == 0, HALF, 0.5 * HALF) * right + (0.5 * HALF) * pltpu.roll(upper, 1, 1)
    product = jnp.where(lane < S, product, 0.0)
    small = lax.dot_general(
        jnp.where(lane < S, lower, 0.0),
        product,
        (((1,), (1,)), ((), ())),
        precision=lax.Precision.HIGHEST,
        preferred_element_type=F32,
    )
    hessenberg[...] = small[:S, :COLS]
    lower = lower * scale
    for k in range(COLS):
        inverse[k] = jnp.broadcast_to(lower[:, k : k + 1], shape)
    for j in range(COLS):
        total = None
        for k in range(j + 1):
            factor = jnp.broadcast_to(inverse[k, j : j + 1, :], (B, LANES))[None]
            term = factor * block[k]
            total = term if total is None else total + term
        basis_q[j] = total


def paired(array, axis, first):
    count = lax.axis_size(axis)
    lower = range(first, count - 1, 2)
    return lax.ppermute(array, axis, [(i, i + 1) for i in lower] + [(i + 1, i) for i in lower])


def body(previous_basis, restart_column, diffusivity, speed, upwind):
    count_x, count_y = lax.axis_size("gx"), lax.axis_size("gz")
    even = jnp.stack([1 - lax.axis_index("gx") % 2, 1 - lax.axis_index("gz") % 2]).astype(jnp.int32)
    faces = (3, B, B, LANES)
    own = pl.pallas_call(
        pack_kernel,
        out_shape=jax.ShapeDtypeStruct((FIELDS, B, B, LANES), F32),
        in_specs=[SMEM] + [HBM] * 4,
        out_specs=VMEM,
        scratch_shapes=[
            pltpu.VMEM(faces, F32),
            pltpu.VMEM(faces, F32),
            pltpu.VMEM(faces, jnp.int32),
            pltpu.SemaphoreType.DMA((4,)),
        ],
        compiler_params=ALL_VMEM,
        name="pack",
    )(restart_column, previous_basis, diffusivity, speed, upwind)
    first = paired(own, "gx", 0)
    second = paired(own, "gx", 1)
    sides = jax.ShapeDtypeStruct((FIELDS, 2 * B, B, LANES), F32)
    strip, to_first, to_second = pl.pallas_call(
        side_kernel,
        out_shape=(jax.ShapeDtypeStruct((FIELDS, WIDE, B, LANES), F32), sides, sides),
        in_specs=[SMEM] + [VMEM] * 3,
        out_specs=(VMEM,) * 3,
        compiler_params=PARAMS,
        name="sides",
    )(even, own, first, second)
    first = paired(to_first, "gz", 0)
    second = paired(to_second, "gz", 1)
    wide = (WIDE, WIDE, LANES)
    block, gram = pl.pallas_call(
        basis_kernel,
        out_shape=(
            jax.ShapeDtypeStruct((COLS, B, B, LANES), F32),
            jax.ShapeDtypeStruct((2 * count_y, LANES), F32),
        ),
        in_specs=[SMEM] + [VMEM] * 3,
        out_specs=(VMEM, VMEM),
        scratch_shapes=[
            pltpu.VMEM((FIELDS,) + wide, F32),
            pltpu.VMEM((2,) + wide, F32),
            pltpu.VMEM((COLS, B, B, LANES), F32),
            pltpu.VMEM((COLS, B, B, LANES), F32),
        ],
        compiler_params=PARAMS,
        name="basis",
    )(even, strip, first, second)
    parts = lax.all_to_all(gram, "gz", 0, 0, tiled=True)
    line = pl.pallas_call(
        sum_kernel,
        out_shape=jax.ShapeDtypeStruct((2 * count_x, LANES), F32),
        in_specs=[VMEM],
        out_specs=VMEM,
        compiler_params=PARAMS,
        name="line_sum",
    )(parts)
    parts = lax.all_to_all(line, "gx", 0, 0, tiled=True)
    scale = math.sqrt(B * B * LANES * count_x * count_y)
    basis_q, factor_r, hessenberg = pl.pallas_call(
        lambda *refs: factor_kernel(scale, *refs),
        out_shape=(
            jax.ShapeDtypeStruct((COLS, B, B, LANES), F32),
            jax.ShapeDtypeStruct((COLS, COLS), F32),
            jax.ShapeDtypeStruct((S, COLS), F32),
        ),
        in_specs=[VMEM] * 2,
        out_specs=(VMEM,) * 3,
        scratch_shapes=[pltpu.VMEM((COLS, 2 * B, LANES), F32)],
        compiler_params=PARAMS,
        name="factor",
    )(parts, block)
    return basis_q, factor_r, jnp.transpose(hessenberg)


def solution(mesh):
    return jax.shard_map(
        body,
        mesh=mesh,
        in_specs=(
            P(None, "gx", "gz", None),
            P(),
            P(None, "gx", "gz", None),
            P(None, "gx", "gz", None),
            P(None, "gx", "gz", None),
        ),
        out_specs=(P(None, "gx", "gz", None), P(), P()),
        check_vma=False,
    )
```

```python
import math

import jax
import jax.numpy as jnp
from jax import lax
from jax.experimental import pallas as pl
from jax.experimental.pallas import tpu as pltpu
from jax.sharding import PartitionSpec as P

S = 8
COLS = S + 1
CENTER = 2.5
HALF = 1.5
B = 8
WIDE = 3 * B
LANES = 128
FIELDS = 7
F32 = jnp.float32
VMEM = pl.BlockSpec(memory_space=pltpu.VMEM)
HBM = pl.BlockSpec(memory_space=pltpu.HBM)
SMEM = pl.BlockSpec(memory_space=pltpu.SMEM)
PARAMS = pltpu.CompilerParams(vmem_limit_bytes=16 * 1024 * 1024)
ALL_VMEM = pltpu.CompilerParams(vmem_limit_bytes=63 * 1024 * 1024)


def iota(shape, dim):
    return lax.broadcasted_iota(jnp.int32, shape, dim)


def two_sum(a, b):
    s = a + b
    t = s - a
    return s, (a - (s - t)) + (b - t)


def fast_two_sum(a, b):
    s = a + b
    return s, b - (s - a)


def split(a):
    c = a * 4097.0
    high = c - (c - a)
    return high, a - high


def two_prod(a, b):
    ah, al = split(a)
    bh, bl = split(b)
    p = a * b
    return p, ((ah * bh - p) + (ah * bl + al * bh)) + al * bl


def pair_add(a, b):
    s, e = two_sum(a[0], b[0])
    return fast_two_sum(s, e + (a[1] + b[1]))


def pair_mul(a, b):
    p, e = two_prod(a[0], b[0])
    return fast_two_sum(p, e + (a[0] * b[1] + a[1] * b[0]))


def pair_roll(a, shift, axis):
    return tuple(pltpu.roll(part, shift, axis) for part in a)


def pair_where(mask, a, b):
    return tuple(jnp.where(mask, x, y) for x, y in zip(a, b))


def pack_kernel(column, basis, diffusivity_in, speed_in, upwind_in, out, diffusivity, speed, upwind, sems):
    copies = [
        pltpu.make_async_copy(src, dst, sems.at[n])
        for n, (src, dst) in enumerate(
            (
                (basis.at[column[0]], out.at[0]),
                (diffusivity_in, diffusivity),
                (speed_in, speed),
                (upwind_in, upwind),
            )
        )
    ]
    for copy in copies:
        copy.start()
    for copy in copies:
        copy.wait()
    factor = -2.0 / HALF
    for dim in range(3):
        flow = upwind[dim].astype(F32)
        out[1 + dim] = (diffusivity[dim] + speed[dim] * flow) * factor
        out[4 + dim] = (diffusivity[dim] + speed[dim] * (1.0 - flow)) * factor


def corner_kernel(even, first, second, strip, to_first, to_second):
    @pl.when(even[0] == 1)
    def _():
        strip[:, 0:B] = second[...]
        strip[:, B : 2 * B] = first[...]

    @pl.when(even[0] == 0)
    def _():
        strip[:, 0:B] = first[...]
        strip[:, B : 2 * B] = second[...]

    @pl.when(even[1] == 1)
    def _():
        emit_corners(strip, to_first, to_second)

    @pl.when(even[1] == 0)
    def _():
        emit_corners(strip, to_second, to_first)


def emit_corners(strip, to_next, to_last):
    row = iota((FIELDS, B, LANES), 1)
    for side in range(2):
        for m in range(1, 5):
            near = strip[:, B - m if side == 0 else B - 1 + m]
            at = 4 * side + m - 1
            if m == 4:
                to_next[:, at] = near
                to_last[:, at] = near
            else:
                far = strip[:, m if side == 0 else 2 * B - 1 - m]
                to_next[:, at] = jnp.where(row >= m, near, pltpu.roll(far, m, 1))
                to_last[:, at] = jnp.where(row < B - m, near, pltpu.roll(far, B - m, 1))


def keep_kernel(own, kept):
    kept[...] = own[...]


def start_fields(kept, strip, last, following, corner_last, corner_following, coeff, field):
    def wide(f, a):
        if B <= a < 2 * B:
            return jnp.concatenate([last[f, a - B], kept[f, a - B], following[f, a - B]], 0)
        side = 0 if a < B else 1
        m = B - a if side == 0 else a - (2 * B - 1)
        middle = strip[f, a if side == 0 else a - B]
        if m == B:
            lower = upper = jnp.zeros((B, LANES), F32)
        elif m <= 4:
            at = 4 * side + m - 1
            lower, upper = corner_last[f, at], corner_following[f, at]
        else:
            other = B - m
            at = 4 * side + other - 1
            lower = pltpu.roll(corner_last[f, at], B - other, 0)
            upper = pltpu.roll(corner_following[f, at], other, 0)
        return jnp.concatenate([lower, middle, upper], 0)

    lane = iota((WIDE, LANES), 1)
    zero = jnp.zeros((WIDE, LANES), F32)
    q_below = wide(4, 0)
    field[0, 0] = wide(0, 0)
    field[0, WIDE - 1] = wide(0, WIDE - 1)
    for a in range(1, WIDE - 1):
        field[0, a] = wide(0, a)
        p = [wide(1 + dim, a) for dim in range(3)]
        q = [wide(4 + dim, a) for dim in range(3)]
        inside = p[0] < 0.0
        qx = jnp.where(inside, q_below, zero)
        qy = jnp.where(inside, pltpu.roll(q[1], 1, 0), zero)
        qz = jnp.where(lane == 0, zero, pltpu.roll(q[2], 1, 1))
        q_below = q[0]
        coeff[0, a] = (-2.0 * (CENTER - 1.0) / HALF) - ((p[0] + p[1]) + (p[2] + qx) + (qy + qz))
        coeff[1, a] = p[0]
        coeff[2, a] = qx
        coeff[3, a] = p[1]
        coeff[4, a] = qy
        coeff[5, a] = jnp.where(lane == LANES - 1, zero, p[2])
        coeff[6, a] = qz


def basis_kernel(
    even, kept, strip, first, second, corner_first, corner_second, block, gram, coeff, field, high, low
):
    @pl.when(even[1] == 1)
    def _():
        start_fields(kept, strip, second, first, corner_second, corner_first, coeff, field)

    @pl.when(even[1] == 0)
    def _():
        start_fields(kept, strip, first, second, corner_first, corner_second, coeff, field)

    block[0] = kept[0]
    for k in range(1, COLS):
        src, dst = (k - 1) % 2, k % 2

        def layer(a, carry, k=k, src=src, dst=dst):
            v = field[src, a]
            x = coeff[0, a] * v + coeff[1, a] * field[src, a + 1] + coeff[2, a] * field[src, a - 1]
            y = coeff[3, a] * pltpu.roll(v, WIDE - 1, 0) + coeff[4, a] * pltpu.roll(v, 1, 0)
            z = coeff[5, a] * pltpu.roll(v, LANES - 1, 1) + coeff[6, a] * pltpu.roll(v, 1, 1)
            total = x + (y + z)
            new = 0.5 * total if k == 1 else total - field[dst, a]
            if k == S:
                block[k, a - B] = new[B : 2 * B]
            else:
                field[dst, a] = new
            return carry

        lax.fori_loop(k, WIDE - k, layer, 0, unroll=True)
        if k < S:
            block[k] = field[dst, B : 2 * B, B : 2 * B, :]

    for k in range(COLS):
        h, l = split(block[k])
        high[k] = h
        low[k] = l

    def product(i, j):
        total = None
        for x in range(B):
            ah, al, bh, bl = high[i, x], low[i, x], high[j, x], low[j, x]
            p = block[i, x] * block[j, x]
            e = ((ah * bh - p) + (ah * bl + al * bh)) + al * bl
            if total is None:
                total, rest = p, e
            else:
                total, err = two_sum(total, p)
                rest = rest + (e + err)
        return fast_two_sum(total, rest)

    row = iota((B, LANES), 0)
    lane = iota((B, LANES), 1)
    nothing = (jnp.zeros((B, LANES), F32),) * 2

    def merged(a, b, distance, axis):
        if a is None and b is None:
            return None
        a = nothing if a is None else a
        b = nothing if b is None else b
        mask = ((row if axis == 0 else lane) & distance) == 0
        return pair_add(pair_where(mask, a, b), pair_roll(pair_where(mask, b, a), distance, axis))

    def fold(items, axis):
        distance = 1
        while len(items) > 1:
            items = [merged(items[t], items[t + 1], distance, axis) for t in range(0, len(items), 2)]
            distance *= 2
        return items[0]

    products = {(i, j): product(i, j) for i in range(COLS) for j in range(i, COLS)}
    slots = []
    for m in range(16):
        if m < COLS:
            items = [products[min(r, m), max(r, m)] for r in range(B)]
        else:
            items = [products[m - COLS, S]] + [products[m - 2, S] if m - 2 < COLS else None] + [None] * 6
        slots.append(fold(items, 0))
    table = fold(slots, 1)
    for distance in (16, 32, 64):
        table = pair_add(table, pair_roll(table, distance, 1))
    mine = lane // 16 == row
    rows = [jnp.sum(jnp.where(mine, part, 0.0), axis=0, keepdims=True) for part in table]
    tile = jnp.where(row % 2 == 0, rows[0], rows[1])
    for t in range(gram.shape[0] // B):
        gram[B * t : B * (t + 1), :] = tile


def summed(ref):
    tiles = [ref[B * t : B * (t + 1), :] for t in range(ref.shape[0] // B)]
    pairs = [(t, pltpu.roll(t, B - 1, 0)) for t in tiles]
    while len(pairs) > 1:
        pairs = [pair_add(pairs[t], pairs[t + 1]) for t in range(0, len(pairs), 2)]
    total = pairs[0]
    for distance in (2, 4):
        total = pair_add(total, pair_roll(total, distance, 0))
    return total


def sum_kernel(parts, out):
    total = summed(parts)
    row = iota((B, LANES), 0)
    tile = jnp.where(row % 2 == 0, total[0], pltpu.roll(total[1], 1, 0))
    for t in range(out.shape[0] // B):
        out[B * t : B * (t + 1), :] = tile


def factor_kernel(scale, parts, block, basis_q, factor_r, hessenberg, inverse):
    shape = (2 * B, LANES)
    row = iota(shape, 0)
    lane = iota(shape, 1)

    def matrix(part):
        line = jnp.broadcast_to(part[0:1, :], shape)
        out = jnp.zeros(shape, F32)
        for r in range(B):
            moved = line if r == 0 else pltpu.roll(line, LANES - 16 * r, 1)
            out = jnp.where((row == r) & (lane < COLS), moved, out)
        out = jnp.where((row == S) & (lane < 7), pltpu.roll(line, LANES - 9, 1), out)
        return jnp.where((row == S) & ((lane == 7) | (lane == 8)), pltpu.roll(line, LANES - 18, 1), out)

    high, low = (matrix(part) for part in summed(parts))
    high = jnp.where((lane == row + 64) & (row < COLS), 1.0, high)
    pivots = jnp.ones(shape, F32)
    for j in range(COLS):
        d = tuple(jnp.broadcast_to(part[j : j + 1, j : j + 1], shape) for part in (high, low))
        pivots = jnp.where(row == j, d[0], pivots)
        if j == S:
            break
        top = tuple(jnp.broadcast_to(part[j : j + 1, :], shape) for part in (high, low))
        col = tuple(jnp.broadcast_to(part[:, j : j + 1], shape) for part in (high, low))
        inv = 1.0 / d[0]
        ratio = col[0] * inv
        back, err = two_prod(ratio, d[0])
        rest = (((col[0] - back) - err) + (col[1] - ratio * d[1])) * inv
        ratio = fast_two_sum(ratio, rest)
        change = pair_mul(ratio, top)
        change = tuple(jnp.where(row > j, -part, 0.0) for part in change)
        high, low = pair_add((high, low), change)
    root = jnp.sqrt(pivots)
    scaled = high / root
    upper = jnp.where((lane >= row) & (lane < COLS) & (row < COLS), scaled, 0.0)
    lower = jnp.where((lane <= row) & (row < COLS), pltpu.roll(scaled, 64, 1), 0.0)
    factor_r[...] = (upper / scale)[:COLS, :COLS]
    right = pltpu.roll(upper, LANES - 1, 1)
    product = CENTER * upper + jnp.where(lane == 0, HALF, 0.5 * HALF) * right + (0.5 * HALF) * pltpu.roll(upper, 1, 1)
    product = jnp.where(lane < S, product, 0.0)
    small = lax.dot_general(
        jnp.where(lane < S, lower, 0.0),
        product,
        (((1,), (1,)), ((), ())),
        precision=lax.Precision.HIGHEST,
        preferred_element_type=F32,
    )
    hessenberg[...] = small[:S, :COLS]
    lower = lower * scale
    for k in range(COLS):
        inverse[k] = jnp.broadcast_to(lower[:, k : k + 1], shape)
    for j in range(COLS):
        total = None
        for k in range(j + 1):
            factor = jnp.broadcast_to(inverse[k, j : j + 1, :], (B, LANES))[None]
            term = factor * block[k]
            total = term if total is None else total + term
        basis_q[j] = total


def paired(array, axis, first):
    count = lax.axis_size(axis)
    lower = range(first, count - 1, 2)
    return lax.ppermute(array, axis, [(i, i + 1) for i in lower] + [(i + 1, i) for i in lower])


def body(previous_basis, restart_column, diffusivity, speed, upwind):
    count_x, count_y = lax.axis_size("gx"), lax.axis_size("gz")
    even = jnp.stack([1 - lax.axis_index("gx") % 2, 1 - lax.axis_index("gz") % 2]).astype(jnp.int32)
    faces = (3, B, B, LANES)
    own = pl.pallas_call(
        pack_kernel,
        out_shape=jax.ShapeDtypeStruct((FIELDS, B, B, LANES), F32),
        in_specs=[SMEM] + [HBM] * 4,
        out_specs=VMEM,
        scratch_shapes=[
            pltpu.VMEM(faces, F32),
            pltpu.VMEM(faces, F32),
            pltpu.VMEM(faces, jnp.int32),
            pltpu.SemaphoreType.DMA((4,)),
        ],
        compiler_params=ALL_VMEM,
        name="pack",
    )(restart_column, previous_basis, diffusivity, speed, upwind)
    first_x = paired(own, "gx", 0)
    second_x = paired(own, "gx", 1)
    brick = jax.ShapeDtypeStruct((FIELDS, B, B, LANES), F32)
    kept = pl.pallas_call(
        keep_kernel, out_shape=brick, in_specs=[VMEM], out_specs=VMEM, compiler_params=PARAMS, name="keep"
    )(own)
    first_y = paired(kept, "gz", 0)
    second_y = paired(kept, "gz", 1)
    strip, to_first, to_second = pl.pallas_call(
        corner_kernel,
        out_shape=(jax.ShapeDtypeStruct((FIELDS, 2 * B, B, LANES), F32), brick, brick),
        in_specs=[SMEM] + [VMEM] * 2,
        out_specs=(VMEM,) * 3,
        compiler_params=PARAMS,
        name="corners",
    )(even, first_x, second_x)
    first_corner = paired(to_first, "gz", 0)
    second_corner = paired(to_second, "gz", 1)
    wide = (WIDE, WIDE, LANES)
    block, gram = pl.pallas_call(
        basis_kernel,
        out_shape=(
            jax.ShapeDtypeStruct((COLS, B, B, LANES), F32),
            jax.ShapeDtypeStruct((2 * count_y, LANES), F32),
        ),
        in_specs=[SMEM] + [VMEM] * 6,
        out_specs=(VMEM, VMEM),
        scratch_shapes=[
            pltpu.VMEM((FIELDS,) + wide, F32),
            pltpu.VMEM((2,) + wide, F32),
            pltpu.VMEM((COLS, B, B, LANES), F32),
            pltpu.VMEM((COLS, B, B, LANES), F32),
        ],
        compiler_params=PARAMS,
        name="basis",
    )(even, kept, strip, first_y, second_y, first_corner, second_corner)
    parts = lax.all_to_all(gram, "gz", 0, 0, tiled=True)
    line = pl.pallas_call(
        sum_kernel,
        out_shape=jax.ShapeDtypeStruct((2 * count_x, LANES), F32),
        in_specs=[VMEM],
        out_specs=VMEM,
        compiler_params=PARAMS,
        name="line_sum",
    )(parts)
    parts = lax.all_to_all(line, "gx", 0, 0, tiled=True)
    scale = math.sqrt(B * B * LANES * count_x * count_y)
    basis_q, factor_r, hessenberg = pl.pallas_call(
        lambda *refs: factor_kernel(scale, *refs),
        out_shape=(
            jax.ShapeDtypeStruct((COLS, B, B, LANES), F32),
            jax.ShapeDtypeStruct((COLS, COLS), F32),
            jax.ShapeDtypeStruct((S, COLS), F32),
        ),
        in_specs=[VMEM] * 2,
        out_specs=(VMEM,) * 3,
        scratch_shapes=[pltpu.VMEM((COLS, 2 * B, LANES), F32)],
        compiler_params=PARAMS,
        name="factor",
    )(parts, block)
    return basis_q, factor_r, jnp.transpose(hessenberg)


def solution(mesh):
    return jax.shard_map(
        body,
        mesh=mesh,
        in_specs=(
            P(None, "gx", "gz", None),
            P(),
            P(None, "gx", "gz", None),
            P(None, "gx", "gz", None),
            P(None, "gx", "gz", None),
        ),
        out_specs=(P(None, "gx", "gz", None), P(), P()),
        check_vma=False,
    )
```

```python
import math

import jax
import jax.numpy as jnp
from jax import lax
from jax.experimental import pallas as pl
from jax.experimental.pallas import tpu as pltpu
from jax.sharding import PartitionSpec as P

S = 8
COLS = S + 1
CENTER = 2.5
HALF = 1.5
B = 8
WIDE = 3 * B
LANES = 128
FIELDS = 7
F32 = jnp.float32
VMEM = pl.BlockSpec(memory_space=pltpu.VMEM)
HBM = pl.BlockSpec(memory_space=pltpu.HBM)
SMEM = pl.BlockSpec(memory_space=pltpu.SMEM)
PARAMS = pltpu.CompilerParams(vmem_limit_bytes=16 * 1024 * 1024)
ALL_VMEM = pltpu.CompilerParams(vmem_limit_bytes=63 * 1024 * 1024)


def iota(shape, dim):
    return lax.broadcasted_iota(jnp.int32, shape, dim)


def two_sum(a, b):
    s = a + b
    t = s - a
    return s, (a - (s - t)) + (b - t)


def fast_two_sum(a, b):
    s = a + b
    return s, b - (s - a)


def split(a):
    c = a * 4097.0
    high = c - (c - a)
    return high, a - high


def two_prod(a, b):
    ah, al = split(a)
    bh, bl = split(b)
    p = a * b
    return p, ((ah * bh - p) + (ah * bl + al * bh)) + al * bl


def pair_add(a, b):
    s, e = two_sum(a[0], b[0])
    return fast_two_sum(s, e + (a[1] + b[1]))


def loose_add(a, b):
    s, e = two_sum(a[0], b[0])
    return s, e + (a[1] + b[1])


def pair_mul(a, b):
    p, e = two_prod(a[0], b[0])
    return fast_two_sum(p, e + (a[0] * b[1] + a[1] * b[0]))


def pair_roll(a, shift, axis):
    return tuple(pltpu.roll(part, shift, axis) for part in a)


def pair_where(mask, a, b):
    return tuple(jnp.where(mask, x, y) for x, y in zip(a, b))


def pack_kernel(column, basis, diffusivity_in, speed_in, upwind_in, out, diffusivity, speed, upwind, sems):
    copies = [
        pltpu.make_async_copy(src, dst, sems.at[n])
        for n, (src, dst) in enumerate(
            (
                (basis.at[column[0]], out.at[0]),
                (diffusivity_in, diffusivity),
                (speed_in, speed),
                (upwind_in, upwind),
            )
        )
    ]
    for copy in copies:
        copy.start()
    for copy in copies:
        copy.wait()
    factor = -2.0 / HALF
    for dim in range(3):
        flow = upwind[dim].astype(F32)
        out[1 + dim] = (diffusivity[dim] + speed[dim] * flow) * factor
        out[4 + dim] = (diffusivity[dim] + speed[dim] * (1.0 - flow)) * factor


def corner_kernel(even, second, first, strip, to_first, to_second):
    @pl.when(even[0] == 1)
    def _():
        strip[:, 0:B] = second[...]
        strip[:, B : 2 * B] = first[...]

    @pl.when(even[0] == 0)
    def _():
        strip[:, 0:B] = first[...]
        strip[:, B : 2 * B] = second[...]

    @pl.when(even[1] == 1)
    def _():
        emit_corners(strip, to_first, to_second)

    @pl.when(even[1] == 0)
    def _():
        emit_corners(strip, to_second, to_first)


def emit_corners(strip, to_next, to_last):
    row = iota((FIELDS, B, LANES), 1)
    for side in range(2):
        for m in range(1, 5):
            near = strip[:, B - m if side == 0 else B - 1 + m]
            at = 4 * side + m - 1
            if m == 4:
                to_next[:, at] = near
                to_last[:, at] = near
            else:
                far = strip[:, m if side == 0 else 2 * B - 1 - m]
                to_next[:, at] = jnp.where(row >= m, near, pltpu.roll(far, m, 1))
                to_last[:, at] = jnp.where(row < B - m, near, pltpu.roll(far, B - m, 1))


def keep_kernel(own, kept):
    kept[...] = own[...]


def start_fields(kept, strip, last, following, corner_last, corner_following, coeff, field):
    def wide(f, a):
        if B <= a < 2 * B:
            return jnp.concatenate([last[f, a - B], kept[f, a - B], following[f, a - B]], 0)
        side = 0 if a < B else 1
        m = B - a if side == 0 else a - (2 * B - 1)
        middle = strip[f, a if side == 0 else a - B]
        if m == B:
            lower = upper = jnp.zeros((B, LANES), F32)
        elif m <= 4:
            at = 4 * side + m - 1
            lower, upper = corner_last[f, at], corner_following[f, at]
        else:
            other = B - m
            at = 4 * side + other - 1
            lower = pltpu.roll(corner_last[f, at], B - other, 0)
            upper = pltpu.roll(corner_following[f, at], other, 0)
        return jnp.concatenate([lower, middle, upper], 0)

    lane = iota((WIDE, LANES), 1)
    zero = jnp.zeros((WIDE, LANES), F32)
    q_below = wide(4, 0)
    field[0, 0] = wide(0, 0)
    field[0, WIDE - 1] = wide(0, WIDE - 1)
    for a in range(1, WIDE - 1):
        field[0, a] = wide(0, a)
        p = [wide(1 + dim, a) for dim in range(3)]
        q = [wide(4 + dim, a) for dim in range(3)]
        inside = p[0] < 0.0
        qx = jnp.where(inside, q_below, zero)
        qy = jnp.where(inside, pltpu.roll(q[1], 1, 0), zero)
        qz = jnp.where(lane == 0, zero, pltpu.roll(q[2], 1, 1))
        q_below = q[0]
        coeff[0, a] = (-2.0 * (CENTER - 1.0) / HALF) - ((p[0] + p[1]) + (p[2] + qx) + (qy + qz))
        coeff[1, a] = p[0]
        coeff[2, a] = qx
        coeff[3, a] = p[1]
        coeff[4, a] = qy
        coeff[5, a] = jnp.where(lane == LANES - 1, zero, p[2])
        coeff[6, a] = qz


def basis_kernel(
    even, kept, strip, second, first, corner_second, corner_first, block, gram, coeff, field, high, low
):
    @pl.when(even[1] == 1)
    def _():
        start_fields(kept, strip, second, first, corner_second, corner_first, coeff, field)

    @pl.when(even[1] == 0)
    def _():
        start_fields(kept, strip, first, second, corner_first, corner_second, coeff, field)

    block[0] = kept[0]
    for k in range(1, COLS):
        src, dst = (k - 1) % 2, k % 2

        def layer(a, carry, k=k, src=src, dst=dst):
            v = field[src, a]
            x = coeff[0, a] * v + coeff[1, a] * field[src, a + 1] + coeff[2, a] * field[src, a - 1]
            y = coeff[3, a] * pltpu.roll(v, WIDE - 1, 0) + coeff[4, a] * pltpu.roll(v, 1, 0)
            z = coeff[5, a] * pltpu.roll(v, LANES - 1, 1) + coeff[6, a] * pltpu.roll(v, 1, 1)
            total = x + (y + z)
            new = 0.5 * total if k == 1 else total - field[dst, a]
            if k == S:
                block[k, a - B] = new[B : 2 * B]
            else:
                field[dst, a] = new
            return carry

        lax.fori_loop(k, WIDE - k, layer, 0, unroll=True)
        if k < S:
            block[k] = field[dst, B : 2 * B, B : 2 * B, :]

    for k in range(COLS):
        h, l = split(block[k])
        high[k] = h
        low[k] = l

    def product(i, j):
        total = None
        for x in range(B):
            ah, al, bh, bl = high[i, x], low[i, x], high[j, x], low[j, x]
            p = block[i, x] * block[j, x]
            e = ((ah * bh - p) + (ah * bl + al * bh)) + al * bl
            if total is None:
                total, rest = p, e
            else:
                total, err = two_sum(total, p)
                rest = rest + (e + err)
        return total, rest

    row = iota((B, LANES), 0)
    lane = iota((B, LANES), 1)
    nothing = (jnp.zeros((B, LANES), F32),) * 2

    def merged(a, b, distance, axis):
        if a is None and b is None:
            return None
        a = nothing if a is None else a
        b = nothing if b is None else b
        mask = ((row if axis == 0 else lane) & distance) == 0
        return loose_add(pair_where(mask, a, b), pair_roll(pair_where(mask, b, a), distance, axis))

    def fold(items, axis):
        distance = 1
        while len(items) > 1:
            items = [merged(items[t], items[t + 1], distance, axis) for t in range(0, len(items), 2)]
            distance *= 2
        return items[0]

    products = {(i, j): product(i, j) for i in range(COLS) for j in range(i, COLS)}
    slots = []
    for m in range(16):
        if m < COLS:
            items = [products[min(r, m), max(r, m)] for r in range(B)]
        else:
            items = [products[m - COLS, S]] + [products[m - 2, S] if m - 2 < COLS else None] + [None] * 6
        slots.append(fold(items, 0))
    table = fold(slots, 1)
    for distance in (16, 32, 64):
        table = loose_add(table, pair_roll(table, distance, 1))
    table = fast_two_sum(*table)
    mine = lane // 16 == row
    rows = [jnp.sum(jnp.where(mine, part, 0.0), axis=0, keepdims=True) for part in table]
    tile = jnp.where(row % 2 == 0, rows[0], rows[1])
    for t in range(gram.shape[0] // B):
        gram[B * t : B * (t + 1), :] = tile


def summed(ref):
    tiles = [ref[B * t : B * (t + 1), :] for t in range(ref.shape[0] // B)]
    pairs = [(t, pltpu.roll(t, B - 1, 0)) for t in tiles]
    while len(pairs) > 1:
        pairs = [pair_add(pairs[t], pairs[t + 1]) for t in range(0, len(pairs), 2)]
    total = pairs[0]
    for distance in (2, 4):
        total = pair_add(total, pair_roll(total, distance, 0))
    return total


def sum_kernel(parts, out):
    total = summed(parts)
    row = iota((B, LANES), 0)
    tile = jnp.where(row % 2 == 0, total[0], pltpu.roll(total[1], 1, 0))
    for t in range(out.shape[0] // B):
        out[B * t : B * (t + 1), :] = tile


def factor_kernel(scale, parts, block, basis_q, factor_r, hessenberg, inverse):
    shape = (2 * B, LANES)
    row = iota(shape, 0)
    lane = iota(shape, 1)

    def matrix(part):
        line = jnp.broadcast_to(part[0:1, :], shape)
        out = jnp.zeros(shape, F32)
        for r in range(B):
            moved = line if r == 0 else pltpu.roll(line, LANES - 16 * r, 1)
            out = jnp.where((row == r) & (lane < COLS), moved, out)
        out = jnp.where((row == S) & (lane < 7), pltpu.roll(line, LANES - 9, 1), out)
        return jnp.where((row == S) & ((lane == 7) | (lane == 8)), pltpu.roll(line, LANES - 18, 1), out)

    high, low = (matrix(part) for part in summed(parts))
    high = jnp.where((lane == row + 64) & (row < COLS), 1.0, high)
    pivots = jnp.ones(shape, F32)
    for j in range(COLS):
        d = tuple(jnp.broadcast_to(part[j : j + 1, j : j + 1], shape) for part in (high, low))
        pivots = jnp.where(row == j, d[0], pivots)
        if j == S:
            break
        top = tuple(jnp.broadcast_to(part[j : j + 1, :], shape) for part in (high, low))
        col = tuple(jnp.broadcast_to(part[:, j : j + 1], shape) for part in (high, low))
        inv = 1.0 / d[0]
        ratio = col[0] * inv
        back, err = two_prod(ratio, d[0])
        rest = (((col[0] - back) - err) + (col[1] - ratio * d[1])) * inv
        ratio = fast_two_sum(ratio, rest)
        change = pair_mul(ratio, top)
        change = tuple(jnp.where(row > j, -part, 0.0) for part in change)
        high, low = pair_add((high, low), change)
    root = jnp.sqrt(pivots)
    scaled = high / root
    upper = jnp.where((lane >= row) & (lane < COLS) & (row < COLS), scaled, 0.0)
    lower = jnp.where((lane <= row) & (row < COLS), pltpu.roll(scaled, 64, 1), 0.0)
    factor_r[...] = (upper / scale)[:COLS, :COLS]
    right = pltpu.roll(upper, LANES - 1, 1)
    product = CENTER * upper + jnp.where(lane == 0, HALF, 0.5 * HALF) * right + (0.5 * HALF) * pltpu.roll(upper, 1, 1)
    product = jnp.where(lane < S, product, 0.0)
    small = lax.dot_general(
        jnp.where(lane < S, lower, 0.0),
        product,
        (((1,), (1,)), ((), ())),
        precision=lax.Precision.HIGHEST,
        preferred_element_type=F32,
    )
    hessenberg[...] = small[:S, :COLS]
    lower = lower * scale
    for k in range(COLS):
        inverse[k] = jnp.broadcast_to(lower[:, k : k + 1], shape)
    for j in range(COLS):
        total = None
        for k in range(j + 1):
            factor = jnp.broadcast_to(inverse[k, j : j + 1, :], (B, LANES))[None]
            term = factor * block[k]
            total = term if total is None else total + term
        basis_q[j] = total


def paired(array, axis, first):
    count = lax.axis_size(axis)
    lower = range(first, count - 1, 2)
    return lax.ppermute(array, axis, [(i, i + 1) for i in lower] + [(i + 1, i) for i in lower])


def body(previous_basis, restart_column, diffusivity, speed, upwind):
    count_x, count_y = lax.axis_size("gx"), lax.axis_size("gz")
    even = jnp.stack([1 - lax.axis_index("gx") % 2, 1 - lax.axis_index("gz") % 2]).astype(jnp.int32)
    faces = (3, B, B, LANES)
    own = pl.pallas_call(
        pack_kernel,
        out_shape=jax.ShapeDtypeStruct((FIELDS, B, B, LANES), F32),
        in_specs=[SMEM] + [HBM] * 4,
        out_specs=VMEM,
        scratch_shapes=[
            pltpu.VMEM(faces, F32),
            pltpu.VMEM(faces, F32),
            pltpu.VMEM(faces, jnp.int32),
            pltpu.SemaphoreType.DMA((4,)),
        ],
        compiler_params=ALL_VMEM,
        name="pack",
    )(restart_column, previous_basis, diffusivity, speed, upwind)
    second_x = paired(own, "gx", 1)
    first_x = paired(own, "gx", 0)
    brick = jax.ShapeDtypeStruct((FIELDS, B, B, LANES), F32)
    kept = pl.pallas_call(
        keep_kernel, out_shape=brick, in_specs=[VMEM], out_specs=VMEM, compiler_params=PARAMS, name="keep"
    )(own)
    second_y = paired(kept, "gz", 1)
    first_y = paired(kept, "gz", 0)
    strip, to_first, to_second = pl.pallas_call(
        corner_kernel,
        out_shape=(jax.ShapeDtypeStruct((FIELDS, 2 * B, B, LANES), F32), brick, brick),
        in_specs=[SMEM] + [VMEM] * 2,
        out_specs=(VMEM,) * 3,
        compiler_params=PARAMS,
        name="corners",
    )(even, second_x, first_x)
    second_corner = paired(to_second, "gz", 1)
    first_corner = paired(to_first, "gz", 0)
    wide = (WIDE, WIDE, LANES)
    block, gram = pl.pallas_call(
        basis_kernel,
        out_shape=(
            jax.ShapeDtypeStruct((COLS, B, B, LANES), F32),
            jax.ShapeDtypeStruct((2 * count_y, LANES), F32),
        ),
        in_specs=[SMEM] + [VMEM] * 6,
        out_specs=(VMEM, VMEM),
        scratch_shapes=[
            pltpu.VMEM((FIELDS,) + wide, F32),
            pltpu.VMEM((2,) + wide, F32),
            pltpu.VMEM((COLS, B, B, LANES), F32),
            pltpu.VMEM((COLS, B, B, LANES), F32),
        ],
        compiler_params=PARAMS,
        name="basis",
    )(even, kept, strip, second_y, first_y, second_corner, first_corner)
    parts = lax.all_to_all(gram, "gz", 0, 0, tiled=True)
    line = pl.pallas_call(
        sum_kernel,
        out_shape=jax.ShapeDtypeStruct((2 * count_x, LANES), F32),
        in_specs=[VMEM],
        out_specs=VMEM,
        compiler_params=PARAMS,
        name="line_sum",
    )(parts)
    parts = lax.all_to_all(line, "gx", 0, 0, tiled=True)
    scale = math.sqrt(B * B * LANES * count_x * count_y)
    basis_q, factor_r, hessenberg = pl.pallas_call(
        lambda *refs: factor_kernel(scale, *refs),
        out_shape=(
            jax.ShapeDtypeStruct((COLS, B, B, LANES), F32),
            jax.ShapeDtypeStruct((COLS, COLS), F32),
            jax.ShapeDtypeStruct((S, COLS), F32),
        ),
        in_specs=[VMEM] * 2,
        out_specs=(VMEM,) * 3,
        scratch_shapes=[pltpu.VMEM((COLS, 2 * B, LANES), F32)],
        compiler_params=PARAMS,
        name="factor",
    )(parts, block)
    return basis_q, factor_r, jnp.transpose(hessenberg)


def solution(mesh):
    return jax.shard_map(
        body,
        mesh=mesh,
        in_specs=(
            P(None, "gx", "gz", None),
            P(),
            P(None, "gx", "gz", None),
            P(None, "gx", "gz", None),
            P(None, "gx", "gz", None),
        ),
        out_specs=(P(None, "gx", "gz", None), P(), P()),
        check_vma=False,
    )
```

```python
import math

import jax
import jax.numpy as jnp
from jax import lax
from jax.experimental import pallas as pl
from jax.experimental.pallas import tpu as pltpu
from jax.sharding import PartitionSpec as P

S = 8
COLS = S + 1
CENTER = 2.5
HALF = 1.5
B = 8
WIDE = 3 * B
LANES = 128
FIELDS = 7
F32 = jnp.float32
VMEM = pl.BlockSpec(memory_space=pltpu.VMEM)
HBM = pl.BlockSpec(memory_space=pltpu.HBM)
SMEM = pl.BlockSpec(memory_space=pltpu.SMEM)
PARAMS = pltpu.CompilerParams(vmem_limit_bytes=16 * 1024 * 1024)


def iota(shape, dim):
    return lax.broadcasted_iota(jnp.int32, shape, dim)


def two_sum(a, b):
    s = a + b
    t = s - a
    return s, (a - (s - t)) + (b - t)


def fast_two_sum(a, b):
    s = a + b
    return s, b - (s - a)


def split(a):
    c = a * 4097.0
    high = c - (c - a)
    return high, a - high


def two_prod(a, b):
    ah, al = split(a)
    bh, bl = split(b)
    p = a * b
    return p, ((ah * bh - p) + (ah * bl + al * bh)) + al * bl


def pair_add(a, b):
    s, e = two_sum(a[0], b[0])
    return fast_two_sum(s, e + (a[1] + b[1]))


def loose_add(a, b):
    s, e = two_sum(a[0], b[0])
    return s, e + (a[1] + b[1])


def pair_mul(a, b):
    p, e = two_prod(a[0], b[0])
    return fast_two_sum(p, e + (a[0] * b[1] + a[1] * b[0]))


def pair_roll(a, shift, axis):
    return tuple(pltpu.roll(part, shift, axis) for part in a)


def pair_where(mask, a, b):
    return tuple(jnp.where(mask, x, y) for x, y in zip(a, b))


def pack_kernel(column, basis, diffusivity_in, speed_in, upwind_in, out, diffusivity, speed, upwind, sems):
    copies = [
        pltpu.make_async_copy(src, dst, sems.at[n])
        for n, (src, dst) in enumerate(
            (
                (basis.at[column[0]], out.at[0]),
                (diffusivity_in, diffusivity),
                (speed_in, speed),
                (upwind_in, upwind),
            )
        )
    ]
    for copy in copies:
        copy.start()
    for copy in copies:
        copy.wait()
    factor = -2.0 / HALF
    for dim in range(3):
        flow = upwind[dim].astype(F32)
        out[1 + dim] = (diffusivity[dim] + speed[dim] * flow) * factor
        out[4 + dim] = (diffusivity[dim] + speed[dim] * (1.0 - flow)) * factor


def corner_kernel(even, second, first, strip, to_first, to_second):
    @pl.when(even[0] == 1)
    def _():
        strip[:, 0:B] = second[...]
        strip[:, B : 2 * B] = first[...]

    @pl.when(even[0] == 0)
    def _():
        strip[:, 0:B] = first[...]
        strip[:, B : 2 * B] = second[...]

    @pl.when(even[1] == 1)
    def _():
        emit_corners(strip, to_first, to_second)

    @pl.when(even[1] == 0)
    def _():
        emit_corners(strip, to_second, to_first)


def emit_corners(strip, to_next, to_last):
    row = iota((FIELDS, B, LANES), 1)
    for side in range(2):
        for m in range(1, 5):
            near = strip[:, B - m if side == 0 else B - 1 + m]
            at = 4 * side + m - 1
            if m == 4:
                to_next[:, at] = near
                to_last[:, at] = near
            else:
                far = strip[:, m if side == 0 else 2 * B - 1 - m]
                to_next[:, at] = jnp.where(row >= m, near, pltpu.roll(far, m, 1))
                to_last[:, at] = jnp.where(row < B - m, near, pltpu.roll(far, B - m, 1))


def start_fields(own, strip, last, following, corner_last, corner_following, coeff, field):
    def wide(f, a):
        if B <= a < 2 * B:
            return jnp.concatenate([last[f, a - B], own[f, a - B], following[f, a - B]], 0)
        side = 0 if a < B else 1
        m = B - a if side == 0 else a - (2 * B - 1)
        middle = strip[f, a if side == 0 else a - B]
        if m == B:
            lower = upper = jnp.zeros((B, LANES), F32)
        elif m <= 4:
            at = 4 * side + m - 1
            lower, upper = corner_last[f, at], corner_following[f, at]
        else:
            other = B - m
            at = 4 * side + other - 1
            lower = pltpu.roll(corner_last[f, at], B - other, 0)
            upper = pltpu.roll(corner_following[f, at], other, 0)
        return jnp.concatenate([lower, middle, upper], 0)

    lane = iota((WIDE, LANES), 1)
    zero = jnp.zeros((WIDE, LANES), F32)
    q_below = wide(4, 0)
    field[0, 0] = wide(0, 0)
    field[0, WIDE - 1] = wide(0, WIDE - 1)
    for a in range(1, WIDE - 1):
        field[0, a] = wide(0, a)
        p = [wide(1 + dim, a) for dim in range(3)]
        q = [wide(4 + dim, a) for dim in range(3)]
        inside = p[0] < 0.0
        qx = jnp.where(inside, q_below, zero)
        qy = jnp.where(inside, pltpu.roll(q[1], 1, 0), zero)
        qz = jnp.where(lane == 0, zero, pltpu.roll(q[2], 1, 1))
        q_below = q[0]
        coeff[0, a] = (-2.0 * (CENTER - 1.0) / HALF) - ((p[0] + p[1]) + (p[2] + qx) + (qy + qz))
        coeff[1, a] = p[0]
        coeff[2, a] = qx
        coeff[3, a] = p[1]
        coeff[4, a] = qy
        coeff[5, a] = jnp.where(lane == LANES - 1, zero, p[2])
        coeff[6, a] = qz


def basis_kernel(
    even, own, strip, second, first, corner_second, corner_first, block, gram, coeff, field, high, low
):
    @pl.when(even[1] == 1)
    def _():
        start_fields(own, strip, second, first, corner_second, corner_first, coeff, field)

    @pl.when(even[1] == 0)
    def _():
        start_fields(own, strip, first, second, corner_first, corner_second, coeff, field)

    block[0] = own[0]
    for k in range(1, COLS):
        src, dst = (k - 1) % 2, k % 2

        def layer(a, carry, k=k, src=src, dst=dst):
            v = field[src, a]
            x = coeff[0, a] * v + coeff[1, a] * field[src, a + 1] + coeff[2, a] * field[src, a - 1]
            y = coeff[3, a] * pltpu.roll(v, WIDE - 1, 0) + coeff[4, a] * pltpu.roll(v, 1, 0)
            z = coeff[5, a] * pltpu.roll(v, LANES - 1, 1) + coeff[6, a] * pltpu.roll(v, 1, 1)
            total = x + (y + z)
            new = 0.5 * total if k == 1 else total - field[dst, a]
            if k == S:
                block[k, a - B] = new[B : 2 * B]
            else:
                field[dst, a] = new
            return carry

        lax.fori_loop(k, WIDE - k, layer, 0, unroll=True)
        if k < S:
            block[k] = field[dst, B : 2 * B, B : 2 * B, :]

    for k in range(COLS):
        h, l = split(block[k])
        high[k] = h
        low[k] = l

    def product(i, j):
        total = None
        for x in range(B):
            ah, al, bh, bl = high[i, x], low[i, x], high[j, x], low[j, x]
            p = block[i, x] * block[j, x]
            e = ((ah * bh - p) + (ah * bl + al * bh)) + al * bl
            if total is None:
                total, rest = p, e
            else:
                total, err = two_sum(total, p)
                rest = rest + (e + err)
        return total, rest

    row = iota((B, LANES), 0)
    lane = iota((B, LANES), 1)
    nothing = (jnp.zeros((B, LANES), F32),) * 2

    def merged(a, b, distance, axis):
        if a is None and b is None:
            return None
        a = nothing if a is None else a
        b = nothing if b is None else b
        mask = ((row if axis == 0 else lane) & distance) == 0
        return loose_add(pair_where(mask, a, b), pair_roll(pair_where(mask, b, a), distance, axis))

    def fold(items, axis):
        distance = 1
        while len(items) > 1:
            items = [merged(items[t], items[t + 1], distance, axis) for t in range(0, len(items), 2)]
            distance *= 2
        return items[0]

    products = {(i, j): product(i, j) for i in range(COLS) for j in range(i, COLS)}
    slots = []
    for m in range(16):
        if m < COLS:
            items = [products[min(r, m), max(r, m)] for r in range(B)]
        else:
            items = [products[m - COLS, S]] + [products[m - 2, S] if m - 2 < COLS else None] + [None] * 6
        slots.append(fold(items, 0))
    table = fold(slots, 1)
    for distance in (16, 32, 64):
        table = loose_add(table, pair_roll(table, distance, 1))
    table = fast_two_sum(*table)
    mine = lane // 16 == row
    rows = [jnp.sum(jnp.where(mine, part, 0.0), axis=0, keepdims=True) for part in table]
    tile = jnp.where(row % 2 == 0, rows[0], rows[1])
    for t in range(gram.shape[0] // B):
        gram[B * t : B * (t + 1), :] = tile


def summed(ref):
    tiles = [ref[B * t : B * (t + 1), :] for t in range(ref.shape[0] // B)]
    pairs = [(t, pltpu.roll(t, B - 1, 0)) for t in tiles]
    while len(pairs) > 1:
        pairs = [pair_add(pairs[t], pairs[t + 1]) for t in range(0, len(pairs), 2)]
    total = pairs[0]
    for distance in (2, 4):
        total = pair_add(total, pair_roll(total, distance, 0))
    return total


def sum_kernel(parts, out):
    total = summed(parts)
    row = iota((B, LANES), 0)
    tile = jnp.where(row % 2 == 0, total[0], pltpu.roll(total[1], 1, 0))
    for t in range(out.shape[0] // B):
        out[B * t : B * (t + 1), :] = tile


def factor_kernel(scale, parts, block, basis_q, factor_r, hessenberg, inverse):
    shape = (2 * B, LANES)
    row = iota(shape, 0)
    lane = iota(shape, 1)

    def matrix(part):
        line = jnp.broadcast_to(part[0:1, :], shape)
        out = jnp.zeros(shape, F32)
        for r in range(B):
            moved = line if r == 0 else pltpu.roll(line, LANES - 16 * r, 1)
            out = jnp.where((row == r) & (lane < COLS), moved, out)
        out = jnp.where((row == S) & (lane < 7), pltpu.roll(line, LANES - 9, 1), out)
        return jnp.where((row == S) & ((lane == 7) | (lane == 8)), pltpu.roll(line, LANES - 18, 1), out)

    high, low = (matrix(part) for part in summed(parts))
    high = jnp.where((lane == row + 64) & (row < COLS), 1.0, high)
    pivots = jnp.ones(shape, F32)
    for j in range(COLS):
        d = tuple(jnp.broadcast_to(part[j : j + 1, j : j + 1], shape) for part in (high, low))
        pivots = jnp.where(row == j, d[0], pivots)
        if j == S:
            break
        top = tuple(jnp.broadcast_to(part[j : j + 1, :], shape) for part in (high, low))
        col = tuple(jnp.broadcast_to(part[:, j : j + 1], shape) for part in (high, low))
        inv = 1.0 / d[0]
        ratio = col[0] * inv
        back, err = two_prod(ratio, d[0])
        rest = (((col[0] - back) - err) + (col[1] - ratio * d[1])) * inv
        ratio = fast_two_sum(ratio, rest)
        change = pair_mul(ratio, top)
        change = tuple(jnp.where(row > j, -part, 0.0) for part in change)
        high, low = pair_add((high, low), change)
    root = jnp.sqrt(pivots)
    scaled = high / root
    upper = jnp.where((lane >= row) & (lane < COLS) & (row < COLS), scaled, 0.0)
    lower = jnp.where((lane <= row) & (row < COLS), pltpu.roll(scaled, 64, 1), 0.0)
    factor_r[...] = (upper / scale)[:COLS, :COLS]
    right = pltpu.roll(upper, LANES - 1, 1)
    product = CENTER * upper + jnp.where(lane == 0, HALF, 0.5 * HALF) * right + (0.5 * HALF) * pltpu.roll(upper, 1, 1)
    product = jnp.where(lane < S, product, 0.0)
    small = lax.dot_general(
        jnp.where(lane < S, lower, 0.0),
        product,
        (((1,), (1,)), ((), ())),
        precision=lax.Precision.HIGHEST,
        preferred_element_type=F32,
    )
    hessenberg[...] = small[:S, :COLS]
    lower = lower * scale
    for k in range(COLS):
        inverse[k] = jnp.broadcast_to(lower[:, k : k + 1], shape)
    for j in range(COLS):
        total = None
        for k in range(j + 1):
            factor = jnp.broadcast_to(inverse[k, j : j + 1, :], (B, LANES))[None]
            term = factor * block[k]
            total = term if total is None else total + term
        basis_q[j] = total


def paired(array, axis, first):
    count = lax.axis_size(axis)
    lower = range(first, count - 1, 2)
    return lax.ppermute(array, axis, [(i, i + 1) for i in lower] + [(i + 1, i) for i in lower])


def in_hbm(array):
    return pltpu.with_memory_space_constraint(array, pltpu.HBM)


def body(previous_basis, restart_column, diffusivity, speed, upwind):
    count_x, count_y = lax.axis_size("gx"), lax.axis_size("gz")
    even = jnp.stack([1 - lax.axis_index("gx") % 2, 1 - lax.axis_index("gz") % 2]).astype(jnp.int32)
    faces = (3, B, B, LANES)
    own = pl.pallas_call(
        pack_kernel,
        out_shape=pltpu.VMEM((FIELDS, B, B, LANES), F32),
        in_specs=[SMEM] + [HBM] * 4,
        out_specs=VMEM,
        scratch_shapes=[
            pltpu.VMEM(faces, F32),
            pltpu.VMEM(faces, F32),
            pltpu.VMEM(faces, jnp.int32),
            pltpu.SemaphoreType.DMA((4,)),
        ],
        compiler_params=PARAMS,
        name="pack",
    )(restart_column, *(in_hbm(array) for array in (previous_basis, diffusivity, speed, upwind)))
    second_x = paired(own, "gx", 1)
    first_x = paired(own, "gx", 0)
    brick = jax.ShapeDtypeStruct((FIELDS, B, B, LANES), F32)
    second_y = paired(own, "gz", 1)
    first_y = paired(own, "gz", 0)
    strip, to_first, to_second = pl.pallas_call(
        corner_kernel,
        out_shape=(jax.ShapeDtypeStruct((FIELDS, 2 * B, B, LANES), F32), brick, brick),
        in_specs=[SMEM] + [VMEM] * 2,
        out_specs=(VMEM,) * 3,
        compiler_params=PARAMS,
        name="corners",
    )(even, second_x, first_x)
    second_corner = paired(to_second, "gz", 1)
    first_corner = paired(to_first, "gz", 0)
    wide = (WIDE, WIDE, LANES)
    block, gram = pl.pallas_call(
        basis_kernel,
        out_shape=(
            jax.ShapeDtypeStruct((COLS, B, B, LANES), F32),
            jax.ShapeDtypeStruct((2 * count_y, LANES), F32),
        ),
        in_specs=[SMEM] + [VMEM] * 6,
        out_specs=(VMEM, VMEM),
        scratch_shapes=[
            pltpu.VMEM((FIELDS,) + wide, F32),
            pltpu.VMEM((2,) + wide, F32),
            pltpu.VMEM((COLS, B, B, LANES), F32),
            pltpu.VMEM((COLS, B, B, LANES), F32),
        ],
        compiler_params=PARAMS,
        name="basis",
    )(even, own, strip, second_y, first_y, second_corner, first_corner)
    parts = lax.all_to_all(gram, "gz", 0, 0, tiled=True)
    line = pl.pallas_call(
        sum_kernel,
        out_shape=jax.ShapeDtypeStruct((2 * count_x, LANES), F32),
        in_specs=[VMEM],
        out_specs=VMEM,
        compiler_params=PARAMS,
        name="line_sum",
    )(parts)
    parts = lax.all_to_all(line, "gx", 0, 0, tiled=True)
    scale = math.sqrt(B * B * LANES * count_x * count_y)
    basis_q, factor_r, hessenberg = pl.pallas_call(
        lambda *refs: factor_kernel(scale, *refs),
        out_shape=(
            jax.ShapeDtypeStruct((COLS, B, B, LANES), F32),
            jax.ShapeDtypeStruct((COLS, COLS), F32),
            jax.ShapeDtypeStruct((S, COLS), F32),
        ),
        in_specs=[VMEM] * 2,
        out_specs=(VMEM,) * 3,
        scratch_shapes=[pltpu.VMEM((COLS, 2 * B, LANES), F32)],
        compiler_params=PARAMS,
        name="factor",
    )(parts, block)
    return basis_q, factor_r, jnp.transpose(hessenberg)


def solution(mesh):
    return jax.shard_map(
        body,
        mesh=mesh,
        in_specs=(
            P(None, "gx", "gz", None),
            P(),
            P(None, "gx", "gz", None),
            P(None, "gx", "gz", None),
            P(None, "gx", "gz", None),
        ),
        out_specs=(P(None, "gx", "gz", None), P(), P()),
        check_vma=False,
    )
```

```python
import math

import jax
import jax.numpy as jnp
from jax import lax
from jax.experimental import pallas as pl
from jax.experimental.pallas import tpu as pltpu
from jax.sharding import PartitionSpec as P

S = 8
COLS = S + 1
CENTER = 2.5
HALF = 1.5
B = 8
WIDE = 3 * B
LANES = 128
FIELDS = 7
NEAR_X = (1, 2, 3, 5, 6)
FAR_X = 2 * B
TILES_X = FAR_X + (B - 1) * len(NEAR_X)
REACH = (8, 7, 7, 7, 8, 8, 7)
HALVES = tuple(reach // 2 for reach in REACH)
CORNER = tuple(2 * sum(HALVES[:f]) for f in range(FIELDS))
TILES_CORNER = 2 * sum(HALVES)
F32 = jnp.float32
VMEM = pl.BlockSpec(memory_space=pltpu.VMEM)
HBM = pl.BlockSpec(memory_space=pltpu.HBM)
SMEM = pl.BlockSpec(memory_space=pltpu.SMEM)
PARAMS = pltpu.CompilerParams(vmem_limit_bytes=16 * 1024 * 1024)


def iota(shape, dim):
    return lax.broadcasted_iota(jnp.int32, shape, dim)


def two_sum(a, b):
    s = a + b
    t = s - a
    return s, (a - (s - t)) + (b - t)


def fast_two_sum(a, b):
    s = a + b
    return s, b - (s - a)


def split(a):
    c = a * 4097.0
    high = c - (c - a)
    return high, a - high


def two_prod(a, b):
    ah, al = split(a)
    bh, bl = split(b)
    p = a * b
    return p, ((ah * bh - p) + (ah * bl + al * bh)) + al * bl


def pair_add(a, b):
    s, e = two_sum(a[0], b[0])
    return fast_two_sum(s, e + (a[1] + b[1]))


def loose_add(a, b):
    s, e = two_sum(a[0], b[0])
    return s, e + (a[1] + b[1])


def loose_mul(a, b):
    p, e = two_prod(a[0], b[0])
    return p, e + (a[0] * b[1] + a[1] * b[0])


def pair_roll(a, shift, axis):
    return tuple(pltpu.roll(part, shift, axis) for part in a)


def pair_where(mask, a, b):
    return tuple(jnp.where(mask, x, y) for x, y in zip(a, b))


def pack_kernel(
    column, even, basis, diffusivity_in, speed_in, upwind_in, out, to_first, to_second, diffusivity, speed, upwind, sems
):
    copies = [
        pltpu.make_async_copy(src, dst, sems.at[n])
        for n, (src, dst) in enumerate(
            (
                (basis.at[column[0]], out.at[0]),
                (diffusivity_in, diffusivity),
                (speed_in, speed),
                (upwind_in, upwind),
            )
        )
    ]
    for copy in copies:
        copy.start()
    for copy in copies:
        copy.wait()
    factor = -2.0 / HALF
    for dim in range(3):
        flow = upwind[dim].astype(F32)
        out[1 + dim] = (diffusivity[dim] + speed[dim] * flow) * factor
        out[4 + dim] = (diffusivity[dim] + speed[dim] * (1.0 - flow)) * factor

    def emit(target, start):
        target[0:B] = out[0]
        target[B:FAR_X] = out[4]
        for n, f in enumerate(NEAR_X):
            target[FAR_X + (B - 1) * n : FAR_X + (B - 1) * (n + 1)] = out[f, start : start + B - 1]

    @pl.when(even[0] == 1)
    def _():
        emit(to_first, 1)
        emit(to_second, 0)

    @pl.when(even[0] == 0)
    def _():
        emit(to_first, 0)
        emit(to_second, 1)


def corner_kernel(even, second, first, strip, to_first, to_second):
    def place(part, side, start):
        strip[0, B * side : B * (side + 1)] = part[0:B]
        strip[4, B * side : B * (side + 1)] = part[B:FAR_X]
        for n, f in enumerate(NEAR_X):
            strip[f, B * side + start : B * (side + 1) - 1 + start] = part[FAR_X + (B - 1) * n : FAR_X + (B - 1) * (n + 1)]
            strip[f, 0 if side == 0 else 2 * B - 1] = jnp.zeros((B, LANES), F32)

    @pl.when(even[0] == 1)
    def _():
        place(second, 0, 1)
        place(first, 1, 0)

    @pl.when(even[0] == 0)
    def _():
        place(first, 0, 1)
        place(second, 1, 0)

    @pl.when(even[1] == 1)
    def _():
        emit_corners(strip, to_first, to_second)

    @pl.when(even[1] == 0)
    def _():
        emit_corners(strip, to_second, to_first)


def emit_corners(strip, to_next, to_last):
    row = iota((B, LANES), 0)
    for f in range(FIELDS):
        for side in range(2):
            for m in range(1, HALVES[f] + 1):
                near = strip[f, B - m if side == 0 else B - 1 + m]
                at = CORNER[f] + HALVES[f] * side + m - 1
                other = REACH[f] - m
                if m == other:
                    to_next[at] = near
                    to_last[at] = near
                else:
                    far = strip[f, B - other if side == 0 else B - 1 + other]
                    to_next[at] = jnp.where(row >= m, near, pltpu.roll(far, m, 0))
                    to_last[at] = jnp.where(row < B - m, near, pltpu.roll(far, B - m, 0))


def start_fields(own, strip, last, following, corner_last, corner_following, coeff, field):
    def wide(f, a):
        if B <= a < 2 * B:
            return jnp.concatenate([last[f, a - B], own[f, a - B], following[f, a - B]], 0)
        side = 0 if a < B else 1
        m = B - a if side == 0 else a - (2 * B - 1)
        middle = strip[f, a if side == 0 else a - B]
        other = REACH[f] - m
        at = CORNER[f] + HALVES[f] * side + min(m, other) - 1
        if other <= 0:
            lower = upper = jnp.zeros((B, LANES), F32)
        elif m <= other:
            lower, upper = corner_last[at], corner_following[at]
        else:
            lower = pltpu.roll(corner_last[at], B - other, 0)
            upper = pltpu.roll(corner_following[at], other, 0)
        return jnp.concatenate([lower, middle, upper], 0)

    lane = iota((WIDE, LANES), 1)
    zero = jnp.zeros((WIDE, LANES), F32)
    q_below = wide(4, 0)
    field[0, 0] = wide(0, 0)
    field[0, WIDE - 1] = wide(0, WIDE - 1)
    for a in range(1, WIDE - 1):
        field[0, a] = wide(0, a)
        p = [wide(1 + dim, a) for dim in range(3)]
        q = [wide(4 + dim, a) for dim in range(3)]
        inside = p[0] < 0.0
        qx = jnp.where(inside, q_below, zero)
        qy = jnp.where(inside, pltpu.roll(q[1], 1, 0), zero)
        qz = jnp.where(lane == 0, zero, pltpu.roll(q[2], 1, 1))
        q_below = q[0]
        coeff[0, a] = (-2.0 * (CENTER - 1.0) / HALF) - ((p[0] + p[1]) + (p[2] + qx) + (qy + qz))
        coeff[1, a] = p[0]
        coeff[2, a] = qx
        coeff[3, a] = p[1]
        coeff[4, a] = qy
        coeff[5, a] = jnp.where(lane == LANES - 1, zero, p[2])
        coeff[6, a] = qz


def basis_kernel(
    even, own, strip, second, first, corner_second, corner_first, block, gram, coeff, field, high, low
):
    @pl.when(even[1] == 1)
    def _():
        start_fields(own, strip, second, first, corner_second, corner_first, coeff, field)

    @pl.when(even[1] == 0)
    def _():
        start_fields(own, strip, first, second, corner_first, corner_second, coeff, field)

    block[0] = own[0]
    for k in range(1, COLS):
        src, dst = (k - 1) % 2, k % 2

        def layer(a, carry, k=k, src=src, dst=dst):
            v = field[src, a]
            x = coeff[0, a] * v + coeff[1, a] * field[src, a + 1] + coeff[2, a] * field[src, a - 1]
            y = coeff[3, a] * pltpu.roll(v, WIDE - 1, 0) + coeff[4, a] * pltpu.roll(v, 1, 0)
            z = coeff[5, a] * pltpu.roll(v, LANES - 1, 1) + coeff[6, a] * pltpu.roll(v, 1, 1)
            total = x + (y + z)
            new = 0.5 * total if k == 1 else total - field[dst, a]
            if k == S:
                block[k, a - B] = new[B : 2 * B]
            else:
                field[dst, a] = new
            return carry

        lax.fori_loop(k, WIDE - k, layer, 0, unroll=True)
        if k < S:
            block[k] = field[dst, B : 2 * B, B : 2 * B, :]

    for k in range(COLS):
        h, l = split(block[k])
        high[k] = h
        low[k] = l

    def product(i, j):
        total = None
        for x in range(B):
            ah, al, bh, bl = high[i, x], low[i, x], high[j, x], low[j, x]
            p = ah * bh
            e = ah * bl + al * block[j, x]
            if total is None:
                total, rest = p, e
            else:
                total, err = two_sum(total, p)
                rest = rest + (e + err)
        return total, rest

    row = iota((B, LANES), 0)
    lane = iota((B, LANES), 1)
    nothing = (jnp.zeros((B, LANES), F32),) * 2

    def merged(a, b, distance, axis):
        if a is None and b is None:
            return None
        a = nothing if a is None else a
        b = nothing if b is None else b
        mask = ((row if axis == 0 else lane) & distance) == 0
        return loose_add(pair_where(mask, a, b), pair_roll(pair_where(mask, b, a), distance, axis))

    def fold(items, axis):
        distance = 1
        while len(items) > 1:
            items = [merged(items[t], items[t + 1], distance, axis) for t in range(0, len(items), 2)]
            distance *= 2
        return items[0]

    products = {(i, j): product(i, j) for i in range(COLS) for j in range(i, COLS)}
    slots = []
    for m in range(16):
        if m < COLS:
            items = [products[min(r, m), max(r, m)] for r in range(B)]
        else:
            items = [products[m - COLS, S]] + [products[m - 2, S] if m - 2 < COLS else None] + [None] * 6
        slots.append(fold(items, 0))
    table = fold(slots, 1)
    for distance in (16, 32, 64):
        table = loose_add(table, pair_roll(table, distance, 1))
    table = fast_two_sum(*table)
    mine = lane // 16 == row
    rows = [jnp.sum(jnp.where(mine, part, 0.0), axis=0, keepdims=True) for part in table]
    tile = jnp.where(row % 2 == 0, rows[0], rows[1])
    for t in range(gram.shape[0] // B):
        gram[B * t : B * (t + 1), :] = tile


def summed(ref):
    tiles = [ref[B * t : B * (t + 1), :] for t in range(ref.shape[0] // B)]
    pairs = [(t, pltpu.roll(t, B - 1, 0)) for t in tiles]
    while len(pairs) > 1:
        pairs = [pair_add(pairs[t], pairs[t + 1]) for t in range(0, len(pairs), 2)]
    total = pairs[0]
    for distance in (2, 4):
        total = pair_add(total, pair_roll(total, distance, 0))
    return total


def sum_kernel(parts, out):
    total = summed(parts)
    row = iota((B, LANES), 0)
    tile = jnp.where(row % 2 == 0, total[0], pltpu.roll(total[1], 1, 0))
    for t in range(out.shape[0] // B):
        out[B * t : B * (t + 1), :] = tile


def factor_kernel(scale, parts, block, basis_q, factor_r, hessenberg, inverse):
    shape = (2 * B, LANES)
    row = iota(shape, 0)
    lane = iota(shape, 1)

    def matrix(part):
        line = jnp.broadcast_to(part[0:1, :], shape)
        out = jnp.zeros(shape, F32)
        for r in range(B):
            moved = line if r == 0 else pltpu.roll(line, LANES - 16 * r, 1)
            out = jnp.where((row == r) & (lane < COLS), moved, out)
        out = jnp.where((row == S) & (lane < 7), pltpu.roll(line, LANES - 9, 1), out)
        return jnp.where((row == S) & ((lane == 7) | (lane == 8)), pltpu.roll(line, LANES - 18, 1), out)

    high, low = (matrix(part) for part in summed(parts))
    high = jnp.where((lane == row + 64) & (row < COLS), 1.0, high)
    pivots = jnp.ones(shape, F32)
    for j in range(COLS):
        d = tuple(jnp.broadcast_to(part[j : j + 1, j : j + 1], shape) for part in (high, low))
        pivots = jnp.where(row == j, d[0], pivots)
        if j == S:
            break
        top = tuple(jnp.broadcast_to(part[j : j + 1, :], shape) for part in (high, low))
        col = tuple(jnp.broadcast_to(part[:, j : j + 1], shape) for part in (high, low))
        inv = 1.0 / d[0]
        ratio = col[0] * inv
        back, err = two_prod(ratio, d[0])
        rest = (((col[0] - back) - err) + (col[1] - ratio * d[1])) * inv
        change = loose_mul((ratio, rest), top)
        change = tuple(jnp.where(row > j, -part, 0.0) for part in change)
        high, low = pair_add((high, low), change)
    root = jnp.sqrt(pivots)
    scaled = high / root
    upper = jnp.where((lane >= row) & (lane < COLS) & (row < COLS), scaled, 0.0)
    lower = jnp.where((lane <= row) & (row < COLS), pltpu.roll(scaled, 64, 1), 0.0)
    factor_r[...] = (upper / scale)[:COLS, :COLS]
    right = pltpu.roll(upper, LANES - 1, 1)
    product = CENTER * upper + jnp.where(lane == 0, HALF, 0.5 * HALF) * right + (0.5 * HALF) * pltpu.roll(upper, 1, 1)
    product = jnp.where(lane < S, product, 0.0)
    small = lax.dot_general(
        jnp.where(lane < S, lower, 0.0),
        product,
        (((1,), (1,)), ((), ())),
        precision=lax.Precision.HIGHEST,
        preferred_element_type=F32,
    )
    hessenberg[...] = small[:S, :COLS]
    lower = lower * scale
    for k in range(COLS):
        inverse[k] = jnp.broadcast_to(lower[:, k : k + 1], shape)
    for j in range(COLS):
        total = None
        for k in range(j + 1):
            factor = jnp.broadcast_to(inverse[k, j : j + 1, :], (B, LANES))[None]
            term = factor * block[k]
            total = term if total is None else total + term
        basis_q[j] = total


def paired(array, axis, first):
    count = lax.axis_size(axis)
    lower = range(first, count - 1, 2)
    return lax.ppermute(array, axis, [(i, i + 1) for i in lower] + [(i + 1, i) for i in lower])


def in_hbm(array):
    return pltpu.with_memory_space_constraint(array, pltpu.HBM)


def body(previous_basis, restart_column, diffusivity, speed, upwind):
    count_x, count_y = lax.axis_size("gx"), lax.axis_size("gz")
    even = jnp.stack([1 - lax.axis_index("gx") % 2, 1 - lax.axis_index("gz") % 2]).astype(jnp.int32)
    faces = (3, B, B, LANES)
    part = (TILES_X, B, LANES)
    own, to_first, to_second = pl.pallas_call(
        pack_kernel,
        out_shape=(pltpu.VMEM((FIELDS, B, B, LANES), F32), pltpu.VMEM(part, F32), pltpu.VMEM(part, F32)),
        in_specs=[SMEM] * 2 + [HBM] * 4,
        out_specs=(VMEM,) * 3,
        scratch_shapes=[
            pltpu.VMEM(faces, F32),
            pltpu.VMEM(faces, F32),
            pltpu.VMEM(faces, jnp.int32),
            pltpu.SemaphoreType.DMA((4,)),
        ],
        compiler_params=PARAMS,
        name="pack",
    )(restart_column, even, *(in_hbm(array) for array in (previous_basis, diffusivity, speed, upwind)))
    second_x = paired(to_second, "gx", 1)
    first_x = paired(to_first, "gx", 0)
    corner = jax.ShapeDtypeStruct((TILES_CORNER, B, LANES), F32)
    second_y = paired(own, "gz", 1)
    first_y = paired(own, "gz", 0)
    strip, to_first, to_second = pl.pallas_call(
        corner_kernel,
        out_shape=(jax.ShapeDtypeStruct((FIELDS, 2 * B, B, LANES), F32), corner, corner),
        in_specs=[SMEM] + [VMEM] * 2,
        out_specs=(VMEM,) * 3,
        compiler_params=PARAMS,
        name="corners",
    )(even, second_x, first_x)
    second_corner = paired(to_second, "gz", 1)
    first_corner = paired(to_first, "gz", 0)
    wide = (WIDE, WIDE, LANES)
    block, gram = pl.pallas_call(
        basis_kernel,
        out_shape=(
            jax.ShapeDtypeStruct((COLS, B, B, LANES), F32),
            jax.ShapeDtypeStruct((2 * count_y, LANES), F32),
        ),
        in_specs=[SMEM] + [VMEM] * 6,
        out_specs=(VMEM, VMEM),
        scratch_shapes=[
            pltpu.VMEM((FIELDS,) + wide, F32),
            pltpu.VMEM((2,) + wide, F32),
            pltpu.VMEM((COLS, B, B, LANES), F32),
            pltpu.VMEM((COLS, B, B, LANES), F32),
        ],
        compiler_params=PARAMS,
        name="basis",
    )(even, own, strip, second_y, first_y, second_corner, first_corner)
    parts = lax.all_to_all(gram, "gz", 0, 0, tiled=True)
    line = pl.pallas_call(
        sum_kernel,
        out_shape=jax.ShapeDtypeStruct((2 * count_x, LANES), F32),
        in_specs=[VMEM],
        out_specs=VMEM,
        compiler_params=PARAMS,
        name="line_sum",
    )(parts)
    parts = lax.all_to_all(line, "gx", 0, 0, tiled=True)
    scale = math.sqrt(B * B * LANES * count_x * count_y)
    basis_q, factor_r, hessenberg = pl.pallas_call(
        lambda *refs: factor_kernel(scale, *refs),
        out_shape=(
            jax.ShapeDtypeStruct((COLS, B, B, LANES), F32),
            jax.ShapeDtypeStruct((COLS, COLS), F32),
            jax.ShapeDtypeStruct((S, COLS), F32),
        ),
        in_specs=[VMEM] * 2,
        out_specs=(VMEM,) * 3,
        scratch_shapes=[pltpu.VMEM((COLS, 2 * B, LANES), F32)],
        compiler_params=PARAMS,
        name="factor",
    )(parts, block)
    return basis_q, factor_r, jnp.transpose(hessenberg)


def solution(mesh):
    return jax.shard_map(
        body,
        mesh=mesh,
        in_specs=(
            P(None, "gx", "gz", None),
            P(),
            P(None, "gx", "gz", None),
            P(None, "gx", "gz", None),
            P(None, "gx", "gz", None),
        ),
        out_specs=(P(None, "gx", "gz", None), P(), P()),
        check_vma=False,
    )
```

```python
import math

import jax
import jax.numpy as jnp
from jax import lax
from jax.experimental import pallas as pl
from jax.experimental.pallas import tpu as pltpu
from jax.sharding import PartitionSpec as P

S = 8
COLS = S + 1
CENTER = 2.5
HALF = 1.5
B = 8
WIDE = 3 * B
LANES = 128
FIELDS = 7
NEAR_X = (1, 2, 3, 5, 6)
FAR_X = 2 * B
TILES_X = FAR_X + (B - 1) * len(NEAR_X)
REACH = (8, 7, 7, 7, 8, 8, 7)
HALVES = tuple(reach // 2 for reach in REACH)
CORNER = tuple(2 * sum(HALVES[:f]) for f in range(FIELDS))
TILES_CORNER = 2 * sum(HALVES)
F32 = jnp.float32
VMEM = pl.BlockSpec(memory_space=pltpu.VMEM)
HBM = pl.BlockSpec(memory_space=pltpu.HBM)
SMEM = pl.BlockSpec(memory_space=pltpu.SMEM)
PARAMS = pltpu.CompilerParams(vmem_limit_bytes=16 * 1024 * 1024)


def iota(shape, dim):
    return lax.broadcasted_iota(jnp.int32, shape, dim)


def two_sum(a, b):
    s = a + b
    t = s - a
    return s, (a - (s - t)) + (b - t)


def fast_two_sum(a, b):
    s = a + b
    return s, b - (s - a)


def split(a):
    c = a * 4097.0
    high = c - (c - a)
    return high, a - high


def two_prod(a, b):
    ah, al = split(a)
    bh, bl = split(b)
    p = a * b
    return p, ((ah * bh - p) + (ah * bl + al * bh)) + al * bl


def pair_add(a, b):
    s, e = two_sum(a[0], b[0])
    return fast_two_sum(s, e + (a[1] + b[1]))


def loose_add(a, b):
    s, e = two_sum(a[0], b[0])
    return s, e + (a[1] + b[1])


def loose_mul(a, b):
    p, e = two_prod(a[0], b[0])
    return p, e + (a[0] * b[1] + a[1] * b[0])


def pair_roll(a, shift, axis):
    return tuple(pltpu.roll(part, shift, axis) for part in a)


def pair_where(mask, a, b):
    return tuple(jnp.where(mask, x, y) for x, y in zip(a, b))


def pack_kernel(
    column, basis, diffusivity_in, speed_in, upwind_in, out, to_first, to_second, diffusivity, speed, upwind, sems
):
    copies = [
        pltpu.make_async_copy(src, dst, sems.at[n])
        for n, (src, dst) in enumerate(
            (
                (basis.at[column[0]], out.at[0]),
                (diffusivity_in, diffusivity),
                (speed_in, speed),
                (upwind_in, upwind),
            )
        )
    ]
    for copy in copies:
        copy.start()
    for copy in copies:
        copy.wait()
    factor = -2.0 / HALF
    for dim in range(3):
        flow = upwind[dim].astype(F32)
        out[1 + dim] = (diffusivity[dim] + speed[dim] * flow) * factor
        out[4 + dim] = (diffusivity[dim] + speed[dim] * (1.0 - flow)) * factor

    def emit(target, start):
        target[0:B] = out[0]
        target[B:FAR_X] = out[4]
        for n, f in enumerate(NEAR_X):
            target[FAR_X + (B - 1) * n : FAR_X + (B - 1) * (n + 1)] = out[f, start : start + B - 1]

    @pl.when(lax.rem(lax.axis_index("gx"), 2) == 0)
    def _():
        emit(to_first, 1)
        emit(to_second, 0)

    @pl.when(lax.rem(lax.axis_index("gx"), 2) == 1)
    def _():
        emit(to_first, 0)
        emit(to_second, 1)


def corner_kernel(second, first, strip, to_first, to_second):
    def place(part, side, start):
        strip[0, B * side : B * (side + 1)] = part[0:B]
        strip[4, B * side : B * (side + 1)] = part[B:FAR_X]
        for n, f in enumerate(NEAR_X):
            strip[f, B * side + start : B * (side + 1) - 1 + start] = part[FAR_X + (B - 1) * n : FAR_X + (B - 1) * (n + 1)]
            strip[f, 0 if side == 0 else 2 * B - 1] = jnp.zeros((B, LANES), F32)

    @pl.when(lax.rem(lax.axis_index("gx"), 2) == 0)
    def _():
        place(second, 0, 1)
        place(first, 1, 0)

    @pl.when(lax.rem(lax.axis_index("gx"), 2) == 1)
    def _():
        place(first, 0, 1)
        place(second, 1, 0)

    @pl.when(lax.rem(lax.axis_index("gz"), 2) == 0)
    def _():
        emit_corners(strip, to_first, to_second)

    @pl.when(lax.rem(lax.axis_index("gz"), 2) == 1)
    def _():
        emit_corners(strip, to_second, to_first)


def emit_corners(strip, to_next, to_last):
    row = iota((B, LANES), 0)
    for f in range(FIELDS):
        for side in range(2):
            for m in range(1, HALVES[f] + 1):
                near = strip[f, B - m if side == 0 else B - 1 + m]
                at = CORNER[f] + HALVES[f] * side + m - 1
                other = REACH[f] - m
                if m == other:
                    to_next[at] = near
                    to_last[at] = near
                else:
                    far = strip[f, B - other if side == 0 else B - 1 + other]
                    to_next[at] = jnp.where(row >= m, near, pltpu.roll(far, m, 0))
                    to_last[at] = jnp.where(row < B - m, near, pltpu.roll(far, B - m, 0))


def start_fields(own, strip, last, following, corner_last, corner_following, coeff, field):
    def wide(f, a):
        if B <= a < 2 * B:
            return jnp.concatenate([last[f, a - B], own[f, a - B], following[f, a - B]], 0)
        side = 0 if a < B else 1
        m = B - a if side == 0 else a - (2 * B - 1)
        middle = strip[f, a if side == 0 else a - B]
        other = REACH[f] - m
        at = CORNER[f] + HALVES[f] * side + min(m, other) - 1
        if other <= 0:
            lower = upper = jnp.zeros((B, LANES), F32)
        elif m <= other:
            lower, upper = corner_last[at], corner_following[at]
        else:
            lower = pltpu.roll(corner_last[at], B - other, 0)
            upper = pltpu.roll(corner_following[at], other, 0)
        return jnp.concatenate([lower, middle, upper], 0)

    lane = iota((WIDE, LANES), 1)
    zero = jnp.zeros((WIDE, LANES), F32)
    q_below = wide(4, 0)
    field[0, 0] = wide(0, 0)
    field[0, WIDE - 1] = wide(0, WIDE - 1)
    for a in range(1, WIDE - 1):
        field[0, a] = wide(0, a)
        p = [wide(1 + dim, a) for dim in range(3)]
        q = [wide(4 + dim, a) for dim in range(3)]
        inside = p[0] < 0.0
        qx = jnp.where(inside, q_below, zero)
        qy = jnp.where(inside, pltpu.roll(q[1], 1, 0), zero)
        qz = jnp.where(lane == 0, zero, pltpu.roll(q[2], 1, 1))
        q_below = q[0]
        coeff[0, a] = (-2.0 * (CENTER - 1.0) / HALF) - ((p[0] + p[1]) + (p[2] + qx) + (qy + qz))
        coeff[1, a] = p[0]
        coeff[2, a] = qx
        coeff[3, a] = p[1]
        coeff[4, a] = qy
        coeff[5, a] = jnp.where(lane == LANES - 1, zero, p[2])
        coeff[6, a] = qz


def basis_kernel(
    own, strip, second, first, corner_second, corner_first, block, gram, coeff, field, high, low
):
    @pl.when(lax.rem(lax.axis_index("gz"), 2) == 0)
    def _():
        start_fields(own, strip, second, first, corner_second, corner_first, coeff, field)

    @pl.when(lax.rem(lax.axis_index("gz"), 2) == 1)
    def _():
        start_fields(own, strip, first, second, corner_first, corner_second, coeff, field)

    block[0] = own[0]
    for k in range(1, COLS):
        src, dst = (k - 1) % 2, k % 2

        def layer(a, carry, k=k, src=src, dst=dst):
            v = field[src, a]
            x = coeff[0, a] * v + coeff[1, a] * field[src, a + 1] + coeff[2, a] * field[src, a - 1]
            y = coeff[3, a] * pltpu.roll(v, WIDE - 1, 0) + coeff[4, a] * pltpu.roll(v, 1, 0)
            z = coeff[5, a] * pltpu.roll(v, LANES - 1, 1) + coeff[6, a] * pltpu.roll(v, 1, 1)
            total = x + (y + z)
            new = 0.5 * total if k == 1 else total - field[dst, a]
            if k == S:
                block[k, a - B] = new[B : 2 * B]
            else:
                field[dst, a] = new
            return carry

        lax.fori_loop(k, WIDE - k, layer, 0, unroll=True)
        if k < S:
            block[k] = field[dst, B : 2 * B, B : 2 * B, :]

    for k in range(COLS):
        h, l = split(block[k])
        high[k] = h
        low[k] = l

    def product(i, j):
        total = None
        for x in range(B):
            ah, al, bh, bl = high[i, x], low[i, x], high[j, x], low[j, x]
            p = ah * bh
            e = ah * bl + al * block[j, x]
            if total is None:
                total, rest = p, e
            else:
                total, err = two_sum(total, p)
                rest = rest + (e + err)
        return total, rest

    row = iota((B, LANES), 0)
    lane = iota((B, LANES), 1)
    nothing = (jnp.zeros((B, LANES), F32),) * 2

    def merged(a, b, distance, axis):
        if a is None and b is None:
            return None
        a = nothing if a is None else a
        b = nothing if b is None else b
        mask = ((row if axis == 0 else lane) & distance) == 0
        return loose_add(pair_where(mask, a, b), pair_roll(pair_where(mask, b, a), distance, axis))

    def fold(items, axis):
        distance = 1
        while len(items) > 1:
            items = [merged(items[t], items[t + 1], distance, axis) for t in range(0, len(items), 2)]
            distance *= 2
        return items[0]

    products = {(i, j): product(i, j) for i in range(COLS) for j in range(i, COLS)}
    slots = []
    for m in range(16):
        if m < COLS:
            items = [products[min(r, m), max(r, m)] for r in range(B)]
        else:
            items = [products[m - COLS, S]] + [products[m - 2, S] if m - 2 < COLS else None] + [None] * 6
        slots.append(fold(items, 0))
    table = fold(slots, 1)
    for distance in (16, 32, 64):
        table = loose_add(table, pair_roll(table, distance, 1))
    table = fast_two_sum(*table)
    mine = lane // 16 == row
    rows = [jnp.sum(jnp.where(mine, part, 0.0), axis=0, keepdims=True) for part in table]
    tile = jnp.where(row % 2 == 0, rows[0], rows[1])
    for t in range(gram.shape[0] // B):
        gram[B * t : B * (t + 1), :] = tile


def summed(ref):
    tiles = [ref[B * t : B * (t + 1), :] for t in range(ref.shape[0] // B)]
    pairs = [(t, pltpu.roll(t, B - 1, 0)) for t in tiles]
    while len(pairs) > 1:
        pairs = [pair_add(pairs[t], pairs[t + 1]) for t in range(0, len(pairs), 2)]
    total = pairs[0]
    for distance in (2, 4):
        total = pair_add(total, pair_roll(total, distance, 0))
    return total


def sum_kernel(parts, out):
    total = summed(parts)
    row = iota((B, LANES), 0)
    tile = jnp.where(row % 2 == 0, total[0], pltpu.roll(total[1], 1, 0))
    for t in range(out.shape[0] // B):
        out[B * t : B * (t + 1), :] = tile


def factor_kernel(scale, parts, block, basis_q, factor_r, hessenberg, inverse):
    shape = (2 * B, LANES)
    row = iota(shape, 0)
    lane = iota(shape, 1)

    def matrix(part):
        line = jnp.broadcast_to(part[0:1, :], shape)
        out = jnp.zeros(shape, F32)
        for r in range(B):
            moved = line if r == 0 else pltpu.roll(line, LANES - 16 * r, 1)
            out = jnp.where((row == r) & (lane < COLS), moved, out)
        out = jnp.where((row == S) & (lane < 7), pltpu.roll(line, LANES - 9, 1), out)
        return jnp.where((row == S) & ((lane == 7) | (lane == 8)), pltpu.roll(line, LANES - 18, 1), out)

    high, low = (matrix(part) for part in summed(parts))
    high = jnp.where((lane == row + 64) & (row < COLS), 1.0, high)
    pivots = jnp.ones(shape, F32)
    for j in range(COLS):
        d = tuple(jnp.broadcast_to(part[j : j + 1, j : j + 1], shape) for part in (high, low))
        pivots = jnp.where(row == j, d[0], pivots)
        if j == S:
            break
        top = tuple(jnp.broadcast_to(part[j : j + 1, :], shape) for part in (high, low))
        col = tuple(jnp.broadcast_to(part[:, j : j + 1], shape) for part in (high, low))
        inv = 1.0 / d[0]
        ratio = col[0] * inv
        back, err = two_prod(ratio, d[0])
        rest = (((col[0] - back) - err) + (col[1] - ratio * d[1])) * inv
        change = loose_mul((ratio, rest), top)
        change = tuple(jnp.where(row > j, -part, 0.0) for part in change)
        high, low = pair_add((high, low), change)
    root = jnp.sqrt(pivots)
    scaled = high / root
    upper = jnp.where((lane >= row) & (lane < COLS) & (row < COLS), scaled, 0.0)
    lower = jnp.where((lane <= row) & (row < COLS), pltpu.roll(scaled, 64, 1), 0.0)
    factor_r[...] = (upper / scale)[:COLS, :COLS]
    right = pltpu.roll(upper, LANES - 1, 1)
    product = CENTER * upper + jnp.where(lane == 0, HALF, 0.5 * HALF) * right + (0.5 * HALF) * pltpu.roll(upper, 1, 1)
    product = jnp.where(lane < S, product, 0.0)
    small = lax.dot_general(
        jnp.where(lane < S, lower, 0.0),
        product,
        (((1,), (1,)), ((), ())),
        precision=lax.Precision.HIGHEST,
        preferred_element_type=F32,
    )
    hessenberg[...] = small[:S, :COLS]
    lower = lower * scale
    for k in range(COLS):
        inverse[k] = jnp.broadcast_to(lower[:, k : k + 1], shape)
    for j in range(COLS):
        total = None
        for k in range(j + 1):
            factor = jnp.broadcast_to(inverse[k, j : j + 1, :], (B, LANES))[None]
            term = factor * block[k]
            total = term if total is None else total + term
        basis_q[j] = total


def paired(array, axis, first):
    count = lax.axis_size(axis)
    lower = range(first, count - 1, 2)
    return lax.ppermute(array, axis, [(i, i + 1) for i in lower] + [(i + 1, i) for i in lower])


def in_hbm(array):
    return pltpu.with_memory_space_constraint(array, pltpu.HBM)


def body(previous_basis, restart_column, diffusivity, speed, upwind):
    count_x, count_y = lax.axis_size("gx"), lax.axis_size("gz")
    faces = (3, B, B, LANES)
    part = (TILES_X, B, LANES)
    own, to_first, to_second = pl.pallas_call(
        pack_kernel,
        out_shape=(pltpu.VMEM((FIELDS, B, B, LANES), F32), pltpu.VMEM(part, F32), pltpu.VMEM(part, F32)),
        in_specs=[SMEM] + [HBM] * 4,
        out_specs=(VMEM,) * 3,
        scratch_shapes=[
            pltpu.VMEM(faces, F32),
            pltpu.VMEM(faces, F32),
            pltpu.VMEM(faces, jnp.int32),
            pltpu.SemaphoreType.DMA((4,)),
        ],
        compiler_params=PARAMS,
        name="pack",
    )(restart_column, *(in_hbm(array) for array in (previous_basis, diffusivity, speed, upwind)))
    second_x = paired(to_second, "gx", 1)
    first_x = paired(to_first, "gx", 0)
    corner = jax.ShapeDtypeStruct((TILES_CORNER, B, LANES), F32)
    second_y = paired(own, "gz", 1)
    first_y = paired(own, "gz", 0)
    strip, to_first, to_second = pl.pallas_call(
        corner_kernel,
        out_shape=(jax.ShapeDtypeStruct((FIELDS, 2 * B, B, LANES), F32), corner, corner),
        in_specs=[VMEM] * 2,
        out_specs=(VMEM,) * 3,
        compiler_params=PARAMS,
        name="corners",
    )(second_x, first_x)
    second_corner = paired(to_second, "gz", 1)
    first_corner = paired(to_first, "gz", 0)
    wide = (WIDE, WIDE, LANES)
    block, gram = pl.pallas_call(
        basis_kernel,
        out_shape=(
            jax.ShapeDtypeStruct((COLS, B, B, LANES), F32),
            jax.ShapeDtypeStruct((2 * count_y, LANES), F32),
        ),
        in_specs=[VMEM] * 6,
        out_specs=(VMEM, VMEM),
        scratch_shapes=[
            pltpu.VMEM((FIELDS,) + wide, F32),
            pltpu.VMEM((2,) + wide, F32),
            pltpu.VMEM((COLS, B, B, LANES), F32),
            pltpu.VMEM((COLS, B, B, LANES), F32),
        ],
        compiler_params=PARAMS,
        name="basis",
    )(own, strip, second_y, first_y, second_corner, first_corner)
    parts = lax.all_to_all(gram, "gz", 0, 0, tiled=True)
    line = pl.pallas_call(
        sum_kernel,
        out_shape=jax.ShapeDtypeStruct((2 * count_x, LANES), F32),
        in_specs=[VMEM],
        out_specs=VMEM,
        compiler_params=PARAMS,
        name="line_sum",
    )(parts)
    parts = lax.all_to_all(line, "gx", 0, 0, tiled=True)
    scale = math.sqrt(B * B * LANES * count_x * count_y)
    basis_q, factor_r, hessenberg = pl.pallas_call(
        lambda *refs: factor_kernel(scale, *refs),
        out_shape=(
            jax.ShapeDtypeStruct((COLS, B, B, LANES), F32),
            jax.ShapeDtypeStruct((COLS, COLS), F32),
            jax.ShapeDtypeStruct((S, COLS), F32),
        ),
        in_specs=[VMEM] * 2,
        out_specs=(VMEM,) * 3,
        scratch_shapes=[pltpu.VMEM((COLS, 2 * B, LANES), F32)],
        compiler_params=PARAMS,
        name="factor",
    )(parts, block)
    return basis_q, factor_r, jnp.transpose(hessenberg)


def solution(mesh):
    return jax.shard_map(
        body,
        mesh=mesh,
        in_specs=(
            P(None, "gx", "gz", None),
            P(),
            P(None, "gx", "gz", None),
            P(None, "gx", "gz", None),
            P(None, "gx", "gz", None),
        ),
        out_specs=(P(None, "gx", "gz", None), P(), P()),
        check_vma=False,
    )
```

```python
import math

import jax
import jax.numpy as jnp
from jax import lax
from jax.experimental import pallas as pl
from jax.experimental.pallas import tpu as pltpu
from jax.sharding import PartitionSpec as P

S = 8
COLS = S + 1
CENTER = 2.5
HALF = 1.5
B = 8
WIDE = 3 * B
LANES = 128
FIELDS = 7
NEAR_X = (1, 2, 3, 5, 6)
FAR_X = 2 * B
TILES_X = FAR_X + (B - 1) * len(NEAR_X)
REACH = (8, 7, 7, 7, 8, 8, 7)
HALVES = tuple(reach // 2 for reach in REACH)
CORNER = tuple(2 * sum(HALVES[:f]) for f in range(FIELDS))
TILES_CORNER = 2 * sum(HALVES)
F32 = jnp.float32
VMEM = pl.BlockSpec(memory_space=pltpu.VMEM)
HBM = pl.BlockSpec(memory_space=pltpu.HBM)
SMEM = pl.BlockSpec(memory_space=pltpu.SMEM)
PARAMS = pltpu.CompilerParams(vmem_limit_bytes=16 * 1024 * 1024)


def iota(shape, dim):
    return lax.broadcasted_iota(jnp.int32, shape, dim)


def two_sum(a, b):
    s = a + b
    t = s - a
    return s, (a - (s - t)) + (b - t)


def fast_two_sum(a, b):
    s = a + b
    return s, b - (s - a)


def split(a):
    c = a * 4097.0
    high = c - (c - a)
    return high, a - high


def two_prod(a, b):
    ah, al = split(a)
    bh, bl = split(b)
    p = a * b
    return p, ((ah * bh - p) + (ah * bl + al * bh)) + al * bl


def pair_add(a, b):
    s, e = two_sum(a[0], b[0])
    return fast_two_sum(s, e + (a[1] + b[1]))


def loose_add(a, b):
    s, e = two_sum(a[0], b[0])
    return s, e + (a[1] + b[1])


def loose_mul(a, b):
    p, e = two_prod(a[0], b[0])
    return p, e + (a[0] * b[1] + a[1] * b[0])


def pair_roll(a, shift, axis):
    return tuple(pltpu.roll(part, shift, axis) for part in a)


def pair_where(mask, a, b):
    return tuple(jnp.where(mask, x, y) for x, y in zip(a, b))


def pack_kernel(
    column, basis, diffusivity_in, speed_in, upwind_in, out, to_first, to_second, diffusivity, speed, upwind, sems
):
    copies = [
        pltpu.make_async_copy(src, dst, sems.at[n])
        for n, (src, dst) in enumerate(
            (
                (basis.at[column[0]], out.at[0]),
                (diffusivity_in, diffusivity),
                (speed_in, speed),
                (upwind_in, upwind),
            )
        )
    ]
    for copy in copies:
        copy.start()
    for copy in copies:
        copy.wait()
    factor = -2.0 / HALF
    for dim in range(3):
        flow = upwind[dim].astype(F32)
        out[1 + dim] = (diffusivity[dim] + speed[dim] * flow) * factor
        out[4 + dim] = (diffusivity[dim] + speed[dim] * (1.0 - flow)) * factor

    def emit(target, start):
        target[0:B] = out[0]
        target[B:FAR_X] = out[4]
        for n, f in enumerate(NEAR_X):
            target[FAR_X + (B - 1) * n : FAR_X + (B - 1) * (n + 1)] = out[f, start : start + B - 1]

    @pl.when(lax.rem(lax.axis_index("gx") + lax.axis_index("gz"), 2) == 0)
    def _():
        emit(to_first, 1)
        emit(to_second, 0)

    @pl.when(lax.rem(lax.axis_index("gx") + lax.axis_index("gz"), 2) == 1)
    def _():
        emit(to_first, 0)
        emit(to_second, 1)


def corner_kernel(second, first, strip, to_first, to_second):
    def place(part, side, start):
        strip[0, B * side : B * (side + 1)] = part[0:B]
        strip[4, B * side : B * (side + 1)] = part[B:FAR_X]
        for n, f in enumerate(NEAR_X):
            strip[f, B * side + start : B * (side + 1) - 1 + start] = part[FAR_X + (B - 1) * n : FAR_X + (B - 1) * (n + 1)]
            strip[f, 0 if side == 0 else 2 * B - 1] = jnp.zeros((B, LANES), F32)

    @pl.when(lax.rem(lax.axis_index("gx") + lax.axis_index("gz"), 2) == 0)
    def _():
        place(second, 0, 1)
        place(first, 1, 0)

    @pl.when(lax.rem(lax.axis_index("gx") + lax.axis_index("gz"), 2) == 1)
    def _():
        place(first, 0, 1)
        place(second, 1, 0)

    @pl.when(lax.rem(lax.axis_index("gz"), 2) == 0)
    def _():
        emit_corners(strip, to_first, to_second)

    @pl.when(lax.rem(lax.axis_index("gz"), 2) == 1)
    def _():
        emit_corners(strip, to_second, to_first)


def emit_corners(strip, to_next, to_last):
    row = iota((B, LANES), 0)
    for f in range(FIELDS):
        for side in range(2):
            for m in range(1, HALVES[f] + 1):
                near = strip[f, B - m if side == 0 else B - 1 + m]
                at = CORNER[f] + HALVES[f] * side + m - 1
                other = REACH[f] - m
                if m == other:
                    to_next[at] = near
                    to_last[at] = near
                else:
                    far = strip[f, B - other if side == 0 else B - 1 + other]
                    to_next[at] = jnp.where(row >= m, near, pltpu.roll(far, m, 0))
                    to_last[at] = jnp.where(row < B - m, near, pltpu.roll(far, B - m, 0))


def start_fields(own, strip, last, following, corner_last, corner_following, coeff, field):
    def wide(f, a):
        if B <= a < 2 * B:
            return jnp.concatenate([last[f, a - B], own[f, a - B], following[f, a - B]], 0)
        side = 0 if a < B else 1
        m = B - a if side == 0 else a - (2 * B - 1)
        middle = strip[f, a if side == 0 else a - B]
        other = REACH[f] - m
        at = CORNER[f] + HALVES[f] * side + min(m, other) - 1
        if other <= 0:
            lower = upper = jnp.zeros((B, LANES), F32)
        elif m <= other:
            lower, upper = corner_last[at], corner_following[at]
        else:
            lower = pltpu.roll(corner_last[at], B - other, 0)
            upper = pltpu.roll(corner_following[at], other, 0)
        return jnp.concatenate([lower, middle, upper], 0)

    lane = iota((WIDE, LANES), 1)
    zero = jnp.zeros((WIDE, LANES), F32)
    q_below = wide(4, 0)
    field[0, 0] = wide(0, 0)
    field[0, WIDE - 1] = wide(0, WIDE - 1)
    for a in range(1, WIDE - 1):
        field[0, a] = wide(0, a)
        p = [wide(1 + dim, a) for dim in range(3)]
        q = [wide(4 + dim, a) for dim in range(3)]
        inside = p[0] < 0.0
        qx = jnp.where(inside, q_below, zero)
        qy = jnp.where(inside, pltpu.roll(q[1], 1, 0), zero)
        qz = jnp.where(lane == 0, zero, pltpu.roll(q[2], 1, 1))
        q_below = q[0]
        coeff[0, a] = (-2.0 * (CENTER - 1.0) / HALF) - ((p[0] + p[1]) + (p[2] + qx) + (qy + qz))
        coeff[1, a] = p[0]
        coeff[2, a] = qx
        coeff[3, a] = p[1]
        coeff[4, a] = qy
        coeff[5, a] = jnp.where(lane == LANES - 1, zero, p[2])
        coeff[6, a] = qz


def basis_kernel(
    own, strip, second, first, corner_second, corner_first, block, gram, coeff, field, high, low
):
    @pl.when(lax.rem(lax.axis_index("gz"), 2) == 0)
    def _():
        start_fields(own, strip, second, first, corner_second, corner_first, coeff, field)

    @pl.when(lax.rem(lax.axis_index("gz"), 2) == 1)
    def _():
        start_fields(own, strip, first, second, corner_first, corner_second, coeff, field)

    block[0] = own[0]
    for k in range(1, COLS):
        src, dst = (k - 1) % 2, k % 2

        def layer(a, carry, k=k, src=src, dst=dst):
            v = field[src, a]
            x = coeff[0, a] * v + coeff[1, a] * field[src, a + 1] + coeff[2, a] * field[src, a - 1]
            y = coeff[3, a] * pltpu.roll(v, WIDE - 1, 0) + coeff[4, a] * pltpu.roll(v, 1, 0)
            z = coeff[5, a] * pltpu.roll(v, LANES - 1, 1) + coeff[6, a] * pltpu.roll(v, 1, 1)
            total = x + (y + z)
            new = 0.5 * total if k == 1 else total - field[dst, a]
            if k == S:
                block[k, a - B] = new[B : 2 * B]
            else:
                field[dst, a] = new
            return carry

        lax.fori_loop(k, WIDE - k, layer, 0, unroll=True)
        if k < S:
            block[k] = field[dst, B : 2 * B, B : 2 * B, :]

    for k in range(COLS):
        h, l = split(block[k])
        high[k] = h
        low[k] = l

    def product(i, j):
        total = None
        for x in range(B):
            ah, al, bh, bl = high[i, x], low[i, x], high[j, x], low[j, x]
            p = ah * bh
            e = ah * bl + al * block[j, x]
            if total is None:
                total, rest = p, e
            else:
                total, err = two_sum(total, p)
                rest = rest + (e + err)
        return total, rest

    row = iota((B, LANES), 0)
    lane = iota((B, LANES), 1)
    nothing = (jnp.zeros((B, LANES), F32),) * 2

    def merged(a, b, distance, axis):
        if a is None and b is None:
            return None
        a = nothing if a is None else a
        b = nothing if b is None else b
        mask = ((row if axis == 0 else lane) & distance) == 0
        return loose_add(pair_where(mask, a, b), pair_roll(pair_where(mask, b, a), distance, axis))

    def fold(items, axis):
        distance = 1
        while len(items) > 1:
            items = [merged(items[t], items[t + 1], distance, axis) for t in range(0, len(items), 2)]
            distance *= 2
        return items[0]

    products = {(i, j): product(i, j) for i in range(COLS) for j in range(i, COLS)}
    slots = []
    for m in range(16):
        if m < COLS:
            items = [products[min(r, m), max(r, m)] for r in range(B)]
        else:
            items = [products[m - COLS, S]] + [products[m - 2, S] if m - 2 < COLS else None] + [None] * 6
        slots.append(fold(items, 0))
    table = fold(slots, 1)
    for distance in (16, 32, 64):
        table = loose_add(table, pair_roll(table, distance, 1))
    table = fast_two_sum(*table)
    mine = lane // 16 == row
    rows = [jnp.sum(jnp.where(mine, part, 0.0), axis=0, keepdims=True) for part in table]
    tile = jnp.where(row % 2 == 0, rows[0], rows[1])
    for t in range(gram.shape[0] // B):
        gram[B * t : B * (t + 1), :] = tile


def summed(ref):
    tiles = [ref[B * t : B * (t + 1), :] for t in range(ref.shape[0] // B)]
    pairs = [(t, pltpu.roll(t, B - 1, 0)) for t in tiles]
    while len(pairs) > 1:
        pairs = [pair_add(pairs[t], pairs[t + 1]) for t in range(0, len(pairs), 2)]
    total = pairs[0]
    for distance in (2, 4):
        total = pair_add(total, pair_roll(total, distance, 0))
    return total


def sum_kernel(parts, out):
    total = summed(parts)
    row = iota((B, LANES), 0)
    tile = jnp.where(row % 2 == 0, total[0], pltpu.roll(total[1], 1, 0))
    for t in range(out.shape[0] // B):
        out[B * t : B * (t + 1), :] = tile


def factor_kernel(scale, parts, block, basis_q, factor_r, hessenberg, inverse):
    shape = (2 * B, LANES)
    row = iota(shape, 0)
    lane = iota(shape, 1)

    def matrix(part):
        line = jnp.broadcast_to(part[0:1, :], shape)
        out = jnp.zeros(shape, F32)
        for r in range(B):
            moved = line if r == 0 else pltpu.roll(line, LANES - 16 * r, 1)
            out = jnp.where((row == r) & (lane < COLS), moved, out)
        out = jnp.where((row == S) & (lane < 7), pltpu.roll(line, LANES - 9, 1), out)
        return jnp.where((row == S) & ((lane == 7) | (lane == 8)), pltpu.roll(line, LANES - 18, 1), out)

    high, low = (matrix(part) for part in summed(parts))
    high = jnp.where((lane == row + 64) & (row < COLS), 1.0, high)
    pivots = jnp.ones(shape, F32)
    for j in range(COLS):
        d = tuple(jnp.broadcast_to(part[j : j + 1, j : j + 1], shape) for part in (high, low))
        pivots = jnp.where(row == j, d[0], pivots)
        if j == S:
            break
        top = tuple(jnp.broadcast_to(part[j : j + 1, :], shape) for part in (high, low))
        col = tuple(jnp.broadcast_to(part[:, j : j + 1], shape) for part in (high, low))
        inv = 1.0 / d[0]
        ratio = col[0] * inv
        back, err = two_prod(ratio, d[0])
        rest = (((col[0] - back) - err) + (col[1] - ratio * d[1])) * inv
        change = loose_mul((ratio, rest), top)
        change = tuple(jnp.where(row > j, -part, 0.0) for part in change)
        high, low = pair_add((high, low), change)
    root = jnp.sqrt(pivots)
    scaled = high / root
    upper = jnp.where((lane >= row) & (lane < COLS) & (row < COLS), scaled, 0.0)
    lower = jnp.where((lane <= row) & (row < COLS), pltpu.roll(scaled, 64, 1), 0.0)
    factor_r[...] = (upper / scale)[:COLS, :COLS]
    right = pltpu.roll(upper, LANES - 1, 1)
    product = CENTER * upper + jnp.where(lane == 0, HALF, 0.5 * HALF) * right + (0.5 * HALF) * pltpu.roll(upper, 1, 1)
    product = jnp.where(lane < S, product, 0.0)
    small = lax.dot_general(
        jnp.where(lane < S, lower, 0.0),
        product,
        (((1,), (1,)), ((), ())),
        precision=lax.Precision.HIGHEST,
        preferred_element_type=F32,
    )
    hessenberg[...] = small[:S, :COLS]
    lower = lower * scale
    for k in range(COLS):
        inverse[k] = jnp.broadcast_to(lower[:, k : k + 1], shape)
    for j in range(COLS):
        total = None
        for k in range(j + 1):
            factor = jnp.broadcast_to(inverse[k, j : j + 1, :], (B, LANES))[None]
            term = factor * block[k]
            total = term if total is None else total + term
        basis_q[j] = total


def paired_x(array, first):
    count_x, count_y = lax.axis_size("gx"), lax.axis_size("gz")
    route = []
    for x in range(count_x - 1):
        for y in range(count_y):
            if (x + y + first) % 2 == 0:
                here, there = x * count_y + y, (x + 1) * count_y + y
                route += [(here, there), (there, here)]
    return lax.ppermute(array, ("gx", "gz"), route)


def paired_y(array, first):
    lower = range(first, lax.axis_size("gz") - 1, 2)
    return lax.ppermute(array, "gz", [(i, i + 1) for i in lower] + [(i + 1, i) for i in lower])


def in_hbm(array):
    return pltpu.with_memory_space_constraint(array, pltpu.HBM)


def body(previous_basis, restart_column, diffusivity, speed, upwind):
    count_x, count_y = lax.axis_size("gx"), lax.axis_size("gz")
    faces = (3, B, B, LANES)
    part = (TILES_X, B, LANES)
    own, to_first, to_second = pl.pallas_call(
        pack_kernel,
        out_shape=(pltpu.VMEM((FIELDS, B, B, LANES), F32), pltpu.VMEM(part, F32), pltpu.VMEM(part, F32)),
        in_specs=[SMEM] + [HBM] * 4,
        out_specs=(VMEM,) * 3,
        scratch_shapes=[
            pltpu.VMEM(faces, F32),
            pltpu.VMEM(faces, F32),
            pltpu.VMEM(faces, jnp.int32),
            pltpu.SemaphoreType.DMA((4,)),
        ],
        compiler_params=PARAMS,
        name="pack",
    )(restart_column, *(in_hbm(array) for array in (previous_basis, diffusivity, speed, upwind)))
    second_x = paired_x(to_second, 1)
    first_x = paired_x(to_first, 0)
    corner = jax.ShapeDtypeStruct((TILES_CORNER, B, LANES), F32)
    second_y = paired_y(own, 1)
    first_y = paired_y(own, 0)
    strip, to_first, to_second = pl.pallas_call(
        corner_kernel,
        out_shape=(jax.ShapeDtypeStruct((FIELDS, 2 * B, B, LANES), F32), corner, corner),
        in_specs=[VMEM] * 2,
        out_specs=(VMEM,) * 3,
        compiler_params=PARAMS,
        name="corners",
    )(second_x, first_x)
    second_corner = paired_y(to_second, 1)
    first_corner = paired_y(to_first, 0)
    wide = (WIDE, WIDE, LANES)
    block, gram = pl.pallas_call(
        basis_kernel,
        out_shape=(
            jax.ShapeDtypeStruct((COLS, B, B, LANES), F32),
            jax.ShapeDtypeStruct((2 * count_y, LANES), F32),
        ),
        in_specs=[VMEM] * 6,
        out_specs=(VMEM, VMEM),
        scratch_shapes=[
            pltpu.VMEM((FIELDS,) + wide, F32),
            pltpu.VMEM((2,) + wide, F32),
            pltpu.VMEM((COLS, B, B, LANES), F32),
            pltpu.VMEM((COLS, B, B, LANES), F32),
        ],
        compiler_params=PARAMS,
        name="basis",
    )(own, strip, second_y, first_y, second_corner, first_corner)
    parts = lax.all_to_all(gram, "gz", 0, 0, tiled=True)
    line = pl.pallas_call(
        sum_kernel,
        out_shape=jax.ShapeDtypeStruct((2 * count_x, LANES), F32),
        in_specs=[VMEM],
        out_specs=VMEM,
        compiler_params=PARAMS,
        name="line_sum",
    )(parts)
    parts = lax.all_to_all(line, "gx", 0, 0, tiled=True)
    scale = math.sqrt(B * B * LANES * count_x * count_y)
    basis_q, factor_r, hessenberg = pl.pallas_call(
        lambda *refs: factor_kernel(scale, *refs),
        out_shape=(
            jax.ShapeDtypeStruct((COLS, B, B, LANES), F32),
            jax.ShapeDtypeStruct((COLS, COLS), F32),
            jax.ShapeDtypeStruct((S, COLS), F32),
        ),
        in_specs=[VMEM] * 2,
        out_specs=(VMEM,) * 3,
        scratch_shapes=[pltpu.VMEM((COLS, 2 * B, LANES), F32)],
        compiler_params=PARAMS,
        name="factor",
    )(parts, block)
    return basis_q, factor_r, jnp.transpose(hessenberg)


def solution(mesh):
    return jax.shard_map(
        body,
        mesh=mesh,
        in_specs=(
            P(None, "gx", "gz", None),
            P(),
            P(None, "gx", "gz", None),
            P(None, "gx", "gz", None),
            P(None, "gx", "gz", None),
        ),
        out_specs=(P(None, "gx", "gz", None), P(), P()),
        check_vma=False,
    )
```

```python
import math

import jax
import jax.numpy as jnp
from jax import lax
from jax.experimental import pallas as pl
from jax.experimental.pallas import tpu as pltpu
from jax.sharding import PartitionSpec as P

S = 8
COLS = S + 1
CENTER = 2.5
HALF = 1.5
B = 8
WIDE = 3 * B
LANES = 128
FIELDS = 7
NEAR_X = (1, 2, 3, 5, 6)
FAR_X = 2 * B
TILES_X = FAR_X + (B - 1) * len(NEAR_X)
REACH = (8, 7, 7, 7, 8, 8, 7)
HALVES = tuple(reach // 2 for reach in REACH)
CORNER = tuple(2 * sum(HALVES[:f]) for f in range(FIELDS))
TILES_CORNER = 2 * sum(HALVES)
F32 = jnp.float32
VMEM = pl.BlockSpec(memory_space=pltpu.VMEM)
HBM = pl.BlockSpec(memory_space=pltpu.HBM)
SMEM = pl.BlockSpec(memory_space=pltpu.SMEM)
PARAMS = pltpu.CompilerParams(vmem_limit_bytes=16 * 1024 * 1024)


def iota(shape, dim):
    return lax.broadcasted_iota(jnp.int32, shape, dim)


def two_sum(a, b):
    s = a + b
    t = s - a
    return s, (a - (s - t)) + (b - t)


def fast_two_sum(a, b):
    s = a + b
    return s, b - (s - a)


def split(a):
    c = a * 4097.0
    high = c - (c - a)
    return high, a - high


def two_prod(a, b):
    ah, al = split(a)
    bh, bl = split(b)
    p = a * b
    return p, ((ah * bh - p) + (ah * bl + al * bh)) + al * bl


def pair_add(a, b):
    s, e = two_sum(a[0], b[0])
    return fast_two_sum(s, e + (a[1] + b[1]))


def loose_add(a, b):
    s, e = two_sum(a[0], b[0])
    return s, e + (a[1] + b[1])


def loose_mul(a, b):
    p, e = two_prod(a[0], b[0])
    return p, e + (a[0] * b[1] + a[1] * b[0])


def pair_roll(a, shift, axis):
    return tuple(pltpu.roll(part, shift, axis) for part in a)


def pair_where(mask, a, b):
    return tuple(jnp.where(mask, x, y) for x, y in zip(a, b))


def pack_kernel(
    column, basis, diffusivity_in, speed_in, upwind_in, out, to_first, to_second, diffusivity, speed, upwind, sems
):
    copies = [
        pltpu.make_async_copy(src, dst, sems.at[n])
        for n, (src, dst) in enumerate(
            (
                (basis.at[column[0]], out.at[0]),
                (diffusivity_in, diffusivity),
                (speed_in, speed),
                (upwind_in, upwind),
            )
        )
    ]
    for copy in copies:
        copy.start()
    for copy in copies:
        copy.wait()
    factor = -2.0 / HALF
    for dim in range(3):
        flow = upwind[dim].astype(F32)
        out[1 + dim] = (diffusivity[dim] + speed[dim] * flow) * factor
        out[4 + dim] = (diffusivity[dim] + speed[dim] * (1.0 - flow)) * factor

    def emit(target, start):
        target[0:B] = out[0]
        target[B:FAR_X] = out[4]
        for n, f in enumerate(NEAR_X):
            target[FAR_X + (B - 1) * n : FAR_X + (B - 1) * (n + 1)] = out[f, start : start + B - 1]

    @pl.when(lax.rem(lax.axis_index("gx"), 2) == 0)
    def _():
        emit(to_first, 1)
        emit(to_second, 0)

    @pl.when(lax.rem(lax.axis_index("gx"), 2) == 1)
    def _():
        emit(to_first, 0)
        emit(to_second, 1)


def corner_kernel(second, first, strip, to_first, to_second):
    def place(part, side, start):
        strip[0, B * side : B * (side + 1)] = part[0:B]
        strip[4, B * side : B * (side + 1)] = part[B:FAR_X]
        for n, f in enumerate(NEAR_X):
            strip[f, B * side + start : B * (side + 1) - 1 + start] = part[FAR_X + (B - 1) * n : FAR_X + (B - 1) * (n + 1)]
            strip[f, 0 if side == 0 else 2 * B - 1] = jnp.zeros((B, LANES), F32)

    @pl.when(lax.rem(lax.axis_index("gx"), 2) == 0)
    def _():
        place(second, 0, 1)
        place(first, 1, 0)

    @pl.when(lax.rem(lax.axis_index("gx"), 2) == 1)
    def _():
        place(first, 0, 1)
        place(second, 1, 0)

    @pl.when(lax.rem(lax.axis_index("gz"), 2) == 0)
    def _():
        emit_corners(strip, to_first, to_second)

    @pl.when(lax.rem(lax.axis_index("gz"), 2) == 1)
    def _():
        emit_corners(strip, to_second, to_first)


def emit_corners(strip, to_next, to_last):
    row = iota((B, LANES), 0)
    for f in range(FIELDS):
        for side in range(2):
            for m in range(1, HALVES[f] + 1):
                near = strip[f, B - m if side == 0 else B - 1 + m]
                at = CORNER[f] + HALVES[f] * side + m - 1
                other = REACH[f] - m
                if m == other:
                    to_next[at] = near
                    to_last[at] = near
                else:
                    far = strip[f, B - other if side == 0 else B - 1 + other]
                    to_next[at] = jnp.where(row >= m, near, pltpu.roll(far, m, 0))
                    to_last[at] = jnp.where(row < B - m, near, pltpu.roll(far, B - m, 0))


def start_fields(own, strip, last, following, corner_last, corner_following, coeff, field):
    def wide(f, a):
        if B <= a < 2 * B:
            return jnp.concatenate([last[f, a - B], own[f, a - B], following[f, a - B]], 0)
        side = 0 if a < B else 1
        m = B - a if side == 0 else a - (2 * B - 1)
        middle = strip[f, a if side == 0 else a - B]
        other = REACH[f] - m
        at = CORNER[f] + HALVES[f] * side + min(m, other) - 1
        if other <= 0:
            lower = upper = jnp.zeros((B, LANES), F32)
        elif m <= other:
            lower, upper = corner_last[at], corner_following[at]
        else:
            lower = pltpu.roll(corner_last[at], B - other, 0)
            upper = pltpu.roll(corner_following[at], other, 0)
        return jnp.concatenate([lower, middle, upper], 0)

    lane = iota((WIDE, LANES), 1)
    zero = jnp.zeros((WIDE, LANES), F32)
    q_below = wide(4, 0)
    field[0, 0] = wide(0, 0)
    field[0, WIDE - 1] = wide(0, WIDE - 1)
    for a in range(1, WIDE - 1):
        field[0, a] = wide(0, a)
        p = [wide(1 + dim, a) for dim in range(3)]
        q = [wide(4 + dim, a) for dim in range(3)]
        inside = p[0] < 0.0
        qx = jnp.where(inside, q_below, zero)
        qy = jnp.where(inside, pltpu.roll(q[1], 1, 0), zero)
        qz = jnp.where(lane == 0, zero, pltpu.roll(q[2], 1, 1))
        q_below = q[0]
        coeff[0, a] = (-2.0 * (CENTER - 1.0) / HALF) - ((p[0] + p[1]) + (p[2] + qx) + (qy + qz))
        coeff[1, a] = p[0]
        coeff[2, a] = qx
        coeff[3, a] = p[1]
        coeff[4, a] = qy
        coeff[5, a] = jnp.where(lane == LANES - 1, zero, p[2])
        coeff[6, a] = qz


def basis_kernel(
    own, strip, second, first, corner_second, corner_first, block, gram, coeff, field, high, low
):
    @pl.when(lax.rem(lax.axis_index("gz"), 2) == 0)
    def _():
        start_fields(own, strip, second, first, corner_second, corner_first, coeff, field)

    @pl.when(lax.rem(lax.axis_index("gz"), 2) == 1)
    def _():
        start_fields(own, strip, first, second, corner_first, corner_second, coeff, field)

    block[0] = own[0]
    for k in range(1, COLS):
        src, dst = (k - 1) % 2, k % 2

        def layer(a, carry, k=k, src=src, dst=dst):
            v = field[src, a]
            x = coeff[0, a] * v + coeff[1, a] * field[src, a + 1] + coeff[2, a] * field[src, a - 1]
            y = coeff[3, a] * pltpu.roll(v, WIDE - 1, 0) + coeff[4, a] * pltpu.roll(v, 1, 0)
            z = coeff[5, a] * pltpu.roll(v, LANES - 1, 1) + coeff[6, a] * pltpu.roll(v, 1, 1)
            total = x + (y + z)
            new = 0.5 * total if k == 1 else total - field[dst, a]
            if k == S:
                block[k, a - B] = new[B : 2 * B]
            else:
                field[dst, a] = new
            return carry

        lax.fori_loop(k, WIDE - k, layer, 0, unroll=True)
        if k < S:
            block[k] = field[dst, B : 2 * B, B : 2 * B, :]

    for k in range(COLS):
        h, l = split(block[k])
        high[k] = h
        low[k] = l

    def product(i, j):
        total = None
        for x in range(B):
            ah, al, bh, bl = high[i, x], low[i, x], high[j, x], low[j, x]
            p = ah * bh
            e = ah * bl + al * block[j, x]
            if total is None:
                total, rest = p, e
            else:
                total, err = two_sum(total, p)
                rest = rest + (e + err)
        return total, rest

    row = iota((B, LANES), 0)
    lane = iota((B, LANES), 1)
    nothing = (jnp.zeros((B, LANES), F32),) * 2

    def merged(a, b, distance, axis):
        if a is None and b is None:
            return None
        a = nothing if a is None else a
        b = nothing if b is None else b
        mask = ((row if axis == 0 else lane) & distance) == 0
        return loose_add(pair_where(mask, a, b), pair_roll(pair_where(mask, b, a), distance, axis))

    def fold(items, axis):
        distance = 1
        while len(items) > 1:
            items = [merged(items[t], items[t + 1], distance, axis) for t in range(0, len(items), 2)]
            distance *= 2
        return items[0]

    products = {(i, j): product(i, j) for i in range(COLS) for j in range(i, COLS)}
    slots = []
    for m in range(16):
        if m < COLS:
            items = [products[min(r, m), max(r, m)] for r in range(B)]
        else:
            items = [products[m - COLS, S]] + [products[m - 2, S] if m - 2 < COLS else None] + [None] * 6
        slots.append(fold(items, 0))
    table = fold(slots, 1)
    for distance in (16, 32, 64):
        table = loose_add(table, pair_roll(table, distance, 1))
    table = fast_two_sum(*table)
    mine = lane // 16 == row
    rows = [jnp.sum(jnp.where(mine, part, 0.0), axis=0, keepdims=True) for part in table]
    tile = jnp.where(row % 2 == 0, rows[0], rows[1])
    for t in range(gram.shape[0] // B):
        gram[B * t : B * (t + 1), :] = tile


def summed(ref):
    tiles = [ref[B * t : B * (t + 1), :] for t in range(ref.shape[0] // B)]
    pairs = [(t, pltpu.roll(t, B - 1, 0)) for t in tiles]
    while len(pairs) > 1:
        pairs = [pair_add(pairs[t], pairs[t + 1]) for t in range(0, len(pairs), 2)]
    total = pairs[0]
    for distance in (2, 4):
        total = pair_add(total, pair_roll(total, distance, 0))
    return total


def sum_kernel(parts, out):
    total = summed(parts)
    row = iota((B, LANES), 0)
    tile = jnp.where(row % 2 == 0, total[0], pltpu.roll(total[1], 1, 0))
    for t in range(out.shape[0] // B):
        out[B * t : B * (t + 1), :] = tile


def factor_kernel(scale, parts, block, basis_q, factor_r, hessenberg, inverse):
    shape = (2 * B, LANES)
    row = iota(shape, 0)
    lane = iota(shape, 1)

    def matrix(part):
        line = jnp.broadcast_to(part[0:1, :], shape)
        out = jnp.zeros(shape, F32)
        for r in range(B):
            moved = line if r == 0 else pltpu.roll(line, LANES - 16 * r, 1)
            out = jnp.where((row == r) & (lane < COLS), moved, out)
        out = jnp.where((row == S) & (lane < 7), pltpu.roll(line, LANES - 9, 1), out)
        return jnp.where((row == S) & ((lane == 7) | (lane == 8)), pltpu.roll(line, LANES - 18, 1), out)

    high, low = (matrix(part) for part in summed(parts))
    high = jnp.where((lane == row + 64) & (row < COLS), 1.0, high)
    pivots = jnp.ones(shape, F32)
    for j in range(COLS):
        d = tuple(jnp.broadcast_to(part[j : j + 1, j : j + 1], shape) for part in (high, low))
        pivots = jnp.where(row == j, d[0], pivots)
        if j == S:
            break
        top = tuple(jnp.broadcast_to(part[j : j + 1, :], shape) for part in (high, low))
        col = tuple(jnp.broadcast_to(part[:, j : j + 1], shape) for part in (high, low))
        inv = 1.0 / d[0]
        ratio = col[0] * inv
        back, err = two_prod(ratio, d[0])
        rest = (((col[0] - back) - err) + (col[1] - ratio * d[1])) * inv
        change = loose_mul((ratio, rest), top)
        change = tuple(jnp.where(row > j, -part, 0.0) for part in change)
        high, low = pair_add((high, low), change)
    root = jnp.sqrt(pivots)
    scaled = high / root
    upper = jnp.where((lane >= row) & (lane < COLS) & (row < COLS), scaled, 0.0)
    lower = jnp.where((lane <= row) & (row < COLS), pltpu.roll(scaled, 64, 1), 0.0)
    factor_r[...] = (upper / scale)[:COLS, :COLS]
    right = pltpu.roll(upper, LANES - 1, 1)
    product = CENTER * upper + jnp.where(lane == 0, HALF, 0.5 * HALF) * right + (0.5 * HALF) * pltpu.roll(upper, 1, 1)
    product = jnp.where(lane < S, product, 0.0)
    small = lax.dot_general(
        jnp.where(lane < S, lower, 0.0),
        product,
        (((1,), (1,)), ((), ())),
        precision=lax.Precision.HIGHEST,
        preferred_element_type=F32,
    )
    hessenberg[...] = small[:S, :COLS]
    lower = lower * scale
    for k in range(COLS):
        inverse[k] = jnp.broadcast_to(lower[:, k : k + 1], shape)
    for j in range(COLS):
        total = None
        for k in range(j + 1):
            factor = jnp.broadcast_to(inverse[k, j : j + 1, :], (B, LANES))[None]
            term = factor * block[k]
            total = term if total is None else total + term
        basis_q[j] = total


def paired(array, axis, first):
    count = lax.axis_size(axis)
    lower = range(first, count - 1, 2)
    return lax.ppermute(array, axis, [(i, i + 1) for i in lower] + [(i + 1, i) for i in lower])


def in_hbm(array):
    return pltpu.with_memory_space_constraint(array, pltpu.HBM)


def body(previous_basis, restart_column, diffusivity, speed, upwind):
    count_x, count_y = lax.axis_size("gx"), lax.axis_size("gz")
    faces = (3, B, B, LANES)
    part = (TILES_X, B, LANES)
    own, to_first, to_second = pl.pallas_call(
        pack_kernel,
        out_shape=(pltpu.VMEM((FIELDS, B, B, LANES), F32), pltpu.VMEM(part, F32), pltpu.VMEM(part, F32)),
        in_specs=[SMEM] + [HBM] * 4,
        out_specs=(VMEM,) * 3,
        scratch_shapes=[
            pltpu.VMEM(faces, F32),
            pltpu.VMEM(faces, F32),
            pltpu.VMEM(faces, jnp.int32),
            pltpu.SemaphoreType.DMA((4,)),
        ],
        compiler_params=PARAMS,
        name="pack",
    )(restart_column, *(in_hbm(array) for array in (previous_basis, diffusivity, speed, upwind)))
    second_x = paired(to_second, "gx", 1)
    first_x = paired(to_first, "gx", 0)
    corner = jax.ShapeDtypeStruct((TILES_CORNER, B, LANES), F32)
    second_y = paired(own, "gz", 1)
    first_y = paired(own, "gz", 0)
    strip, to_first, to_second = pl.pallas_call(
        corner_kernel,
        out_shape=(jax.ShapeDtypeStruct((FIELDS, 2 * B, B, LANES), F32), corner, corner),
        in_specs=[VMEM] * 2,
        out_specs=(VMEM,) * 3,
        compiler_params=PARAMS,
        name="corners",
    )(second_x, first_x)
    second_corner = paired(to_second, "gz", 1)
    first_corner = paired(to_first, "gz", 0)
    wide = (WIDE, WIDE, LANES)
    block, gram = pl.pallas_call(
        basis_kernel,
        out_shape=(
            jax.ShapeDtypeStruct((COLS, B, B, LANES), F32),
            jax.ShapeDtypeStruct((2 * count_x, LANES), F32),
        ),
        in_specs=[VMEM] * 6,
        out_specs=(VMEM, VMEM),
        scratch_shapes=[
            pltpu.VMEM((FIELDS,) + wide, F32),
            pltpu.VMEM((2,) + wide, F32),
            pltpu.VMEM((COLS, B, B, LANES), F32),
            pltpu.VMEM((COLS, B, B, LANES), F32),
        ],
        compiler_params=PARAMS,
        name="basis",
    )(own, strip, second_y, first_y, second_corner, first_corner)
    parts = lax.all_to_all(gram, "gx", 0, 0, tiled=True)
    line = pl.pallas_call(
        sum_kernel,
        out_shape=jax.ShapeDtypeStruct((2 * count_y, LANES), F32),
        in_specs=[VMEM],
        out_specs=VMEM,
        compiler_params=PARAMS,
        name="line_sum",
    )(parts)
    parts = lax.all_to_all(line, "gz", 0, 0, tiled=True)
    scale = math.sqrt(B * B * LANES * count_x * count_y)
    basis_q, factor_r, hessenberg = pl.pallas_call(
        lambda *refs: factor_kernel(scale, *refs),
        out_shape=(
            jax.ShapeDtypeStruct((COLS, B, B, LANES), F32),
            jax.ShapeDtypeStruct((COLS, COLS), F32),
            jax.ShapeDtypeStruct((S, COLS), F32),
        ),
        in_specs=[VMEM] * 2,
        out_specs=(VMEM,) * 3,
        scratch_shapes=[pltpu.VMEM((COLS, 2 * B, LANES), F32)],
        compiler_params=PARAMS,
        name="factor",
    )(parts, block)
    return basis_q, factor_r, jnp.transpose(hessenberg)


def solution(mesh):
    return jax.shard_map(
        body,
        mesh=mesh,
        in_specs=(
            P(None, "gx", "gz", None),
            P(),
            P(None, "gx", "gz", None),
            P(None, "gx", "gz", None),
            P(None, "gx", "gz", None),
        ),
        out_specs=(P(None, "gx", "gz", None), P(), P()),
        check_vma=False,
    )
```

```python
import math

import jax
import jax.numpy as jnp
from jax import lax
from jax.experimental import pallas as pl
from jax.experimental.pallas import tpu as pltpu
from jax.sharding import PartitionSpec as P

S = 8
COLS = S + 1
CENTER = 2.5
HALF = 1.5
B = 8
WIDE = 3 * B
LANES = 128
FIELDS = 7
NEAR_X = (1, 2, 3, 5, 6)
FAR_X = 2 * B
TILES_X = FAR_X + (B - 1) * len(NEAR_X)
REACH = (8, 7, 7, 7, 8, 8, 7)
HALVES = tuple(reach // 2 for reach in REACH)
CORNER = tuple(2 * sum(HALVES[:f]) for f in range(FIELDS))
TILES_CORNER = 2 * sum(HALVES)
F32 = jnp.float32
VMEM = pl.BlockSpec(memory_space=pltpu.VMEM)
HBM = pl.BlockSpec(memory_space=pltpu.HBM)
SMEM = pl.BlockSpec(memory_space=pltpu.SMEM)
PARAMS = pltpu.CompilerParams(vmem_limit_bytes=16 * 1024 * 1024)


def iota(shape, dim):
    return lax.broadcasted_iota(jnp.int32, shape, dim)


def two_sum(a, b):
    s = a + b
    t = s - a
    return s, (a - (s - t)) + (b - t)


def fast_two_sum(a, b):
    s = a + b
    return s, b - (s - a)


def split(a):
    c = a * 4097.0
    high = c - (c - a)
    return high, a - high


def two_prod(a, b):
    ah, al = split(a)
    bh, bl = split(b)
    p = a * b
    return p, ((ah * bh - p) + (ah * bl + al * bh)) + al * bl


def pair_add(a, b):
    s, e = two_sum(a[0], b[0])
    return fast_two_sum(s, e + (a[1] + b[1]))


def loose_add(a, b):
    s, e = two_sum(a[0], b[0])
    return s, e + (a[1] + b[1])


def loose_mul(a, b):
    p, e = two_prod(a[0], b[0])
    return p, e + (a[0] * b[1] + a[1] * b[0])


def pair_roll(a, shift, axis):
    return tuple(pltpu.roll(part, shift, axis) for part in a)


def pair_where(mask, a, b):
    return tuple(jnp.where(mask, x, y) for x, y in zip(a, b))


def pack_kernel(
    column_in,
    basis_in,
    diffusivity_in,
    speed_in,
    upwind_in,
    out,
    to_first,
    to_second,
    column,
    basis,
    diffusivity,
    speed,
    upwind,
    sems,
):
    copies = [
        pltpu.make_async_copy(src, dst, sems.at[n])
        for n, (src, dst) in enumerate(
            (
                (column_in, column),
                (basis_in, basis),
                (diffusivity_in, diffusivity),
                (speed_in, speed),
                (upwind_in, upwind),
            )
        )
    ]
    for copy in copies:
        copy.start()
    for copy in copies:
        copy.wait()
    out[0] = basis[column[0, 0]]
    factor = -2.0 / HALF
    for dim in range(3):
        flow = upwind[dim].astype(F32)
        out[1 + dim] = (diffusivity[dim] + speed[dim] * flow) * factor
        out[4 + dim] = (diffusivity[dim] + speed[dim] * (1.0 - flow)) * factor

    def emit(target, start):
        target[0:B] = out[0]
        target[B:FAR_X] = out[4]
        for n, f in enumerate(NEAR_X):
            target[FAR_X + (B - 1) * n : FAR_X + (B - 1) * (n + 1)] = out[f, start : start + B - 1]

    @pl.when(lax.rem(lax.axis_index("gx"), 2) == 0)
    def _():
        emit(to_first, 1)
        emit(to_second, 0)

    @pl.when(lax.rem(lax.axis_index("gx"), 2) == 1)
    def _():
        emit(to_first, 0)
        emit(to_second, 1)


def corner_kernel(second, first, strip, to_first, to_second):
    def place(part, side, start):
        strip[0, B * side : B * (side + 1)] = part[0:B]
        strip[4, B * side : B * (side + 1)] = part[B:FAR_X]
        for n, f in enumerate(NEAR_X):
            strip[f, B * side + start : B * (side + 1) - 1 + start] = part[FAR_X + (B - 1) * n : FAR_X + (B - 1) * (n + 1)]
            strip[f, 0 if side == 0 else 2 * B - 1] = jnp.zeros((B, LANES), F32)

    @pl.when(lax.rem(lax.axis_index("gx"), 2) == 0)
    def _():
        place(second, 0, 1)
        place(first, 1, 0)

    @pl.when(lax.rem(lax.axis_index("gx"), 2) == 1)
    def _():
        place(first, 0, 1)
        place(second, 1, 0)

    @pl.when(lax.rem(lax.axis_index("gz"), 2) == 0)
    def _():
        emit_corners(strip, to_first, to_second)

    @pl.when(lax.rem(lax.axis_index("gz"), 2) == 1)
    def _():
        emit_corners(strip, to_second, to_first)


def emit_corners(strip, to_next, to_last):
    row = iota((B, LANES), 0)
    for f in range(FIELDS):
        for side in range(2):
            for m in range(1, HALVES[f] + 1):
                near = strip[f, B - m if side == 0 else B - 1 + m]
                at = CORNER[f] + HALVES[f] * side + m - 1
                other = REACH[f] - m
                if m == other:
                    to_next[at] = near
                    to_last[at] = near
                else:
                    far = strip[f, B - other if side == 0 else B - 1 + other]
                    to_next[at] = jnp.where(row >= m, near, pltpu.roll(far, m, 0))
                    to_last[at] = jnp.where(row < B - m, near, pltpu.roll(far, B - m, 0))


def start_fields(own, strip, last, following, corner_last, corner_following, coeff, field):
    def wide(f, a):
        if B <= a < 2 * B:
            return jnp.concatenate([last[f, a - B], own[f, a - B], following[f, a - B]], 0)
        side = 0 if a < B else 1
        m = B - a if side == 0 else a - (2 * B - 1)
        middle = strip[f, a if side == 0 else a - B]
        other = REACH[f] - m
        at = CORNER[f] + HALVES[f] * side + min(m, other) - 1
        if other <= 0:
            lower = upper = jnp.zeros((B, LANES), F32)
        elif m <= other:
            lower, upper = corner_last[at], corner_following[at]
        else:
            lower = pltpu.roll(corner_last[at], B - other, 0)
            upper = pltpu.roll(corner_following[at], other, 0)
        return jnp.concatenate([lower, middle, upper], 0)

    lane = iota((WIDE, LANES), 1)
    zero = jnp.zeros((WIDE, LANES), F32)
    q_below = wide(4, 0)
    field[0, 0] = wide(0, 0)
    field[0, WIDE - 1] = wide(0, WIDE - 1)
    for a in range(1, WIDE - 1):
        field[0, a] = wide(0, a)
        p = [wide(1 + dim, a) for dim in range(3)]
        q = [wide(4 + dim, a) for dim in range(3)]
        inside = p[0] < 0.0
        qx = jnp.where(inside, q_below, zero)
        qy = jnp.where(inside, pltpu.roll(q[1], 1, 0), zero)
        qz = jnp.where(lane == 0, zero, pltpu.roll(q[2], 1, 1))
        q_below = q[0]
        coeff[0, a] = (-2.0 * (CENTER - 1.0) / HALF) - ((p[0] + p[1]) + (p[2] + qx) + (qy + qz))
        coeff[1, a] = p[0]
        coeff[2, a] = qx
        coeff[3, a] = p[1]
        coeff[4, a] = qy
        coeff[5, a] = jnp.where(lane == LANES - 1, zero, p[2])
        coeff[6, a] = qz


def basis_kernel(
    own, strip, second, first, corner_second, corner_first, block, gram, coeff, field, high, low
):
    @pl.when(lax.rem(lax.axis_index("gz"), 2) == 0)
    def _():
        start_fields(own, strip, second, first, corner_second, corner_first, coeff, field)

    @pl.when(lax.rem(lax.axis_index("gz"), 2) == 1)
    def _():
        start_fields(own, strip, first, second, corner_first, corner_second, coeff, field)

    block[0] = own[0]
    for k in range(1, COLS):
        src, dst = (k - 1) % 2, k % 2

        def layer(a, carry, k=k, src=src, dst=dst):
            v = field[src, a]
            x = coeff[0, a] * v + coeff[1, a] * field[src, a + 1] + coeff[2, a] * field[src, a - 1]
            y = coeff[3, a] * pltpu.roll(v, WIDE - 1, 0) + coeff[4, a] * pltpu.roll(v, 1, 0)
            z = coeff[5, a] * pltpu.roll(v, LANES - 1, 1) + coeff[6, a] * pltpu.roll(v, 1, 1)
            total = x + (y + z)
            new = 0.5 * total if k == 1 else total - field[dst, a]
            if k == S:
                block[k, a - B] = new[B : 2 * B]
            else:
                field[dst, a] = new
            return carry

        lax.fori_loop(k, WIDE - k, layer, 0, unroll=True)
        if k < S:
            block[k] = field[dst, B : 2 * B, B : 2 * B, :]

    for k in range(COLS):
        h, l = split(block[k])
        high[k] = h
        low[k] = l

    def product(i, j):
        total = None
        for x in range(B):
            ah, al, bh, bl = high[i, x], low[i, x], high[j, x], low[j, x]
            p = ah * bh
            e = ah * bl + al * block[j, x]
            if total is None:
                total, rest = p, e
            else:
                total, err = two_sum(total, p)
                rest = rest + (e + err)
        return total, rest

    row = iota((B, LANES), 0)
    lane = iota((B, LANES), 1)
    nothing = (jnp.zeros((B, LANES), F32),) * 2

    def merged(a, b, distance, axis):
        if a is None and b is None:
            return None
        a = nothing if a is None else a
        b = nothing if b is None else b
        mask = ((row if axis == 0 else lane) & distance) == 0
        return loose_add(pair_where(mask, a, b), pair_roll(pair_where(mask, b, a), distance, axis))

    def fold(items, axis):
        distance = 1
        while len(items) > 1:
            items = [merged(items[t], items[t + 1], distance, axis) for t in range(0, len(items), 2)]
            distance *= 2
        return items[0]

    products = {(i, j): product(i, j) for i in range(COLS) for j in range(i, COLS)}
    slots = []
    for m in range(16):
        if m < COLS:
            items = [products[min(r, m), max(r, m)] for r in range(B)]
        else:
            items = [products[m - COLS, S]] + [products[m - 2, S] if m - 2 < COLS else None] + [None] * 6
        slots.append(fold(items, 0))
    table = fold(slots, 1)
    for distance in (16, 32, 64):
        table = loose_add(table, pair_roll(table, distance, 1))
    table = fast_two_sum(*table)
    mine = lane // 16 == row
    rows = [jnp.sum(jnp.where(mine, part, 0.0), axis=0, keepdims=True) for part in table]
    tile = jnp.where(row % 2 == 0, rows[0], rows[1])
    for t in range(gram.shape[0] // B):
        gram[B * t : B * (t + 1), :] = tile


def summed(ref):
    tiles = [ref[B * t : B * (t + 1), :] for t in range(ref.shape[0] // B)]
    pairs = [(t, pltpu.roll(t, B - 1, 0)) for t in tiles]
    while len(pairs) > 1:
        pairs = [pair_add(pairs[t], pairs[t + 1]) for t in range(0, len(pairs), 2)]
    total = pairs[0]
    for distance in (2, 4):
        total = pair_add(total, pair_roll(total, distance, 0))
    return total


def sum_kernel(parts, out):
    total = summed(parts)
    row = iota((B, LANES), 0)
    tile = jnp.where(row % 2 == 0, total[0], pltpu.roll(total[1], 1, 0))
    for t in range(out.shape[0] // B):
        out[B * t : B * (t + 1), :] = tile


def factor_kernel(scale, parts, block, basis_q, factor_r, hessenberg, inverse):
    shape = (2 * B, LANES)
    row = iota(shape, 0)
    lane = iota(shape, 1)

    def matrix(part):
        line = jnp.broadcast_to(part[0:1, :], shape)
        out = jnp.zeros(shape, F32)
        for r in range(B):
            moved = line if r == 0 else pltpu.roll(line, LANES - 16 * r, 1)
            out = jnp.where((row == r) & (lane < COLS), moved, out)
        out = jnp.where((row == S) & (lane < 7), pltpu.roll(line, LANES - 9, 1), out)
        return jnp.where((row == S) & ((lane == 7) | (lane == 8)), pltpu.roll(line, LANES - 18, 1), out)

    high, low = (matrix(part) for part in summed(parts))
    high = jnp.where((lane == row + 64) & (row < COLS), 1.0, high)
    pivots = jnp.ones(shape, F32)
    for j in range(COLS):
        d = tuple(jnp.broadcast_to(part[j : j + 1, j : j + 1], shape) for part in (high, low))
        pivots = jnp.where(row == j, d[0], pivots)
        if j == S:
            break
        top = tuple(jnp.broadcast_to(part[j : j + 1, :], shape) for part in (high, low))
        col = tuple(jnp.broadcast_to(part[:, j : j + 1], shape) for part in (high, low))
        inv = 1.0 / d[0]
        ratio = col[0] * inv
        back, err = two_prod(ratio, d[0])
        rest = (((col[0] - back) - err) + (col[1] - ratio * d[1])) * inv
        change = loose_mul((ratio, rest), top)
        change = tuple(jnp.where(row > j, -part, 0.0) for part in change)
        high, low = pair_add((high, low), change)
    root = jnp.sqrt(pivots)
    scaled = high / root
    upper = jnp.where((lane >= row) & (lane < COLS) & (row < COLS), scaled, 0.0)
    lower = jnp.where((lane <= row) & (row < COLS), pltpu.roll(scaled, 64, 1), 0.0)
    factor_r[...] = (upper / scale)[:COLS, :COLS]
    right = pltpu.roll(upper, LANES - 1, 1)
    product = CENTER * upper + jnp.where(lane == 0, HALF, 0.5 * HALF) * right + (0.5 * HALF) * pltpu.roll(upper, 1, 1)
    product = jnp.where(lane < S, product, 0.0)
    small = lax.dot_general(
        jnp.where(lane < S, lower, 0.0),
        product,
        (((1,), (1,)), ((), ())),
        precision=lax.Precision.HIGHEST,
        preferred_element_type=F32,
    )
    hessenberg[...] = small[:S, :COLS]
    lower = lower * scale
    for k in range(COLS):
        inverse[k] = jnp.broadcast_to(lower[:, k : k + 1], shape)
    for j in range(COLS):
        total = None
        for k in range(j + 1):
            factor = jnp.broadcast_to(inverse[k, j : j + 1, :], (B, LANES))[None]
            term = factor * block[k]
            total = term if total is None else total + term
        basis_q[j] = total


def paired(array, axis, first):
    count = lax.axis_size(axis)
    lower = range(first, count - 1, 2)
    return lax.ppermute(array, axis, [(i, i + 1) for i in lower] + [(i + 1, i) for i in lower])


def in_hbm(array):
    return pltpu.with_memory_space_constraint(array, pltpu.HBM)


def body(previous_basis, restart_column, diffusivity, speed, upwind):
    count_x, count_y = lax.axis_size("gx"), lax.axis_size("gz")
    faces = (3, B, B, LANES)
    part = (TILES_X, B, LANES)
    own, to_first, to_second = pl.pallas_call(
        pack_kernel,
        out_shape=(pltpu.VMEM((FIELDS, B, B, LANES), F32), pltpu.VMEM(part, F32), pltpu.VMEM(part, F32)),
        in_specs=[HBM] * 5,
        out_specs=(VMEM,) * 3,
        scratch_shapes=[
            pltpu.SMEM((1, 1), jnp.int32),
            pltpu.VMEM((4, B, B, LANES), F32),
            pltpu.VMEM(faces, F32),
            pltpu.VMEM(faces, F32),
            pltpu.VMEM(faces, jnp.int32),
            pltpu.SemaphoreType.DMA((5,)),
        ],
        compiler_params=PARAMS,
        name="pack",
    )(jnp.reshape(restart_column, (1, 1)), *(in_hbm(array) for array in (previous_basis, diffusivity, speed, upwind)))
    second_x = paired(to_second, "gx", 1)
    first_x = paired(to_first, "gx", 0)
    corner = jax.ShapeDtypeStruct((TILES_CORNER, B, LANES), F32)
    second_y = paired(own, "gz", 1)
    first_y = paired(own, "gz", 0)
    strip, to_first, to_second = pl.pallas_call(
        corner_kernel,
        out_shape=(jax.ShapeDtypeStruct((FIELDS, 2 * B, B, LANES), F32), corner, corner),
        in_specs=[VMEM] * 2,
        out_specs=(VMEM,) * 3,
        compiler_params=PARAMS,
        name="corners",
    )(second_x, first_x)
    second_corner = paired(to_second, "gz", 1)
    first_corner = paired(to_first, "gz", 0)
    wide = (WIDE, WIDE, LANES)
    block, gram = pl.pallas_call(
        basis_kernel,
        out_shape=(
            jax.ShapeDtypeStruct((COLS, B, B, LANES), F32),
            jax.ShapeDtypeStruct((2 * count_y, LANES), F32),
        ),
        in_specs=[VMEM] * 6,
        out_specs=(VMEM, VMEM),
        scratch_shapes=[
            pltpu.VMEM((FIELDS,) + wide, F32),
            pltpu.VMEM((2,) + wide, F32),
            pltpu.VMEM((COLS, B, B, LANES), F32),
            pltpu.VMEM((COLS, B, B, LANES), F32),
        ],
        compiler_params=PARAMS,
        name="basis",
    )(own, strip, second_y, first_y, second_corner, first_corner)
    parts = lax.all_to_all(gram, "gz", 0, 0, tiled=True)
    line = pl.pallas_call(
        sum_kernel,
        out_shape=jax.ShapeDtypeStruct((2 * count_x, LANES), F32),
        in_specs=[VMEM],
        out_specs=VMEM,
        compiler_params=PARAMS,
        name="line_sum",
    )(parts)
    parts = lax.all_to_all(line, "gx", 0, 0, tiled=True)
    scale = math.sqrt(B * B * LANES * count_x * count_y)
    basis_q, factor_r, hessenberg = pl.pallas_call(
        lambda *refs: factor_kernel(scale, *refs),
        out_shape=(
            jax.ShapeDtypeStruct((COLS, B, B, LANES), F32),
            jax.ShapeDtypeStruct((COLS, COLS), F32),
            jax.ShapeDtypeStruct((S, COLS), F32),
        ),
        in_specs=[VMEM] * 2,
        out_specs=(VMEM,) * 3,
        scratch_shapes=[pltpu.VMEM((COLS, 2 * B, LANES), F32)],
        compiler_params=PARAMS,
        name="factor",
    )(parts, block)
    return basis_q, factor_r, jnp.transpose(hessenberg)


def solution(mesh):
    return jax.shard_map(
        body,
        mesh=mesh,
        in_specs=(
            P(None, "gx", "gz", None),
            P(),
            P(None, "gx", "gz", None),
            P(None, "gx", "gz", None),
            P(None, "gx", "gz", None),
        ),
        out_specs=(P(None, "gx", "gz", None), P(), P()),
        check_vma=False,
    )
```

```python
import math

import jax
import jax.numpy as jnp
from jax import lax
from jax.experimental import pallas as pl
from jax.experimental.pallas import tpu as pltpu
from jax.sharding import PartitionSpec as P

S = 8
COLS = S + 1
CENTER = 2.5
HALF = 1.5
B = 8
WIDE = 3 * B
LANES = 128
FIELDS = 7
NEAR_X = (1, 2, 3, 5, 6)
FAR_X = 2 * B
TILES_X = FAR_X + (B - 1) * len(NEAR_X)
REACH = (8, 7, 7, 7, 8, 8, 7)
HALVES = tuple(reach // 2 for reach in REACH)
CORNER = tuple(2 * sum(HALVES[:f]) for f in range(FIELDS))
TILES_CORNER = 2 * sum(HALVES)
F32 = jnp.float32
VMEM = pl.BlockSpec(memory_space=pltpu.VMEM)
HBM = pl.BlockSpec(memory_space=pltpu.HBM)
SMEM = pl.BlockSpec(memory_space=pltpu.SMEM)
PARAMS = pltpu.CompilerParams(vmem_limit_bytes=16 * 1024 * 1024)


def iota(shape, dim):
    return lax.broadcasted_iota(jnp.int32, shape, dim)


def two_sum(a, b):
    s = a + b
    t = s - a
    return s, (a - (s - t)) + (b - t)


def fast_two_sum(a, b):
    s = a + b
    return s, b - (s - a)


def split(a):
    c = a * 4097.0
    high = c - (c - a)
    return high, a - high


def two_prod(a, b):
    ah, al = split(a)
    bh, bl = split(b)
    p = a * b
    return p, ((ah * bh - p) + (ah * bl + al * bh)) + al * bl


def pair_add(a, b):
    s, e = two_sum(a[0], b[0])
    return fast_two_sum(s, e + (a[1] + b[1]))


def loose_add(a, b):
    s, e = two_sum(a[0], b[0])
    return s, e + (a[1] + b[1])


def loose_mul(a, b):
    p, e = two_prod(a[0], b[0])
    return p, e + (a[0] * b[1] + a[1] * b[0])


def pair_roll(a, shift, axis):
    return tuple(pltpu.roll(part, shift, axis) for part in a)


def pair_where(mask, a, b):
    return tuple(jnp.where(mask, x, y) for x, y in zip(a, b))


def pack_kernel(
    column, basis, diffusivity_in, speed_in, upwind_in, out, to_first, to_second, diffusivity, speed, upwind, sems
):
    copies = [
        pltpu.make_async_copy(src, dst, sems.at[n])
        for n, (src, dst) in enumerate(
            (
                (basis.at[column[0]], out.at[0]),
                (diffusivity_in, diffusivity),
                (speed_in, speed),
                (upwind_in, upwind),
            )
        )
    ]
    for copy in copies:
        copy.start()
    for copy in copies:
        copy.wait()
    factor = -2.0 / HALF
    for dim in range(3):
        flow = upwind[dim].astype(F32)
        out[1 + dim] = (diffusivity[dim] + speed[dim] * flow) * factor
        out[4 + dim] = (diffusivity[dim] + speed[dim] * (1.0 - flow)) * factor

    def emit(target, start):
        target[0:B] = out[0]
        target[B:FAR_X] = out[4]
        for n, f in enumerate(NEAR_X):
            target[FAR_X + (B - 1) * n : FAR_X + (B - 1) * (n + 1)] = out[f, start : start + B - 1]

    @pl.when(lax.rem(lax.axis_index("gx"), 2) == 0)
    def _():
        emit(to_first, 1)
        emit(to_second, 0)

    @pl.when(lax.rem(lax.axis_index("gx"), 2) == 1)
    def _():
        emit(to_first, 0)
        emit(to_second, 1)


def corner_kernel(second, first, strip, to_first, to_second):
    def place(part, side, start):
        strip[0, B * side : B * (side + 1)] = part[0:B]
        strip[4, B * side : B * (side + 1)] = part[B:FAR_X]
        for n, f in enumerate(NEAR_X):
            strip[f, B * side + start : B * (side + 1) - 1 + start] = part[FAR_X + (B - 1) * n : FAR_X + (B - 1) * (n + 1)]
            strip[f, 0 if side == 0 else 2 * B - 1] = jnp.zeros((B, LANES), F32)

    @pl.when(lax.rem(lax.axis_index("gx"), 2) == 0)
    def _():
        place(second, 0, 1)
        place(first, 1, 0)

    @pl.when(lax.rem(lax.axis_index("gx"), 2) == 1)
    def _():
        place(first, 0, 1)
        place(second, 1, 0)

    @pl.when(lax.rem(lax.axis_index("gz"), 2) == 0)
    def _():
        emit_corners(strip, to_first, to_second)

    @pl.when(lax.rem(lax.axis_index("gz"), 2) == 1)
    def _():
        emit_corners(strip, to_second, to_first)


def emit_corners(strip, to_next, to_last):
    row = iota((B, LANES), 0)
    for f in range(FIELDS):
        for side in range(2):
            for m in range(1, HALVES[f] + 1):
                near = strip[f, B - m if side == 0 else B - 1 + m]
                at = CORNER[f] + HALVES[f] * side + m - 1
                other = REACH[f] - m
                if m == other:
                    to_next[at] = near
                    to_last[at] = near
                else:
                    far = strip[f, B - other if side == 0 else B - 1 + other]
                    to_next[at] = jnp.where(row >= m, near, pltpu.roll(far, m, 0))
                    to_last[at] = jnp.where(row < B - m, near, pltpu.roll(far, B - m, 0))


def start_fields(own, strip, last, following, corner_last, corner_following, coeff, field):
    def wide(f, a):
        if B <= a < 2 * B:
            return jnp.concatenate([last[f, a - B], own[f, a - B], following[f, a - B]], 0)
        side = 0 if a < B else 1
        m = B - a if side == 0 else a - (2 * B - 1)
        middle = strip[f, a if side == 0 else a - B]
        other = REACH[f] - m
        at = CORNER[f] + HALVES[f] * side + min(m, other) - 1
        if other <= 0:
            lower = upper = jnp.zeros((B, LANES), F32)
        elif m <= other:
            lower, upper = corner_last[at], corner_following[at]
        else:
            lower = pltpu.roll(corner_last[at], B - other, 0)
            upper = pltpu.roll(corner_following[at], other, 0)
        return jnp.concatenate([lower, middle, upper], 0)

    lane = iota((WIDE, LANES), 1)
    zero = jnp.zeros((WIDE, LANES), F32)
    q_below = wide(4, 0)
    field[0, 0] = wide(0, 0)
    field[0, WIDE - 1] = wide(0, WIDE - 1)
    for a in range(1, WIDE - 1):
        field[0, a] = wide(0, a)
        p = [wide(1 + dim, a) for dim in range(3)]
        q = [wide(4 + dim, a) for dim in range(3)]
        inside = p[0] < 0.0
        qx = jnp.where(inside, q_below, zero)
        qy = jnp.where(inside, pltpu.roll(q[1], 1, 0), zero)
        qz = jnp.where(lane == 0, zero, pltpu.roll(q[2], 1, 1))
        q_below = q[0]
        coeff[0, a] = (-2.0 * (CENTER - 1.0) / HALF) - ((p[0] + p[1]) + (p[2] + qx) + (qy + qz))
        coeff[1, a] = p[0]
        coeff[2, a] = qx
        coeff[3, a] = p[1]
        coeff[4, a] = qy
        coeff[5, a] = jnp.where(lane == LANES - 1, zero, p[2])
        coeff[6, a] = qz


def basis_kernel(
    own, strip, second, first, corner_second, corner_first, block, gram, coeff, field, high, low
):
    @pl.when(lax.rem(lax.axis_index("gz"), 2) == 0)
    def _():
        start_fields(own, strip, second, first, corner_second, corner_first, coeff, field)

    @pl.when(lax.rem(lax.axis_index("gz"), 2) == 1)
    def _():
        start_fields(own, strip, first, second, corner_first, corner_second, coeff, field)

    block[0] = own[0]
    for k in range(1, COLS):
        src, dst = (k - 1) % 2, k % 2

        def layer(a, k=k, src=src, dst=dst):
            v = field[src, a]
            x = coeff[0, a] * v + coeff[1, a] * field[src, a + 1] + coeff[2, a] * field[src, a - 1]
            y = coeff[3, a] * pltpu.roll(v, WIDE - 1, 0) + coeff[4, a] * pltpu.roll(v, 1, 0)
            z = coeff[5, a] * pltpu.roll(v, LANES - 1, 1) + coeff[6, a] * pltpu.roll(v, 1, 1)
            total = x + (y + z)
            new = 0.5 * total if k == 1 else total - field[dst, a]
            if k == S:
                block[k, a - B] = new[B : 2 * B]
            elif a == k or a == WIDE - 1 - k:
                field[dst, a, B : 2 * B] = new[B : 2 * B]
            else:
                field[dst, a] = new

        for a in range(k, WIDE - k):
            layer(a)
        if k < S:
            block[k] = field[dst, B : 2 * B, B : 2 * B, :]

    for k in range(COLS):
        h, l = split(block[k])
        high[k] = h
        low[k] = l

    def product(i, j):
        total = None
        for x in range(B):
            ah, al, bh, bl = high[i, x], low[i, x], high[j, x], low[j, x]
            p = ah * bh
            e = ah * bl + al * block[j, x]
            if total is None:
                total, rest = p, e
            else:
                total, err = two_sum(total, p)
                rest = rest + (e + err)
        return total, rest

    row = iota((B, LANES), 0)
    lane = iota((B, LANES), 1)
    nothing = (jnp.zeros((B, LANES), F32),) * 2

    def merged(a, b, distance, axis):
        if a is None and b is None:
            return None
        a = nothing if a is None else a
        b = nothing if b is None else b
        mask = ((row if axis == 0 else lane) & distance) == 0
        return loose_add(pair_where(mask, a, b), pair_roll(pair_where(mask, b, a), distance, axis))

    def fold(items, axis):
        distance = 1
        while len(items) > 1:
            items = [merged(items[t], items[t + 1], distance, axis) for t in range(0, len(items), 2)]
            distance *= 2
        return items[0]

    products = {(i, j): product(i, j) for i in range(COLS) for j in range(i, COLS)}
    slots = []
    for m in range(16):
        if m < COLS:
            items = [products[min(r, m), max(r, m)] for r in range(B)]
        else:
            items = [products[m - COLS, S]] + [products[m - 2, S] if m - 2 < COLS else None] + [None] * 6
        slots.append(fold(items, 0))
    table = fold(slots, 1)
    for distance in (16, 32, 64):
        table = loose_add(table, pair_roll(table, distance, 1))
    table = fast_two_sum(*table)
    mine = lane // 16 == row
    rows = [jnp.sum(jnp.where(mine, part, 0.0), axis=0, keepdims=True) for part in table]
    tile = jnp.where(row % 2 == 0, rows[0], rows[1])
    for t in range(gram.shape[0] // B):
        gram[B * t : B * (t + 1), :] = tile


def summed(ref):
    tiles = [ref[B * t : B * (t + 1), :] for t in range(ref.shape[0] // B)]
    pairs = [(t, pltpu.roll(t, B - 1, 0)) for t in tiles]
    while len(pairs) > 1:
        pairs = [loose_add(pairs[t], pairs[t + 1]) for t in range(0, len(pairs), 2)]
    total = pairs[0]
    for distance in (2, 4):
        total = loose_add(total, pair_roll(total, distance, 0))
    return fast_two_sum(*total)


def sum_kernel(parts, out):
    total = summed(parts)
    row = iota((B, LANES), 0)
    tile = jnp.where(row % 2 == 0, total[0], pltpu.roll(total[1], 1, 0))
    for t in range(out.shape[0] // B):
        out[B * t : B * (t + 1), :] = tile


def factor_kernel(scale, parts, block, basis_q, factor_r, hessenberg, inverse):
    shape = (2 * B, LANES)
    row = iota(shape, 0)
    lane = iota(shape, 1)

    def matrix(part):
        line = jnp.broadcast_to(part[0:1, :], shape)
        out = jnp.zeros(shape, F32)
        for r in range(B):
            moved = line if r == 0 else pltpu.roll(line, LANES - 16 * r, 1)
            out = jnp.where((row == r) & (lane < COLS), moved, out)
        out = jnp.where((row == S) & (lane < 7), pltpu.roll(line, LANES - 9, 1), out)
        return jnp.where((row == S) & ((lane == 7) | (lane == 8)), pltpu.roll(line, LANES - 18, 1), out)

    high, low = (matrix(part) for part in summed(parts))
    high = jnp.where((lane == row + 64) & (row < COLS), 1.0, high)
    pivots = jnp.ones(shape, F32)
    for j in range(COLS):
        d = tuple(jnp.broadcast_to(part[j : j + 1, j : j + 1], shape) for part in (high, low))
        pivots = jnp.where(row == j, d[0], pivots)
        if j == S:
            break
        top = tuple(jnp.broadcast_to(part[j : j + 1, :], shape) for part in (high, low))
        col = tuple(jnp.broadcast_to(part[:, j : j + 1], shape) for part in (high, low))
        inv = 1.0 / d[0]
        ratio = col[0] * inv
        back, err = two_prod(ratio, d[0])
        rest = (((col[0] - back) - err) + (col[1] - ratio * d[1])) * inv
        change = loose_mul((ratio, rest), top)
        change = tuple(jnp.where(row > j, -part, 0.0) for part in change)
        high, low = pair_add((high, low), change)
    root = jnp.sqrt(pivots)
    scaled = high / root
    upper = jnp.where((lane >= row) & (lane < COLS) & (row < COLS), scaled, 0.0)
    lower = jnp.where((lane <= row) & (row < COLS), pltpu.roll(scaled, 64, 1), 0.0)
    factor_r[...] = (upper / scale)[:COLS, :COLS]
    right = pltpu.roll(upper, LANES - 1, 1)
    product = CENTER * upper + jnp.where(lane == 0, HALF, 0.5 * HALF) * right + (0.5 * HALF) * pltpu.roll(upper, 1, 1)
    product = jnp.where(lane < S, product, 0.0)
    small = lax.dot_general(
        jnp.where(lane < S, lower, 0.0),
        product,
        (((1,), (1,)), ((), ())),
        precision=lax.Precision.HIGHEST,
        preferred_element_type=F32,
    )
    hessenberg[...] = small[:S, :COLS]
    lower = lower * scale
    for k in range(COLS):
        inverse[k] = jnp.broadcast_to(lower[:, k : k + 1], shape)
    for j in range(COLS):
        total = None
        for k in range(j + 1):
            factor = jnp.broadcast_to(inverse[k, j : j + 1, :], (B, LANES))[None]
            term = factor * block[k]
            total = term if total is None else total + term
        basis_q[j] = total


def paired(array, axis, first):
    count = lax.axis_size(axis)
    lower = range(first, count - 1, 2)
    return lax.ppermute(array, axis, [(i, i + 1) for i in lower] + [(i + 1, i) for i in lower])


def in_hbm(array):
    return pltpu.with_memory_space_constraint(array, pltpu.HBM)


def body(previous_basis, restart_column, diffusivity, speed, upwind):
    count_x, count_y = lax.axis_size("gx"), lax.axis_size("gz")
    faces = (3, B, B, LANES)
    part = (TILES_X, B, LANES)
    own, to_first, to_second = pl.pallas_call(
        pack_kernel,
        out_shape=(pltpu.VMEM((FIELDS, B, B, LANES), F32), pltpu.VMEM(part, F32), pltpu.VMEM(part, F32)),
        in_specs=[SMEM] + [HBM] * 4,
        out_specs=(VMEM,) * 3,
        scratch_shapes=[
            pltpu.VMEM(faces, F32),
            pltpu.VMEM(faces, F32),
            pltpu.VMEM(faces, jnp.int32),
            pltpu.SemaphoreType.DMA((4,)),
        ],
        compiler_params=PARAMS,
        name="pack",
    )(restart_column, *(in_hbm(array) for array in (previous_basis, diffusivity, speed, upwind)))
    second_x = paired(to_second, "gx", 1)
    first_x = paired(to_first, "gx", 0)
    corner = jax.ShapeDtypeStruct((TILES_CORNER, B, LANES), F32)
    second_y = paired(own, "gz", 1)
    first_y = paired(own, "gz", 0)
    strip, to_first, to_second = pl.pallas_call(
        corner_kernel,
        out_shape=(jax.ShapeDtypeStruct((FIELDS, 2 * B, B, LANES), F32), corner, corner),
        in_specs=[VMEM] * 2,
        out_specs=(VMEM,) * 3,
        compiler_params=PARAMS,
        name="corners",
    )(second_x, first_x)
    second_corner = paired(to_second, "gz", 1)
    first_corner = paired(to_first, "gz", 0)
    wide = (WIDE, WIDE, LANES)
    block, gram = pl.pallas_call(
        basis_kernel,
        out_shape=(
            jax.ShapeDtypeStruct((COLS, B, B, LANES), F32),
            jax.ShapeDtypeStruct((2 * count_y, LANES), F32),
        ),
        in_specs=[VMEM] * 6,
        out_specs=(VMEM, VMEM),
        scratch_shapes=[
            pltpu.VMEM((FIELDS,) + wide, F32),
            pltpu.VMEM((2,) + wide, F32),
            pltpu.VMEM((COLS, B, B, LANES), F32),
            pltpu.VMEM((COLS, B, B, LANES), F32),
        ],
        compiler_params=PARAMS,
        name="basis",
    )(own, strip, second_y, first_y, second_corner, first_corner)
    parts = lax.all_to_all(gram, "gz", 0, 0, tiled=True)
    line = pl.pallas_call(
        sum_kernel,
        out_shape=jax.ShapeDtypeStruct((2 * count_x, LANES), F32),
        in_specs=[VMEM],
        out_specs=VMEM,
        compiler_params=PARAMS,
        name="line_sum",
    )(parts)
    parts = lax.all_to_all(line, "gx", 0, 0, tiled=True)
    scale = math.sqrt(B * B * LANES * count_x * count_y)
    basis_q, factor_r, hessenberg = pl.pallas_call(
        lambda *refs: factor_kernel(scale, *refs),
        out_shape=(
            jax.ShapeDtypeStruct((COLS, B, B, LANES), F32),
            jax.ShapeDtypeStruct((COLS, COLS), F32),
            jax.ShapeDtypeStruct((S, COLS), F32),
        ),
        in_specs=[VMEM] * 2,
        out_specs=(VMEM,) * 3,
        scratch_shapes=[pltpu.VMEM((COLS, 2 * B, LANES), F32)],
        compiler_params=PARAMS,
        name="factor",
    )(parts, block)
    return basis_q, factor_r, jnp.transpose(hessenberg)


def solution(mesh):
    return jax.shard_map(
        body,
        mesh=mesh,
        in_specs=(
            P(None, "gx", "gz", None),
            P(),
            P(None, "gx", "gz", None),
            P(None, "gx", "gz", None),
            P(None, "gx", "gz", None),
        ),
        out_specs=(P(None, "gx", "gz", None), P(), P()),
        check_vma=False,
    )
```
